32 devices in a mesh: fsdp: 16 (over z, x, core), dp: 2 (over y).
Axes of the slice: x: 2, y: 2, z: 4, core: 2. Of those that a mesh axis runs over, the one named last changes fastest.
Arguments:
- tokens: bfloat16 [16384, 1024], P(('fsdp', 'dp')), may hold values from -6 to 6
- encoder: bfloat16 [16384, 1024], P(('fsdp', 'dp')), may hold values from -6 to 6
- cotangent: bfloat16 [16384, 1024], P(('fsdp', 'dp')), may hold values from -6 to 6
- self_qkv: bfloat16 [3, 1024, 1024], P(None, 'fsdp'), may hold values from -0.1875 to 0.1875
- self_out: bfloat16 [1024, 1024], P('fsdp'), may hold values from -0.75 to 0.75
- cross_qkv: bfloat16 [3, 1024, 1024], P(None, 'fsdp'), may hold values from -0.1875 to 0.1875
- cross_out: bfloat16 [1024, 1024], P('fsdp'), may hold values from -0.75 to 0.75
- ffn_in: bfloat16 [1024, 4096], P('fsdp'), may hold values from -0.1875 to 0.1875
- ffn_out: bfloat16 [4096, 1024], P('fsdp'), may hold values from -0.09375 to 0.09375
- adapt_down: bfloat16 [1024, 512], replicated, may hold values from -0.1875 to 0.1875
- down_bias: float32 [512], replicated, may hold values from -2 to 2
- adapt_up: bfloat16 [512, 1024], replicated, may hold values from -0.25 to 0.25
- up_bias: float32 [1024], replicated, may hold values from -2 to 2
- norm_gain: float32 [3, 1024], replicated, may hold values from 0.25 to 1.75
- norm_bias: float32 [3, 1024], replicated, may hold values from -2 to 2
- bucket_shift: int32 [32], P(('fsdp', 'dp')), may hold values from 0 to 2, as said below
- seq_lengths: int32 [32, 4], P(('fsdp', 'dp')), may hold values from 64 to 512, as said below
- enc_lengths: int32 [32, 4], P(('fsdp', 'dp')), may hold values from 64 to 512, as said below
Outputs:
- output: bfloat16 [16384, 1024], P(('fsdp', 'dp'))
- grad_tokens: bfloat16 [16384, 1024], P(('fsdp', 'dp'))
- grad_encoder: bfloat16 [16384, 1024], P(('fsdp', 'dp'))
- grad_adapt_down: float32 [1024, 512], replicated
- grad_down_bias: float32 [512], replicated
- grad_adapt_up: float32 [512, 1024], replicated
- grad_up_bias: float32 [1024], replicated
- grad_norm_gain: float32 [3, 1024], replicated
- grad_norm_bias: float32 [3, 1024], replicated
The draws below stay inside these ranges and needn't reach their ends.
Inputs may be any that keep to these rules, and one draw needn't show every extreme that they name: Some group has bucket_shift 0 and some group has 2; group g holds 4 >> bucket_shift[g] sequences. `seq_lengths`: entry j of a group is the valid length of its j-th sequence for j < 4 >> bucket_shift[g], and lies between half the bucket and the bucket; later entries are unused; in every group one sequence fills its bucket. `enc_lengths`: entry j of a group is the valid encoder length of its j-th sequence for j < 4 >> bucket_shift[g], and lies between half the bucket and the bucket; later entries are unused; in every group one sequence fills its bucket.
All inputs are finite; a program needn't handle non-finite values.
Results may differ from the reference program's by a relative error of at most 0.02.
Values may be sent and summed in bfloat16 or wider, within the bound.
A program may use at most 256 MiB of HBM per device.

```python
import jax
import jax.numpy as jnp
from jax import lax

D = 1024
HEADS = 16
FF = 4096
ADAPT = 512
STEP = 12
TOK_DEV = 512
HD = 64
MINLEN = 128
GROUPS = 32
TOKENS = 16384


def bucket_ids_of(key):
    key = jax.random.fold_in(key, 101)
    key_one, key_two = jax.random.split(key)
    bucket_ids = jax.random.randint(key_one, (GROUPS,), 0, 3)
    order = jax.random.permutation(key_two, GROUPS)
    bucket_ids = bucket_ids.at[order[0]].set(2)
    bucket_ids = bucket_ids.at[order[1]].set(0)
    return bucket_ids.astype(jnp.int32)


def valid_lengths(key, bucket_ids):
    key_one, key_two = jax.random.split(key)
    bucket = MINLEN * jnp.where(bucket_ids == 0, 1, jnp.where(bucket_ids == 1, 2, 4))
    half_len = bucket // 2
    random_bits = jax.random.randint(key_one, (GROUPS, 4), 0, 1 << 20)
    lengths = half_len[:, None] + random_bits % (bucket[:, None] - half_len[:, None] + 1)
    used = 4 // (bucket // MINLEN)
    full_at = jax.random.randint(key_two, (GROUPS,), 0, 1 << 20) % used
    slot_ids = jnp.arange(4)
    filled = (slot_ids[None, :] == full_at[:, None]) | (slot_ids[None, :] >= used[:, None])
    lengths = jnp.where(filled, bucket[:, None], lengths)
    return lengths.astype(jnp.int32)


def draw_bucket_shift(key, part):
    return bucket_ids_of(key)


def draw_seq_lengths(key, part):
    bucket_ids = bucket_ids_of(key)
    key = jax.random.fold_in(key, 3)
    return valid_lengths(key, bucket_ids)


def draw_enc_lengths(key, part):
    bucket_ids = bucket_ids_of(key)
    key = jax.random.fold_in(key, 4)
    return valid_lengths(key, bucket_ids)


def block_levels(rng, dims, shards, smallest, largest):
    def one(dim, parts):
        draws = jax.random.uniform(jax.random.fold_in(jax.random.fold_in(rng, 6), dim), (parts,), jnp.float32, smallest / len(shards), largest / len(shards))
        return jnp.repeat(jnp.exp(draws), dims[dim] // parts).reshape((-1,) + (1,) * (len(dims) - dim - 1))

    loudness = one(*shards[0])
    for cut in shards[1:]:
        loudness = loudness * one(*cut)
    return loudness


def scatter_about(rng, shape, spread, most, cuts=(), held_as=jnp.bfloat16):
    entries = jax.random.normal(rng, shape, jnp.float32) * spread
    if len(cuts) > 0:
        entries = block_levels(rng, shape, cuts, -0.22, 0.18) * entries
    return jnp.clip(entries, min=-most, max=most).astype(held_as)


def setup_inputs(seed: int = 0) -> dict:
    keys = jax.random.split(jax.random.key(seed), 19)
    tokens = scatter_about(keys[0], (TOKENS, D), 1.0, 6.0, ((0, 32),))
    encoder = scatter_about(keys[1], (TOKENS, D), 1.0, 6.0, ((0, 32),))
    cotangent = scatter_about(keys[2], (TOKENS, D), 1.0, 6.0, ((0, 32),))
    self_qkv = scatter_about(keys[3], (3, D, D), D ** -0.5, 0.1875, ((1, 16),))
    self_out = scatter_about(keys[4], (D, D), (D // 16) ** -0.5, 0.75, ((0, 16),))
    cross_qkv = scatter_about(keys[5], (3, D, D), D ** -0.5, 0.1875, ((1, 16),))
    cross_out = scatter_about(keys[6], (D, D), (D // 16) ** -0.5, 0.75, ((0, 16),))
    ffn_in = scatter_about(keys[7], (D, FF), D ** -0.5, 0.1875, ((0, 16),))
    ffn_out = scatter_about(keys[8], (FF, D), FF ** -0.5, 0.09375, ((0, 16),))
    adapt_down = scatter_about(keys[9], (D, ADAPT), D ** -0.5, 0.1875)
    down_bias = scatter_about(keys[10], (ADAPT,), 0.3, 2.0, (), jnp.float32)
    adapt_up = scatter_about(keys[11], (ADAPT, D), ADAPT ** -0.5, 0.25)
    up_bias = scatter_about(keys[12], (D,), 0.3, 2.0, (), jnp.float32)
    norm_gain = jnp.clip(1.0 + 0.15 * jax.random.normal(keys[13], (3, D), jnp.float32), 0.25, 1.75)
    norm_bias = scatter_about(keys[14], (3, D), 0.3, 2.0, (), jnp.float32)
    bucket_shift = draw_bucket_shift(jax.random.fold_in(keys[18], 71), 0)
    seq_lengths = draw_seq_lengths(jax.random.fold_in(keys[18], 71), 0)
    enc_lengths = draw_enc_lengths(jax.random.fold_in(keys[18], 71), 0)
    return dict(tokens=tokens, encoder=encoder, cotangent=cotangent, self_qkv=self_qkv, self_out=self_out, cross_qkv=cross_qkv, cross_out=cross_out, ffn_in=ffn_in, ffn_out=ffn_out, adapt_down=adapt_down, down_bias=down_bias, adapt_up=adapt_up, up_bias=up_bias, norm_gain=norm_gain, norm_bias=norm_bias, bucket_shift=bucket_shift, seq_lengths=seq_lengths, enc_lengths=enc_lengths)


@jax.custom_vjp
def low(v):
    return lax.optimization_barrier(v.astype(jnp.bfloat16)).astype(jnp.float32)

@jax.custom_vjp
def low_back(v):
    return v

def low_keep(v):
    return (low(v), None)

def low_pass(kept, grad):
    return (grad,)

def back_keep(v):
    return (v, None)

def back_low(kept, grad):
    return (low(grad),)
low.defvjp(low_keep, low_pass)
low_back.defvjp(back_keep, back_low)
epsilon = 1e-05
ramp_steps = 4.0
masked_score = -1e+30
highest = lax.Precision.HIGHEST

def rounded(values_in):
    return low_back(low(values_in))

def matmul(left, right):
    return jnp.dot(left, right, precision=highest)

def layer_norm(values_in, norm_scale, norm_shift):
    average = lax.optimization_barrier(jnp.mean(values_in, -1, keepdims=True))
    centred = values_in - average
    variance = lax.optimization_barrier(jnp.mean(centred * centred, -1, keepdims=True))
    return centred * lax.rsqrt(variance + epsilon) * norm_scale + norm_shift

def group_masks(bucket_code, seq_lens, enc_lens):
    bucket = MINLEN * jnp.where(bucket_code == 0, 1, jnp.where(bucket_code == 1, 2, 4))
    position = jnp.arange(TOK_DEV, dtype=jnp.int32)
    sequence = position // bucket
    inside = position - sequence * bucket
    slot_ids = jnp.arange(4, dtype=jnp.int32)
    chosen = sequence[:, None] == slot_ids[None, :]
    length = lax.optimization_barrier(jnp.sum(jnp.where(chosen, seq_lens[None, :], 0), 1))
    enc_length = lax.optimization_barrier(jnp.sum(jnp.where(chosen, enc_lens[None, :], 0), 1))
    same_seq = sequence[:, None] == sequence[None, :]
    self_mask = same_seq & (inside[None, :] <= inside[:, None]) & (inside[None, :] < length[None, :])
    cross_mask = same_seq & (inside[None, :] < enc_length[None, :])
    return (self_mask, cross_mask)

def attend(query_rows, key_rows, value_rows, mask_rows):
    rows_here = query_rows.shape[0]
    query_heads = query_rows.reshape(rows_here, HEADS, -1)
    key_heads = key_rows.reshape(key_rows.shape[0], HEADS, -1)
    value_heads = value_rows.reshape(value_rows.shape[0], HEADS, -1)
    scaling = HD ** (-0.5)
    scores = jnp.einsum('thd,shd->hts', query_heads, key_heads, precision=highest) * scaling
    scores = low_back(jnp.where(mask_rows[None], scores, masked_score))
    attn_probs = low(jax.nn.softmax(scores, axis=-1))
    attended = jnp.einsum('hts,shd->thd', attn_probs, value_heads, precision=highest)
    return attended.reshape(rows_here, -1)

def group_forward(params, frozen, branch_scale, item):
    tokens, encoder, bucket_code, seq_lens, enc_lens = item
    adapt_down, down_bias, adapt_up, up_bias, norm_gain, norm_bias = params
    self_qkv, self_out, cross_qkv, cross_out, ffn_in, ffn_out = frozen
    self_mask, cross_mask = group_masks(bucket_code, seq_lens, enc_lens)
    queries = rounded(matmul(tokens, self_qkv[0]))
    key_rows = rounded(matmul(tokens, self_qkv[1]))
    value_rows = rounded(matmul(tokens, self_qkv[2]))
    mixed = rounded(attend(queries, key_rows, value_rows, self_mask))
    first = layer_norm(tokens + low_back(matmul(mixed, self_out)), norm_gain[0], norm_bias[0])
    first_low = low(first)
    cross_queries = rounded(matmul(first_low, cross_qkv[0]))
    cross_keys = rounded(matmul(encoder, cross_qkv[1]))
    cross_values = rounded(matmul(encoder, cross_qkv[2]))
    joined = rounded(attend(cross_queries, cross_keys, cross_values, cross_mask))
    second = layer_norm(first + low_back(matmul(joined, cross_out)), norm_gain[1], norm_bias[1])
    second_low = low(second)
    inner = low_back(matmul(second_low, ffn_in))
    active = low(jax.nn.gelu(inner, approximate=False))
    feed = low_back(matmul(active, ffn_out))
    narrow = low_back(matmul(second_low, adapt_down) + down_bias)
    narrow_act = low(jax.nn.silu(narrow))
    branch = low_back(matmul(narrow_act, adapt_up) + up_bias)
    return layer_norm(second + feed + branch_scale * branch, norm_gain[2], norm_bias[2])

def reference(tokens, encoder, cotangent, self_qkv, self_out, cross_qkv, cross_out, ffn_in, ffn_out, adapt_down, down_bias, adapt_up, up_bias, norm_gain, norm_bias, bucket_shift, seq_lengths, enc_lengths):
    frozen = (self_qkv.astype(jnp.float32), self_out.astype(jnp.float32), cross_qkv.astype(jnp.float32), cross_out.astype(jnp.float32), ffn_in.astype(jnp.float32), ffn_out.astype(jnp.float32))
    step_value = jnp.float32(STEP)
    branch_scale = step_value / (step_value + ramp_steps)
    params = (adapt_down.astype(jnp.float32), down_bias, adapt_up.astype(jnp.float32), up_bias, norm_gain, norm_bias)
    token_groups = tokens.astype(jnp.float32).reshape(GROUPS, TOK_DEV, D)
    encoder_groups = encoder.astype(jnp.float32).reshape(GROUPS, TOK_DEV, D)

    def forward(params_in, token_rows, encoder_rows):

        def one_group(item):
            return group_forward(params_in, frozen, branch_scale, item)
        return lax.map(jax.checkpoint(one_group), (token_rows, encoder_rows, bucket_shift, seq_lengths, enc_lengths))
    result, pullback = jax.vjp(forward, params, token_groups, encoder_groups)
    grad_params, grad_tokens, grad_encoder = pullback(cotangent.astype(jnp.float32).reshape(GROUPS, TOK_DEV, D))
    return (result.reshape(TOKENS, D).astype(jnp.bfloat16), grad_tokens.reshape(TOKENS, D).astype(jnp.bfloat16), grad_encoder.reshape(TOKENS, D).astype(jnp.bfloat16), grad_params[0], grad_params[1], grad_params[2], grad_params[3], grad_params[4], grad_params[5])
```

```python
import functools

import jax
import jax.numpy as jnp
from jax import lax
from jax.experimental import pallas as pl
from jax.experimental.pallas import tpu as pltpu
from jax.sharding import PartitionSpec as P

HEADS = 16
STEP = 12


epsilon = 1e-05
ramp_steps = 4.0
masked_score = -1e30


def gelu_exact(values_in):
    return jax.nn.gelu(values_in, approximate=False)


def layer_stats(values_in):
    average = jnp.mean(values_in, -1, keepdims=True)
    centred = values_in - average
    inverse = lax.rsqrt(jnp.mean(centred * centred, -1, keepdims=True) + epsilon)
    return (centred * inverse, inverse)


def norm_back(grad_out, normal, inverse, norm_scale):
    grad_normal = grad_out * norm_scale
    grad_in = inverse * (
        grad_normal
        - jnp.mean(grad_normal, -1, keepdims=True)
        - normal * jnp.mean(grad_normal * normal, -1, keepdims=True)
    )
    return (grad_in, jnp.sum(grad_out * normal, 0), jnp.sum(grad_out, 0))


def mask_maker(bucket_code, seq_lens, rows_here, causal):
    bucket = rows_here // 4 * jnp.where(bucket_code == 0, 1, jnp.where(bucket_code == 1, 2, 4))
    key_pos = jnp.arange(rows_here, dtype=jnp.int32)
    key_seq = key_pos // bucket
    key_place = key_pos - key_seq * bucket
    slot_ids = jnp.arange(4, dtype=jnp.int32)
    key_len = jnp.sum(jnp.where(key_seq[:, None] == slot_ids[None, :], seq_lens[None, :], 0), 1)

    def mask_of(offset, block_rows):
        query_pos = offset + jnp.arange(block_rows, dtype=jnp.int32)
        query_seq = query_pos // bucket
        query_place = query_pos - query_seq * bucket
        allowed = (query_seq[:, None] == key_seq[None, :]) & (key_place[None, :] < key_len[None, :])
        if causal:
            allowed = allowed & (key_place[None, :] <= query_place[:, None])
        return allowed

    return mask_of


def split_heads(values_in):
    return values_in.reshape(values_in.shape[0], HEADS, -1)


def attend_forward(query_rows, key_rows, value_rows, mask_of):
    rows_here = query_rows.shape[0]
    block_rows = min(rows_here, 512)
    query_heads = split_heads(query_rows)
    key_heads = split_heads(key_rows)
    value_heads = split_heads(value_rows)
    scaling = query_heads.shape[-1] ** (-0.5)

    def one_block(offset):
        scores = (
            jnp.einsum("thd,shd->hts", query_heads, key_heads, preferred_element_type=jnp.float32)
            * scaling
        )
        scores = jnp.where(mask_of(offset, block_rows)[None], scores, masked_score)
        row_peak = jnp.max(scores, -1, keepdims=True)
        expanded = jnp.exp(scores - row_peak)
        row_total = jnp.sum(expanded, -1, keepdims=True)
        attn_probs = (expanded / row_total).astype(jnp.bfloat16)
        attended = jnp.einsum(
            "hts,shd->thd", attn_probs, value_heads, preferred_element_type=jnp.float32
        )
        return (attended.reshape(block_rows, -1), (row_peak + jnp.log(row_total))[..., 0])

    offsets = jnp.arange(rows_here // block_rows, dtype=jnp.int32) * block_rows
    attended, log_totals = lax.map(one_block, offsets)
    return (attended.reshape(rows_here, -1), log_totals)


def attend_backward(query_rows, key_rows, value_rows, grad_rows, log_totals, mask_of):
    rows_here = query_rows.shape[0]
    block_rows = min(rows_here, 512)
    query_heads = split_heads(query_rows)
    key_heads = split_heads(key_rows)
    value_heads = split_heads(value_rows)
    grad_heads = split_heads(grad_rows)
    scaling = query_heads.shape[-1] ** (-0.5)

    def one_block(running, item):
        offset, block_totals = item
        scores = (
            jnp.einsum("thd,shd->hts", query_heads, key_heads, preferred_element_type=jnp.float32)
            * scaling
        )
        scores = jnp.where(mask_of(offset, block_rows)[None], scores, masked_score)
        attn_probs = jnp.exp(scores - block_totals[..., None])
        grad_probs = jnp.einsum(
            "thd,shd->hts", grad_heads, value_heads, preferred_element_type=jnp.float32
        )
        row_delta = jnp.sum(attn_probs * grad_probs, -1, keepdims=True)
        grad_scores = (attn_probs * (grad_probs - row_delta)).astype(jnp.bfloat16)
        grad_query = (
            jnp.einsum("hts,shd->thd", grad_scores, key_heads, preferred_element_type=jnp.float32)
            * scaling
        )
        grad_keys = (
            running[0]
            + jnp.einsum(
                "hts,thd->shd", grad_scores, query_heads, preferred_element_type=jnp.float32
            )
            * scaling
        )
        grad_values = running[1] + jnp.einsum(
            "hts,thd->shd",
            attn_probs.astype(jnp.bfloat16),
            grad_heads,
            preferred_element_type=jnp.float32,
        )
        return ((grad_keys, grad_values), grad_query.reshape(block_rows, -1))

    offsets = jnp.arange(rows_here // block_rows, dtype=jnp.int32) * block_rows
    zeros_kd = jnp.zeros(key_heads.shape, jnp.float32)
    (grad_keys, grad_values), grad_query = lax.scan(
        one_block, (zeros_kd, zeros_kd), (offsets, log_totals)
    )
    return (
        grad_query.reshape(rows_here, -1).astype(jnp.bfloat16),
        grad_keys.reshape(key_rows.shape[0], -1).astype(jnp.bfloat16),
        grad_values.reshape(value_rows.shape[0], -1).astype(jnp.bfloat16),
    )


MESH = pl.DeviceIdType.MESH
LINE = 4


def nearest(place, count, rank):
    under, over = place, count - 1 - place
    both = jnp.minimum(under, over)
    paired = jnp.where(rank % 2 == 1, place - (rank + 1) // 2, place + rank // 2)
    alone = jnp.where(over > under, place + rank - both, place - (rank - both))
    return jnp.where(rank <= 2 * both, paired, alone)


class Gather:
    def __init__(self, count, views, send_sem, recv_sem):
        self.views, self.send_sem, self.recv_sem = views, send_sem, recv_sem
        self.line = min(LINE, count // 2)
        self.wide = count // (2 * self.line)
        index = lax.axis_index("fsdp")
        self.dp = lax.axis_index("dp")
        self.core = index % 2
        self.x = (index // 2) % self.wide
        self.z = index // (2 * self.wide)
        self.plane = self.dp % 2
        self.other_core = (self.place(self.z, self.x, 1 - self.core), self.dp)
        self.other_plane = (index, self.dp + 1 - 2 * self.plane)
        self.sends = []
        self.counts = [0] * len(views)

    def place(self, z, x, core):
        return (z * self.wide + x) * 2 + core

    def enter(self):
        barrier = pltpu.get_barrier_semaphore()

        def greet(target):
            pl.semaphore_signal(barrier, inc=1, device_id=target, device_id_type=MESH)

        greet(self.other_core)
        greet(self.other_plane)
        total = 2
        for along, size, target in (
            (self.z, self.line, lambda to: (self.place(to, self.x, self.core), self.dp)),
            (self.x, self.wide, lambda to: (self.place(self.z, to, self.core), self.dp)),
        ):
            for step in (-1, 1):
                inside = (along + step >= 0) & (along + step < size)

                @pl.when(inside)
                def _():
                    greet(target(along + step))

                total = total + inside.astype(jnp.int32)
        pl.semaphore_wait(barrier, total)

    def send(self, phase, core, z, x, kind, first, units, target, when=None):
        view = self.views[phase](self.place(z, x, core), first, units)
        slot = self.counts[phase]
        self.counts[phase] += 1
        copy = pltpu.make_async_remote_copy(
            src_ref=view,
            dst_ref=view,
            send_sem=self.send_sem.at[phase, slot],
            recv_sem=self.recv_sem.at[phase, core, z * self.wide + x, kind],
            device_id=target,
            device_id_type=MESH,
        )
        if when is None:
            copy.start()
        else:
            pl.when(when)(copy.start)
        self.sends.append((copy, when))

    def arrive(self, phase, core, z, x, kind, first, units):
        view = self.views[phase](self.place(z, x, core), first, units)
        pltpu.make_async_copy(view, view, self.recv_sem.at[phase, core, z * self.wide + x, kind]).wait()

    def spans(self, other):
        p = self.plane
        if other:
            return ((2 * p, 2), (4 + p, 3), (2 - 2 * p, 2), (7 - 3 * p, 1))
        return ((2 * p, 2), (4, 4), (2 - 2 * p, 2))

    def along_z(self, step):
        return (self.place(self.z + step, self.x, self.core), self.dp)

    def along_x(self, step):
        return (self.place(self.z, self.x + step, self.core), self.dp)

    def own(self, phase):
        at = (phase, self.core, self.z, self.x)
        spans = self.spans(False)
        cross = self.spans(True)
        for kind in (0, 1):
            self.send(*at, kind, *spans[kind], self.along_z(1), self.z < self.line - 1)
            self.send(*at, kind, *spans[kind], self.along_z(-1), self.z > 0)
            self.over_x(at, kind, cross[kind])
        self.send(*at, 0, 0, 8, self.other_core)

    def over_x(self, at, kind, span):
        if self.wide == 2:
            self.send(*at, kind, *span, self.along_x(1 - 2 * self.x))
            return
        self.send(*at, kind, *span, self.along_x(1), self.x < self.wide - 1)
        self.send(*at, kind, *span, self.along_x(-1), self.x > 0)

    def ticks(self, phase):
        for step in range(1, self.line + self.wide):
            if step < self.line:
                yield from self.from_z(phase, nearest(self.z, self.line, step))
            for apart in range(1, self.wide):
                if 0 <= step - apart < self.line:
                    z_from = nearest(self.z, self.line, step - apart)
                    yield from self.from_x(phase, z_from, nearest(self.x, self.wide, apart))
            if 0 <= step - 1 < self.line and step > 1:
                yield from self.from_plane(phase, nearest(self.z, self.line, step - 1), self.x, False)
            for apart in range(1, self.wide):
                if 0 <= step - apart - 1 < self.line:
                    z_from = nearest(self.z, self.line, step - apart - 1)
                    yield from self.from_plane(phase, z_from, nearest(self.x, self.wide, apart), True)

    def from_z(self, phase, z_from):
        at = (phase, self.core, z_from, self.x)
        upward = z_from < self.z
        onward = (upward & (self.z < self.line - 1)) | (~upward & (self.z > 0))
        target = self.along_z(jnp.where(upward, 1, -1))
        spans, cross = self.spans(False), self.spans(True)
        for kind in (0, 1):
            self.arrive(*at, kind, *spans[kind])
            self.send(*at, kind, *spans[kind], target, onward)
            self.over_x(at, kind, cross[kind])
            if kind == 0:
                self.send(*at, 2, *spans[kind], self.other_plane)
            self.send(*at, kind, *spans[kind], self.other_core)
            yield

    def from_x(self, phase, z_from, x_from):
        at = (phase, self.core, z_from, x_from)
        cross = self.spans(True)
        p = self.plane
        upward = x_from < self.x
        onward = (upward & (self.x < self.wide - 1)) | (~upward & (self.x > 0))
        target = self.along_x(jnp.where(upward, 1, -1))
        for kind in (0, 1):
            self.arrive(*at, kind, *cross[kind])
            if self.wide > 2:
                self.send(*at, kind, *cross[kind], target, onward)
            self.send(*at, kind + 2, *(cross[0] if kind == 0 else (4 + 3 * p, 1)), self.other_plane)
            self.send(*at, kind, *cross[kind], self.other_core)
            yield

    def from_plane(self, phase, z_from, x_from, other):
        at = (phase, self.core, z_from, x_from)
        spans = self.spans(other)
        for kind in range(2, len(spans)):
            self.arrive(*at, kind, *spans[kind])
            self.send(*at, kind, *spans[kind], self.other_core)
        yield

    def arrived(self, phase, z, x):
        def pieces(other):
            for kind, span in enumerate(self.spans(other)):
                self.arrive(phase, 1 - self.core, z, x, kind, *span)

        own_chip = (z == self.z) & (x == self.x)
        same = (x == self.x) & (z != self.z)
        pl.when(own_chip)(lambda: self.arrive(phase, 1 - self.core, z, x, 0, 0, 8))
        pl.when(same)(lambda: pieces(False))
        pl.when(x != self.x)(lambda: pieces(True))

    def finish(self):
        for copy, when in self.sends:
            if when is None:
                copy.wait_send()
            else:
                pl.when(when)(copy.wait_send)


def sends_per_phase(count):
    line = min(LINE, count // 2)
    wide = count // (2 * line)
    across = 1 if wide == 2 else 2
    each = 2 * (2 + across) + 1
    return line * each + (wide - 1) * line * 2 * (1 + across) + (line - 1) + (wide - 1) * line * 2


def gather_kernel(count, self_qkv, self_out, cross_qkv, cross_out, ffn_in, ffn_out, attn, wide_in, wide_out, send_sem, recv_sem, own_sem):
    index = lax.axis_index("fsdp")
    thin = self_out.shape[0]
    deep = ffn_out.shape[0]
    unit = self_out.shape[1] // 8
    unit_in = ffn_in.shape[1] // 8

    def rows(start, many):
        return pl.ds(pl.multiple_of(start * many, many), many)

    def columns(first, units, width):
        return pl.ds(pl.multiple_of(first * width, width), units * width)

    views = (
        lambda f, first, units: attn.at[pl.ds(0, 3), rows(f, thin), columns(first, units, unit)],
        lambda f, first, units: attn.at[pl.ds(3, 5), rows(f, thin), columns(first, units, unit)],
        lambda f, first, units: wide_in.at[rows(f, thin), columns(first, units, unit_in)],
        lambda f, first, units: wide_out.at[rows(f, deep), columns(first, units, unit)],
    )
    mine = rows(index, thin)
    owned = [
        [(self_qkv, attn.at[pl.ds(0, 3), mine])],
        [(self_out, attn.at[3, mine]), (cross_qkv, attn.at[pl.ds(4, 3), mine]), (cross_out, attn.at[7, mine])],
        [(ffn_in, wide_in.at[mine])],
        [(ffn_out, wide_out.at[rows(index, deep)])],
    ]
    copies = []
    for group in owned:
        copies.append([])
        for one, to in group:
            copy = pltpu.make_async_copy(one, to, own_sem.at[sum(map(len, copies))])
            copy.start()
            copies[-1].append(copy)
    gather = Gather(count, views, send_sem, recv_sem)
    gather.enter()

    def begin(phase):
        for copy in copies[phase]:
            copy.wait()
        gather.own(phase)

    begin(0)
    for phase in range(4):
        if phase < 3:
            begin(phase + 1)
        for _ in gather.ticks(phase):
            pass
    for phase in range(4):
        for z in range(gather.line):
            for x in range(gather.wide):
                gather.arrived(phase, z, x)
    gather.finish()


def gather_all(count, *parts):
    line = min(LINE, count // 2)
    return pl.pallas_call(
        functools.partial(gather_kernel, count),
        out_shape=[
            jax.ShapeDtypeStruct((8, 1024, 1024), jnp.bfloat16),
            jax.ShapeDtypeStruct((parts[4].shape[0] * count, parts[4].shape[1]), jnp.bfloat16),
            jax.ShapeDtypeStruct((parts[5].shape[0] * count, parts[5].shape[1]), jnp.bfloat16),
        ],
        in_specs=[pl.BlockSpec(memory_space=pl.ANY)] * 6,
        out_specs=[pl.BlockSpec(memory_space=pl.ANY)] * 3,
        scratch_shapes=[
            pltpu.SemaphoreType.DMA((4, sends_per_phase(count))),
            pltpu.SemaphoreType.DMA((4, 2, count // 2, 4)),
            pltpu.SemaphoreType.DMA((6,)),
        ],
        compiler_params=pltpu.CompilerParams(collective_id=0, has_side_effects=True),
        name="gather_weights",
    )(*parts)


def local(
    tokens,
    encoder,
    cotangent,
    self_qkv,
    self_out,
    cross_qkv,
    cross_out,
    ffn_in,
    ffn_out,
    adapt_down,
    down_bias,
    adapt_up,
    up_bias,
    norm_gain,
    norm_bias,
    bucket_shift,
    seq_lengths,
    enc_lengths,
):
    rows_here = tokens.shape[0]
    step_value = jnp.float32(STEP)
    branch_scale = step_value / (step_value + ramp_steps)
    self_mask = mask_maker(bucket_shift[0], seq_lengths[0], rows_here, True)
    cross_mask = mask_maker(bucket_shift[0], enc_lengths[0], rows_here, False)
    attn_whole, ffn_whole_in, ffn_whole_out = gather_all(
        lax.axis_size("fsdp"), self_qkv, self_out, cross_qkv, cross_out, ffn_in, ffn_out
    )
    self_whole, self_proj = attn_whole[:3], attn_whole[3]
    projected = jnp.einsum(
        "td,kde->kte", tokens, self_whole, preferred_element_type=jnp.float32
    ).astype(jnp.bfloat16)
    queries, key_rows, value_rows = (projected[0], projected[1], projected[2])
    mixed, self_totals = attend_forward(queries, key_rows, value_rows, self_mask)
    mixed = mixed.astype(jnp.bfloat16)
    normal_one, inverse_one = layer_stats(
        tokens.astype(jnp.float32) + jnp.dot(mixed, self_proj, preferred_element_type=jnp.float32)
    )
    first = normal_one * norm_gain[0] + norm_bias[0]
    first_low = first.astype(jnp.bfloat16)
    cross_whole, cross_proj = attn_whole[4:7], attn_whole[7]
    cross_queries = jnp.dot(first_low, cross_whole[0], preferred_element_type=jnp.float32).astype(
        jnp.bfloat16
    )
    cross_pairs = jnp.einsum(
        "td,kde->kte", encoder, cross_whole[1:], preferred_element_type=jnp.float32
    ).astype(jnp.bfloat16)
    joined, cross_totals = attend_forward(cross_queries, cross_pairs[0], cross_pairs[1], cross_mask)
    joined = joined.astype(jnp.bfloat16)
    normal_two, inverse_two = layer_stats(
        first + jnp.dot(joined, cross_proj, preferred_element_type=jnp.float32)
    )
    second = normal_two * norm_gain[1] + norm_bias[1]
    second_low = second.astype(jnp.bfloat16)
    inner = jnp.dot(second_low, ffn_whole_in, preferred_element_type=jnp.float32)
    active = gelu_exact(inner).astype(jnp.bfloat16)
    narrow = jnp.dot(second_low, adapt_down, preferred_element_type=jnp.float32) + down_bias
    narrow_act = jax.nn.silu(narrow).astype(jnp.bfloat16)
    branch = jnp.dot(narrow_act, adapt_up, preferred_element_type=jnp.float32) + up_bias
    sum_three = (
        second
        + jnp.dot(active, ffn_whole_out, preferred_element_type=jnp.float32)
        + branch_scale * branch
    )
    normal_three, inverse_three = layer_stats(sum_three)
    output = (normal_three * norm_gain[2] + norm_bias[2]).astype(jnp.bfloat16)
    grad_three, gain_three, bias_three = norm_back(
        cotangent.astype(jnp.float32), normal_three, inverse_three, norm_gain[2]
    )
    grad_feed = grad_three.astype(jnp.bfloat16)
    grad_branch = (branch_scale * grad_three).astype(jnp.bfloat16)
    grad_up = jnp.einsum("ta,td->ad", narrow_act, grad_branch, preferred_element_type=jnp.float32)
    grad_upb = jnp.sum(grad_branch.astype(jnp.float32), 0)
    grad_act = jnp.einsum("td,ad->ta", grad_branch, adapt_up, preferred_element_type=jnp.float32)
    grad_narrow = jax.vjp(jax.nn.silu, narrow)[1](grad_act)[0].astype(jnp.bfloat16)
    grad_down = jnp.einsum("td,ta->da", second_low, grad_narrow, preferred_element_type=jnp.float32)
    grad_downb = jnp.sum(grad_narrow.astype(jnp.float32), 0)
    ffn_back_in, ffn_back_out = (ffn_whole_in, ffn_whole_out)
    grad_active = jnp.einsum(
        "td,fd->tf", grad_feed, ffn_back_out, preferred_element_type=jnp.float32
    )
    grad_inner = jax.vjp(gelu_exact, inner)[1](grad_active)[0].astype(jnp.bfloat16)
    grad_second = (
        grad_three
        + jnp.einsum("tf,df->td", grad_inner, ffn_back_in, preferred_element_type=jnp.float32)
        + jnp.einsum("ta,da->td", grad_narrow, adapt_down, preferred_element_type=jnp.float32)
    )
    grad_two, gain_two, bias_two = norm_back(grad_second, normal_two, inverse_two, norm_gain[1])
    cross_back, cross_back_proj = (cross_whole, cross_proj)
    grad_joined = jnp.einsum(
        "td,ed->te",
        grad_two.astype(jnp.bfloat16),
        cross_back_proj,
        preferred_element_type=jnp.float32,
    ).astype(jnp.bfloat16)
    grad_cquery, grad_ckeys, grad_cvalues = attend_backward(
        cross_queries, cross_pairs[0], cross_pairs[1], grad_joined, cross_totals, cross_mask
    )
    grad_first = grad_two + jnp.einsum(
        "te,de->td", grad_cquery, cross_back[0], preferred_element_type=jnp.float32
    )
    grad_encoder = (
        jnp.einsum("te,de->td", grad_ckeys, cross_back[1], preferred_element_type=jnp.float32)
        + jnp.einsum("te,de->td", grad_cvalues, cross_back[2], preferred_element_type=jnp.float32)
    ).astype(jnp.bfloat16)
    grad_one, gain_one, bias_one = norm_back(grad_first, normal_one, inverse_one, norm_gain[0])
    self_back, self_back_proj = (self_whole, self_proj)
    grad_mixed = jnp.einsum(
        "td,ed->te",
        grad_one.astype(jnp.bfloat16),
        self_back_proj,
        preferred_element_type=jnp.float32,
    ).astype(jnp.bfloat16)
    grad_query, grad_keys, grad_values = attend_backward(
        queries, key_rows, value_rows, grad_mixed, self_totals, self_mask
    )
    grad_tokens = grad_one + jnp.einsum(
        "te,de->td", grad_query, self_back[0], preferred_element_type=jnp.float32
    )
    grad_tokens = grad_tokens + jnp.einsum(
        "te,de->td", grad_keys, self_back[1], preferred_element_type=jnp.float32
    )
    grad_tokens = (
        grad_tokens
        + jnp.einsum("te,de->td", grad_values, self_back[2], preferred_element_type=jnp.float32)
    ).astype(jnp.bfloat16)
    gain_grads = jnp.stack([gain_one, gain_two, gain_three])
    bias_grads = jnp.stack([bias_one, bias_two, bias_three])
    summed = lax.psum(
        (grad_down, grad_downb, grad_up, grad_upb, gain_grads, bias_grads), ("fsdp", "dp")
    )
    return (
        output,
        grad_tokens,
        grad_encoder,
        summed[0],
        summed[1],
        summed[2],
        summed[3],
        summed[4],
        summed[5],
    )


def solution(mesh):
    placed = (
        P(("fsdp", "dp"), None),
        P(("fsdp", "dp"), None),
        P(("fsdp", "dp"), None),
        P(None, "fsdp", None),
        P("fsdp", None),
        P(None, "fsdp", None),
        P("fsdp", None),
        P("fsdp", None),
        P("fsdp", None),
        P(),
        P(),
        P(),
        P(),
        P(),
        P(),
        P(("fsdp", "dp")),
        P(("fsdp", "dp"), None),
        P(("fsdp", "dp"), None),
    )
    return jax.shard_map(
        local,
        mesh=mesh,
        in_specs=placed,
        out_specs=(
            P(("fsdp", "dp"), None),
            P(("fsdp", "dp"), None),
            P(("fsdp", "dp"), None),
            P(),
            P(),
            P(),
            P(),
            P(),
            P(),
        ),
        check_vma=False,
    )
```

```python
import functools

import jax
import jax.numpy as jnp
from jax import lax
from jax.experimental import pallas as pl
from jax.experimental.pallas import tpu as pltpu
from jax.sharding import PartitionSpec as P

HEADS = 16
STEP = 12
LINE = 4
MESH = pl.DeviceIdType.MESH
ANY = pl.BlockSpec(memory_space=pl.ANY)
SMEM = pl.BlockSpec(memory_space=pltpu.SMEM)
bf16 = jnp.bfloat16
f32 = jnp.float32

epsilon = 1e-05
ramp_steps = 4.0
masked_score = -1e30
lead = 1.0


def dot(left, right):
    return jnp.dot(left, right, preferred_element_type=f32)


def dot_t(left, right):
    return lax.dot_general(left, right, (((1,), (1,)), ((), ())), preferred_element_type=f32)


def t_dot(left, right):
    return lax.dot_general(left, right, (((0,), (0,)), ((), ())), preferred_element_type=f32)


def part(index, size):
    return pl.ds(pl.multiple_of(index * size, size), size)


def layer_stats(values_in):
    average = jnp.mean(values_in, -1, keepdims=True)
    centred = values_in - average
    inverse = lax.rsqrt(jnp.mean(centred * centred, -1, keepdims=True) + epsilon)
    return (centred * inverse, inverse)


def norm_back(grad_out, normal, inverse, norm_scale):
    grad_normal = grad_out * norm_scale
    return inverse * (
        grad_normal
        - jnp.mean(grad_normal, -1, keepdims=True)
        - normal * jnp.mean(grad_normal * normal, -1, keepdims=True)
    )


def nearest(place, count, rank):
    under, over = place, count - 1 - place
    both = jnp.minimum(under, over)
    paired = jnp.where(rank % 2 == 1, place - (rank + 1) // 2, place + rank // 2)
    alone = jnp.where(over > under, place + rank - both, place - (rank - both))
    return jnp.where(rank <= 2 * both, paired, alone)


def mesh_shape(count):
    line = min(LINE, count // 2)
    return line, count // (2 * line)


def sends_per_phase(count):
    line, wide = mesh_shape(count)
    across = 1 if wide == 2 else 2
    each = 2 * (2 + across) + 1
    return line * each + (wide - 1) * line * 2 * (1 + across) + (line - 1) + (wide - 1) * line * 2


class Gather:
    def __init__(self, count, views, send_sem, recv_sem):
        self.views, self.send_sem, self.recv_sem = views, send_sem, recv_sem
        self.line, self.wide = mesh_shape(count)
        index = lax.axis_index("fsdp")
        self.dp = lax.axis_index("dp")
        self.core = index % 2
        self.x = (index // 2) % self.wide
        self.z = index // (2 * self.wide)
        p = self.dp % 2
        self.other_core = (self.place(self.z, self.x, 1 - self.core), self.dp)
        self.other_plane = (index, self.dp + 1 - 2 * p)
        self.same = ((2 * p, 2), (4, 4), (2 - 2 * p, 2))
        self.cross = ((2 * p, 2), (4 + p, 3), (2 - 2 * p, 2), (7 - 3 * p, 1))
        self.single = (4 + 3 * p, 1)
        self.z_up = (self.along_z(1), self.z < self.line - 1)
        self.z_down = (self.along_z(-1), self.z > 0)
        if self.wide == 2:
            self.x_ways = ((self.along_x(1 - 2 * self.x), None),)
        else:
            self.x_ways = ((self.along_x(1), self.x < self.wide - 1), (self.along_x(-1), self.x > 0))
        self.sends = []
        self.counts = [0] * len(views)
        self.steps = self.plan()
        self.done = 0

    def place(self, z, x, core):
        return (z * self.wide + x) * 2 + core

    def along_z(self, step):
        return (self.place(self.z + step, self.x, self.core), self.dp)

    def along_x(self, step):
        return (self.place(self.z, self.x + step, self.core), self.dp)

    def enter(self):
        barrier = pltpu.get_barrier_semaphore()

        def greet(target):
            pl.semaphore_signal(barrier, inc=1, device_id=target, device_id_type=MESH)

        greet(self.other_core)
        greet(self.other_plane)
        total = 2
        for target, inside in (self.z_up, self.z_down) + self.x_ways:
            if inside is None:
                greet(target)
                total = total + 1
            else:
                pl.when(inside)(functools.partial(greet, target))
                total = total + inside.astype(jnp.int32)
        pl.semaphore_wait(barrier, total)

    def copy(self, at, kind, span, slot, target):
        phase, core, z, x = at
        view = self.views[phase](self.place(z, x, core), *span)
        return pltpu.make_async_remote_copy(
            src_ref=view,
            dst_ref=view,
            send_sem=self.send_sem.at[phase, slot],
            recv_sem=self.recv_sem.at[phase, core, z * self.wide + x, kind],
            device_id=target,
            device_id_type=MESH,
        )

    def send(self, at, kind, span, target, when=None):
        slot = self.counts[at[0]]
        self.counts[at[0]] += 1
        remake = functools.partial(self.copy, at, kind, span, slot, target)
        if when is None:
            remake().start()
        else:
            pl.when(when)(lambda: remake().start())
        self.sends.append((remake, when))

    def arrive(self, at, kind, span):
        phase, core, z, x = at
        view = self.views[phase](self.place(z, x, core), *span)
        pltpu.make_async_copy(view, view, self.recv_sem.at[phase, core, z * self.wide + x, kind]).wait()

    def plan(self):
        span = self.line - 1
        steps = []
        for phase in range(len(self.views)):
            base = span * phase

            def add(when, makers):
                steps.extend((base + when, phase, maker) for maker in makers)

            for far in range(self.line):
                z_from = nearest(self.z, self.line, far)
                if far:
                    add(far, self.from_z((phase, self.core, z_from, self.x)))
                    add(far + 1.1, self.from_plane((phase, self.core, z_from, self.x), self.same))
                for apart in range(1, self.wide):
                    at = (phase, self.core, z_from, nearest(self.x, self.wide, apart))
                    add(far + apart + 0.05, self.from_x(at))
                    add(far + apart + 1.15, self.from_plane(at, self.cross))
            if phase:
                add(-lead, [functools.partial(self.own, phase)])
        return sorted(steps, key=lambda item: item[0])

    def own(self, phase):
        at = (phase, self.core, self.z, self.x)
        for kind in (0, 1):
            self.send(at, kind, self.same[kind], *self.z_up)
            self.send(at, kind, self.same[kind], *self.z_down)
            self.over_x(at, kind)
        self.send(at, 0, (0, 8), self.other_core)

    def over_x(self, at, kind):
        for way in self.x_ways:
            self.send(at, kind, self.cross[kind], *way)

    def from_z(self, at):
        upward = at[2] < self.z
        onward = (upward & self.z_up[1]) | (~upward & self.z_down[1])
        target = self.along_z(jnp.where(upward, 1, -1))

        def step(kind):
            self.arrive(at, kind, self.same[kind])
            self.send(at, kind, self.same[kind], target, onward)
            self.over_x(at, kind)
            if kind == 0:
                self.send(at, 2, self.same[0], self.other_plane)
            self.send(at, kind, self.same[kind], self.other_core)

        return [functools.partial(step, 0), functools.partial(step, 1)]

    def from_x(self, at):
        upward = at[3] < self.x
        onward = (upward & (self.x < self.wide - 1)) | (~upward & (self.x > 0))
        target = self.along_x(jnp.where(upward, 1, -1))

        def step(kind):
            self.arrive(at, kind, self.cross[kind])
            if self.wide > 2:
                self.send(at, kind, self.cross[kind], target, onward)
            self.send(at, kind + 2, self.cross[0] if kind == 0 else self.single, self.other_plane)
            self.send(at, kind, self.cross[kind], self.other_core)

        return [functools.partial(step, 0), functools.partial(step, 1)]

    def from_plane(self, at, spans):
        def step():
            for kind in range(2, len(spans)):
                self.arrive(at, kind, spans[kind])
                self.send(at, kind, spans[kind], self.other_core)

        return [step]

    def tick(self, many=1):
        for _ in range(many):
            if self.done < len(self.steps):
                self.done += 1
                self.steps[self.done - 1][2]()

    def take(self, many):
        first = self.done
        self.done = min(len(self.steps), first + many)
        return [step[2] for step in self.steps[first : self.done]]

    def need(self, phase):
        last = max(i for i, step in enumerate(self.steps) if step[1] == phase)
        self.tick(last + 1 - self.done)
        for z in range(self.line):
            for x in range(self.wide):
                self.other_half(phase, z, x)

    def other_half(self, phase, z, x):
        at = (phase, 1 - self.core, z, x)

        def pieces(spans):
            for kind, span in enumerate(spans):
                self.arrive(at, kind, span)

        own_chip = (z == self.z) & (x == self.x)
        pl.when(own_chip)(lambda: self.arrive(at, 0, (0, 8)))
        pl.when((x == self.x) & (z != self.z))(lambda: pieces(self.same))
        pl.when(x != self.x)(lambda: pieces(self.cross))

    def finish(self):
        for remake, when in self.sends:
            if when is None:
                remake().wait_send()
            else:
                pl.when(when)(lambda: remake().wait_send())


def place_masks(bias, shift, lengths, causal):
    rows = bias.shape[0]
    wide = 128
    bits = shift + (rows // 4).bit_length() - 1

    @pl.loop(0, rows // wide)
    def _(block):
        shape = (wide, rows)
        key = lax.broadcasted_iota(jnp.int32, shape, 0) + block * wide
        query = lax.broadcasted_iota(jnp.int32, shape, 1)
        key_seq = lax.shift_right_logical(key, jnp.full(shape, bits, jnp.int32))
        query_seq = lax.shift_right_logical(query, jnp.full(shape, bits, jnp.int32))
        start = lax.shift_left(key_seq, jnp.full(shape, bits, jnp.int32))
        length = jnp.zeros(shape, jnp.int32)
        for slot in range(4):
            length = jnp.where(key_seq == slot, lengths[0, slot], length)
        allowed = (key_seq == query_seq) & (key - start < length)
        if causal:
            allowed = allowed & (key <= query)
        bias[part(block, wide), :] = jnp.where(allowed, 0.0, masked_score)


def tiles_of(rows, causal):
    half = rows // 2
    return ((0, half, half), (half, half, rows)) if causal else ((0, rows, rows),)


def head_lanes(values, half):
    lane = lax.broadcasted_iota(jnp.int32, values.shape, 1)
    return jnp.where((lane // 64) == half, values, jnp.zeros_like(values))


def attend_pair(pair, query, key, value_t, bias, probs, out, causal):
    rows = query.shape[0]
    columns = part(pair, 128)
    keys = key[:, columns]
    queries = query[:, columns]
    halves = []
    for half in range(2):
        head_queries = head_lanes(queries, half)
        lanes = pl.ds(pl.multiple_of(pair * 128 + half * 64, 64), 64)
        pieces = []
        for first, many, deep in tiles_of(rows, causal):
            scores = dot_t(keys[:deep], head_queries[first : first + many])
            scores = scores + bias[:deep, first : first + many]
            expanded = jnp.exp(scores - jnp.max(scores, 0, keepdims=True))
            total = jnp.sum(expanded, 0, keepdims=True)
            block = (expanded * (1.0 / total)).astype(bf16)
            probs[half, :deep, first : first + many] = block
            pieces.append(dot(value_t[lanes, :deep], block))
        halves.append(jnp.concatenate(pieces, 1) if len(pieces) > 1 else pieces[0])
    both = jnp.concatenate(halves, 0).astype(bf16)
    out[:, columns] = both.T


def gelu_both(inner):
    spread = 0.5 + 0.5 * lax.erf(inner * (0.5**0.5))
    bell = jnp.exp(inner * inner * -0.5) * 0.3989422804014327
    return inner * spread, spread + inner * bell


def forward_kernel(
    count,
    tokens,
    encoder,
    cotangent,
    self_qkv,
    self_out,
    cross_qkv,
    cross_out,
    ffn_in,
    ffn_out,
    adapt_down,
    down_bias,
    adapt_up,
    up_bias,
    norm_gain,
    norm_bias,
    shift,
    seq_lengths,
    enc_lengths,
    output,
    attn_kept,
    self_kept,
    self_key_kept,
    self_probs,
    cross_kept,
    cross_key_kept,
    cross_probs,
    normal_kept,
    inverse_kept,
    grad_kept,
    adapt_grads,
    vector_grads,
    attn,
    wide_in,
    wide_out,
    held,
    turned,
    low,
    tok,
    enc,
    bias,
    probs,
    total,
    normal,
    inverse,
    narrow_act,
    narrow_slope,
    narrow_grad,
    down,
    up,
    vectors,
    packed,
    send_sem,
    recv_sem,
    own_sem,
    load_sem,
    kept_sem,
    probs_sem,
):
    index = lax.axis_index("fsdp")
    thin = self_out.shape[0]
    deep = ffn_out.shape[0]
    rows, model = tok.shape
    unit = model // 8
    unit_in = ffn_in.shape[1] // 8
    hidden = ffn_in.shape[1]
    step_value = jnp.float32(STEP)
    branch_scale = step_value / (step_value + ramp_steps)

    def columns_of(first, units, width):
        return pl.ds(pl.multiple_of(first * width, width), units * width)

    views = (
        lambda f, first, units: attn.at[pl.ds(0, 3), part(f, thin), columns_of(first, units, unit)],
        lambda f, first, units: attn.at[pl.ds(3, 5), part(f, thin), columns_of(first, units, unit)],
        lambda f, first, units: wide_in.at[part(f, thin), columns_of(first, units, unit_in)],
        lambda f, first, units: wide_out.at[part(f, deep), columns_of(first, units, unit)],
    )
    mine = part(index, thin)
    owned = (
        ((self_qkv, attn.at[pl.ds(0, 3), mine]),),
        ((self_out, attn.at[3, mine]), (cross_qkv, attn.at[pl.ds(4, 3), mine]), (cross_out, attn.at[7, mine])),
        ((ffn_in, wide_in.at[mine]),),
        ((ffn_out, wide_out.at[part(index, deep)]),),
    )
    loads = []
    for group in owned:
        for source, target in group:
            loads.append(pltpu.make_async_copy(source, target, own_sem.at[len(loads)]))
    for load in loads:
        load.start()
    load_tok = pltpu.make_async_copy(tokens, tok, load_sem.at[0])
    load_enc = pltpu.make_async_copy(encoder, enc, load_sem.at[1])
    load_down = pltpu.make_async_copy(adapt_down, down, load_sem.at[2])
    load_up = pltpu.make_async_copy(adapt_up, up, load_sem.at[3])
    for load in (load_tok, load_enc, load_down, load_up):
        load.start()
    gather = Gather(count, views, send_sem, recv_sem)
    gather.enter()
    loads[0].wait()
    gather.own(0)
    for load in loads[1:]:
        load.wait()
    kept = []

    def keep(source, target):
        copy = pltpu.make_async_copy(source, target, kept_sem.at[len(kept)])
        copy.start()
        kept.append(copy)
        return copy

    def project(source, target, weight, scale=None):
        for block in range(2):
            columns = pl.ds(block * (model // 2), model // 2)
            product = dot(source[...], attn[weight, :, columns]).astype(bf16)
            target[:, columns] = product if scale is None else product * scale
            gather.tick()

    def attention(query, key, value, mixed, saved, key_saved, probs_saved, causal):
        turned[0] = value[...].T
        gather.tick()
        turned[1] = (key[...] * bf16(0.125)).T
        gather.tick()
        keep(turned.at[1], key_saved)
        steps = gather.take(16)

        def out_copy(pair, slot):
            return pltpu.make_async_copy(probs.at[slot], probs_saved.at[pl.ds(pair * 2, 2)], probs_sem.at[slot])

        pairs = HEADS // 2

        @pl.loop(0, pairs)
        def _(pair):
            slot = pair % 2
            pl.when(pair >= 2)(lambda: out_copy(pair - 2, slot).wait())
            attend_pair(pair, query, key, turned.at[0], bias, probs.at[slot], mixed, causal)
            out_copy(pair, slot).start()
            for at in range(pairs):
                mine_now = steps[2 * at : 2 * at + 2]

                @pl.when(pair == at)
                def _():
                    for step in mine_now:
                        step()

        for pair in (pairs - 2, pairs - 1):
            out_copy(pair, pair % 2).wait()

    place_masks(bias, shift[0], seq_lengths, True)
    load_tok.wait()
    gather.need(0)
    keep(attn.at[pl.ds(0, 3)], attn_kept.at[pl.ds(0, 3)])
    project(tok, held.at[0], 0, bf16(0.125))
    project(tok, held.at[1], 1)
    project(tok, held.at[2], 2)
    attention(held.at[0], held.at[1], held.at[2], held.at[3], self_kept, self_key_kept, self_probs, True)
    keep(held.at[pl.ds(0, 4)], self_kept)
    turned_out = kept[1]

    gather.need(1)
    keep(attn.at[pl.ds(3, 5)], attn_kept.at[pl.ds(3, 5)])
    block_rows = 128
    blocks = rows // block_rows
    for half in range(2):
        columns = pl.ds(half * (model // 2), model // 2)
        total[:, columns] = tok[:, columns].astype(f32) + dot(held[3], attn[3, :, columns])
        gather.tick()

    @pl.loop(0, blocks)
    def _(block):
        here = part(block, block_rows)
        normal_one, inverse_one = layer_stats(total[here, :])
        normal[here, :] = normal_one
        inverse[here, :] = jnp.broadcast_to(inverse_one, (block_rows, 128))
        low[here, :] = (normal_one * norm_gain[0:1, :] + norm_bias[0:1, :]).astype(bf16)

    normal_out = keep(normal, normal_kept)
    inverse_out = keep(inverse, inverse_kept)
    place_masks(bias, shift[0], enc_lengths, False)
    load_enc.wait()
    turned_out.wait()
    project(low, held.at[4], 4, bf16(0.125))
    project(enc, held.at[5], 5)
    project(enc, held.at[6], 6)
    load_cot = pltpu.make_async_copy(cotangent, enc, load_sem.at[1])
    load_cot.start()
    attention(held.at[4], held.at[5], held.at[6], held.at[7], cross_kept, cross_key_kept, cross_probs, False)
    keep(held.at[pl.ds(4, 4)], cross_kept)
    for half in range(2):
        columns = pl.ds(half * (model // 2), model // 2)
        first = normal[:, columns] * norm_gain[0:1, columns] + norm_bias[0:1, columns]
        total[:, columns] = first + dot(held[7], attn[7, :, columns])
        gather.tick()
    normal_out.wait()
    inverse_out.wait()

    @pl.loop(0, blocks)
    def _(block):
        here = part(block, block_rows)
        normal_two, inverse_two = layer_stats(total[here, :])
        normal[here, :] = normal_two
        inverse[here, :] = jnp.broadcast_to(inverse_two, (block_rows, 128))
        second = normal_two * norm_gain[1:2, :] + norm_bias[1:2, :]
        low[here, :] = second.astype(bf16)
        total[here, :] = second

    load_down.wait()
    load_up.wait()
    narrow = dot(low[...], down[...]) + down_bias[...]
    gate = 1.0 / (1.0 + jnp.exp(-narrow))
    narrow_act[...] = (narrow * gate).astype(bf16)
    narrow_slope[...] = gate * (1.0 + narrow * (1.0 - gate))
    gather.tick()
    for half in range(2):
        columns = pl.ds(half * (model // 2), model // 2)
        branch = dot(narrow_act[...], up[:, columns]) + up_bias[:, columns]
        total[:, columns] += branch_scale * branch
        gather.tick()

    for copy in kept:
        if copy is not normal_out and copy is not inverse_out and copy is not turned_out:
            copy.wait()
    gather.need(2)
    tile = model // 2
    act, slope = held.at[pl.ds(0, 4)], held.at[pl.ds(4, 4)]
    for block in range(hidden // tile):
        at, columns = block // 2, pl.ds((block % 2) * tile, tile)
        inner = dot(low[...], wide_in[:, pl.ds(block * tile, tile)])
        active, slant = gelu_both(inner)
        act[at, :, columns] = active.astype(bf16)
        slope[at, :, columns] = slant.astype(bf16)
        gather.tick(2)
    gather.need(3)
    for half in range(2):
        columns = pl.ds(half * (model // 2), model // 2)
        feed = total[:, columns]
        for at in range(hidden // model):
            feed += dot(act[at], wide_out[pl.ds(at * model, model), columns])
        total[:, columns] = feed
    load_cot.wait()
    feed_grad, branch_grad = tok, enc
    for name in range(8):
        vectors[name : name + 1, :] = jnp.zeros((1, model), f32)

    @pl.loop(0, blocks)
    def _(block):
        here = part(block, block_rows)
        normal_three, inverse_three = layer_stats(total[here, :])
        tok_out = (normal_three * norm_gain[2:3, :] + norm_bias[2:3, :]).astype(bf16)
        low_grad = enc[here, :].astype(f32)
        grad_three = norm_back(low_grad, normal_three, inverse_three, norm_gain[2:3, :])
        total[here, :] = grad_three
        tok[here, :] = grad_three.astype(bf16)
        scaled = (branch_scale * grad_three).astype(bf16)
        enc[here, :] = scaled
        turned[0, here, :] = tok_out[:, : model // 2]
        turned[1, here, :] = tok_out[:, model // 2 :]
        vectors[2:3, :] += jnp.sum(low_grad * normal_three, 0, keepdims=True)
        vectors[5:6, :] += jnp.sum(low_grad, 0, keepdims=True)
        vectors[6:7, :] += jnp.sum(scaled.astype(f32), 0, keepdims=True)

    out_copies = []
    for half in range(2):
        copy = pltpu.make_async_copy(
            turned.at[half, pl.ds(0, rows)],
            output.at[:, pl.ds(half * (model // 2), model // 2)],
            probs_sem.at[half],
        )
        copy.start()
        out_copies.append(copy)

    adapt = narrow_act.shape[1]
    quarter = packed.shape[1]
    for half in range(2):
        lifted = t_dot(narrow_act[...], branch_grad[:, pl.ds(half * tile, tile)]).astype(bf16)
        for at in range(tile // quarter):
            first = model * adapt // quarter + (half * (tile // quarter) + at) * adapt
            packed[pl.ds(first, adapt), :] = lifted[:, at * quarter : (at + 1) * quarter]
    small = dot_t(branch_grad[...], up[...]) * narrow_slope[...]
    narrow_grad[...] = small.astype(bf16)
    vectors[7:8, :adapt] = jnp.sum(narrow_grad[...].astype(f32), 0, keepdims=True)
    lowered = t_dot(low[...], narrow_grad[...]).astype(bf16)
    for at in range(adapt // quarter):
        packed[pl.ds(at * model, model), :] = lowered[:, at * quarter : (at + 1) * quarter]
    packed_out = pltpu.make_async_copy(packed, adapt_grads, load_sem.at[0])
    packed_out.start()
    for at in range(hidden // model):
        for half in range(2):
            columns = pl.ds(half * tile, tile)
            grown = dot_t(feed_grad[...], wide_out[pl.ds(at * model + half * tile, tile), :])
            act[at, :, columns] = (grown * slope[at, :, columns].astype(f32)).astype(bf16)
    for half in range(2):
        columns = pl.ds(half * (model // 2), model // 2)
        second_grad = total[:, columns] + dot_t(narrow_grad[...], down[columns, :])
        for at in range(hidden // model):
            second_grad += dot_t(act[at], wide_in[columns, pl.ds(at * model, model)])
        total[:, columns] = second_grad

    @pl.loop(0, blocks)
    def _(block):
        here = part(block, block_rows)
        grad_second = total[here, :]
        normal_two = normal[here, :]
        vectors[1:2, :] += jnp.sum(grad_second * normal_two, 0, keepdims=True)
        vectors[4:5, :] += jnp.sum(grad_second, 0, keepdims=True)
        total[here, :] = norm_back(grad_second, normal_two, inverse[here, 0:1], norm_gain[1:2, :])

    last = [
        pltpu.make_async_copy(total, grad_kept, load_sem.at[1]),
        pltpu.make_async_copy(vectors, vector_grads, load_sem.at[2]),
    ]
    for copy in last:
        copy.start()
    gather.finish()
    for copy in out_copies + [packed_out] + last:
        copy.wait()


def forward(count, *args):
    tokens, ffn_in, adapt_down = args[0], args[7], args[9]
    rows, model = tokens.shape
    hidden, adapt = ffn_in.shape[1], adapt_down.shape[1]
    shape = jax.ShapeDtypeStruct
    quarter = 128
    packed = (2 * model * adapt // quarter, quarter)
    return pl.pallas_call(
        functools.partial(forward_kernel, count),
        out_shape=[
            shape((rows, model), bf16),
            shape((8, model, model), bf16),
            shape((4, rows, model), bf16),
            shape((model, rows), bf16),
            shape((HEADS, rows, rows), bf16),
            shape((4, rows, model), bf16),
            shape((model, rows), bf16),
            shape((HEADS, rows, rows), bf16),
            shape((rows, model), f32),
            shape((rows, 128), f32),
            shape((rows, model), f32),
            shape(packed, bf16),
            shape((8, model), f32),
        ],
        in_specs=[ANY] * 10
        + [pl.BlockSpec(memory_space=pltpu.VMEM), ANY]
        + [pl.BlockSpec(memory_space=pltpu.VMEM)] * 3
        + [SMEM] * 3,
        out_specs=[ANY] * 13,
        scratch_shapes=[
            pltpu.VMEM((8, model, model), bf16),
            pltpu.VMEM((model, hidden), bf16),
            pltpu.VMEM((hidden, model), bf16),
            pltpu.VMEM((8, rows, model), bf16),
            pltpu.VMEM((2, model, rows), bf16),
            pltpu.VMEM((rows, model), bf16),
            pltpu.VMEM((rows, model), bf16),
            pltpu.VMEM((rows, model), bf16),
            pltpu.VMEM((rows, rows), f32),
            pltpu.VMEM((2, 2, rows, rows), bf16),
            pltpu.VMEM((rows, model), f32),
            pltpu.VMEM((rows, model), f32),
            pltpu.VMEM((rows, 128), f32),
            pltpu.VMEM((rows, adapt), bf16),
            pltpu.VMEM((rows, adapt), f32),
            pltpu.VMEM((rows, adapt), bf16),
            pltpu.VMEM((model, adapt), bf16),
            pltpu.VMEM((adapt, model), bf16),
            pltpu.VMEM((8, model), f32),
            pltpu.VMEM(packed, bf16),
            pltpu.SemaphoreType.DMA((4, sends_per_phase(count))),
            pltpu.SemaphoreType.DMA((4, 2, count // 2, 4)),
            pltpu.SemaphoreType.DMA((6,)),
            pltpu.SemaphoreType.DMA((4,)),
            pltpu.SemaphoreType.DMA((10,)),
            pltpu.SemaphoreType.DMA((2,)),
        ],
        compiler_params=pltpu.CompilerParams(
            collective_id=0, has_side_effects=True, vmem_limit_bytes=63 * 2**20
        ),
        name="forward_and_feed_back",
    )(*args)


class Reduction:
    def __init__(self, count, copies, mass, inbox, whole, send_sem, recv_sem, vectors, letters, post_sem, mail_sem):
        self.mass, self.inbox, self.whole = mass, inbox, whole
        self.send_sem, self.recv_sem = send_sem, recv_sem
        self.vectors, self.letters, self.post_sem, self.mail_sem = vectors, letters, post_sem, mail_sem
        line, wide = mesh_shape(count)
        index, dp = lax.axis_index("fsdp"), lax.axis_index("dp")

        def along(coordinate, weight, size, move):
            found = []
            step = 1
            while step < size:
                bit = (coordinate // step) % 2
                found.append((bit, move((1 - 2 * bit) * step * weight)))
                step *= 2
            return found

        def fsdp(weight, size):
            return along((index // weight) % size, weight, size, lambda by: (index + by, dp))

        core, x, z = fsdp(1, 2), fsdp(2, wide), fsdp(2 * wide, line)
        planes = along(dp, 1, copies, lambda by: (index, dp + by))
        self.orders = (core + x + planes + z, core + planes + x + z)
        self.bits = len(self.orders[0])
        self.sends = []
        self.regions = []
        rows = mass.shape[0] // len(self.orders)
        for at, order in enumerate(self.orders):
            start, size, box = at * rows, rows, at * rows
            regions = []
            for bit, target in order:
                size //= 2
                regions.append((start + bit * size, start + (1 - bit) * size, size, box, target))
                start = start + bit * size
                box += size
            self.regions.append(regions)
        self.steps = []
        for step in range(self.bits):
            self.steps.append(functools.partial(self.scatter, step))
            self.steps.append(functools.partial(self.add, step))
        for step in reversed(range(self.bits)):
            self.steps.append(functools.partial(self.spread, step))
            self.steps.append(functools.partial(self.landed, step))
        self.post_steps = []
        for step in range(self.bits):
            self.post_steps.append(functools.partial(self.post, step))
            self.post_steps.append(functools.partial(self.read, step))
        self.done = 0

    def enter(self):
        barrier = pltpu.get_barrier_semaphore()
        for _, target in self.orders[0]:
            pl.semaphore_signal(barrier, inc=1, device_id=target, device_id_type=MESH)
        pl.semaphore_wait(barrier, self.bits)

    def tick(self, many=1):
        for _ in range(many):
            if self.done < len(self.steps):
                self.done += 1
                self.steps[self.done - 1]()

    def take(self, many):
        first = self.done
        self.done = min(len(self.steps), first + many)
        return self.steps[first : self.done]

    def mix(self):
        rest, posts = self.steps[self.done :], self.post_steps
        mixed = [step for both in zip(rest, posts) for step in both]
        shorter = min(len(rest), len(posts))
        self.steps = self.steps[: self.done] + mixed + rest[shorter:] + posts[shorter:]

    def remote(self, source, target_ref, sems, slot, target):
        return pltpu.make_async_remote_copy(
            src_ref=source,
            dst_ref=target_ref,
            send_sem=sems[0].at[slot],
            recv_sem=sems[1].at[slot],
            device_id=target,
            device_id_type=MESH,
        )

    def rows(self, start, size):
        return pl.ds(pl.multiple_of(start, 16), size)

    def scatter_copy(self, at, step):
        _, away, size, box, target = self.regions[at][step]
        return self.remote(
            self.mass.at[self.rows(away, size)],
            self.inbox.at[pl.ds(box, size)],
            (self.send_sem, self.recv_sem),
            at * 2 * self.bits + step,
            target,
        )

    def spread_copy(self, at, step):
        stay, _, size, _, target = self.regions[at][step]
        view = self.whole.at[self.rows(stay, size)]
        sems = (self.send_sem, self.recv_sem)
        return self.remote(view, view, sems, at * 2 * self.bits + self.bits + step, target)

    def scatter(self, step):
        for at in range(len(self.orders)):
            self.scatter_copy(at, step).start()
            self.sends.append(functools.partial(self.scatter_copy, at, step))

    def add(self, step):
        for at in range(len(self.orders)):
            stay, _, size, box, _ = self.regions[at][step]
            self.scatter_copy(at, step).wait_recv()
            here = self.rows(stay, size)
            into = self.whole if step == self.bits - 1 else self.mass
            both = self.mass[here, :].astype(f32) + self.inbox[pl.ds(box, size), :].astype(f32)
            into[here, :] = both.astype(bf16)

    def spread(self, step):
        for at in range(len(self.orders)):
            self.spread_copy(at, step).start()
            self.sends.append(functools.partial(self.spread_copy, at, step))

    def landed(self, step):
        for at in range(len(self.orders)):
            _, away, size, _, _ = self.regions[at][step]
            view = self.whole.at[self.rows(away, size)]
            slot = at * 2 * self.bits + self.bits + step
            pltpu.make_async_copy(view, view, self.recv_sem.at[slot]).wait()

    def post_copy(self, step):
        return self.remote(
            self.vectors.at[step],
            self.letters.at[step],
            (self.post_sem, self.mail_sem),
            step,
            self.orders[0][step][1],
        )

    def post(self, step):
        self.post_copy(step).start()
        self.sends.append(functools.partial(self.post_copy, step))

    def read(self, step):
        self.post_copy(step).wait_recv()
        self.vectors[step + 1] = self.vectors[step] + self.letters[step]

    def finish(self):
        for remake in self.sends:
            remake().wait_send()


def back_pair(pair, query, key_t, value, grad, probs, delta, grad_query, grad_key, grad_value, causal):
    rows = query.shape[0]
    columns = part(pair, 128)
    values, queries, grads = value[:, columns], query[:, columns], grad[:, columns]
    tiles = tiles_of(rows, causal)
    key_sums = [None] * len(tiles)
    value_sums = [None] * len(tiles)
    halves = []
    for half in range(2):
        head_grads = head_lanes(grads, half)
        head_queries = head_lanes(queries, half)
        lanes = pl.ds(pl.multiple_of(pair * 128 + half * 64, 64), 64)
        shift = delta[pl.ds(pair * 2 + half, 1), :]
        pieces = []
        for at, (first, many, deep) in enumerate(tiles):
            weights = probs[half, :deep, first : first + many]
            grown = dot_t(values[:deep], head_grads[first : first + many])
            slopes = (weights.astype(f32) * (grown - shift[:, first : first + many])).astype(bf16)
            value_part = dot(weights, head_grads[first : first + many])
            key_part = dot(slopes, head_queries[first : first + many])
            value_sums[at] = value_part if half == 0 else value_sums[at] + value_part
            key_sums[at] = key_part if half == 0 else key_sums[at] + key_part
            pieces.append(dot(key_t[lanes, :deep], slopes))
        halves.append(jnp.concatenate(pieces, 1) if len(pieces) > 1 else pieces[0])
    both = jnp.concatenate(halves, 0).astype(bf16)
    grad_query[:, columns] = both.T
    for sums, out in ((key_sums, grad_key), (value_sums, grad_value)):
        if len(tiles) == 1:
            out[:, columns] = sums[0].astype(bf16)
        else:
            half_rows = rows // 2
            out[:half_rows, columns] = (sums[0] + sums[1][:half_rows]).astype(bf16)
            out[half_rows:, columns] = sums[1][half_rows:].astype(bf16)


def backward_kernel(
    count,
    copies,
    attn_kept,
    self_kept,
    self_key_kept,
    self_probs,
    cross_kept,
    cross_key_kept,
    cross_probs,
    normal_kept,
    inverse_kept,
    grad_kept,
    adapt_grads,
    vector_grads,
    norm_gain,
    grad_tokens,
    grad_encoder,
    grad_down,
    grad_up,
    vector_sums,
    attn,
    saved,
    saved_key,
    probs,
    total,
    normal,
    inverse,
    low,
    grad,
    grad_query,
    grad_key,
    grad_value,
    delta,
    mass,
    inbox,
    whole,
    vectors,
    letters,
    load_sem,
    probs_sem,
    out_sem,
    send_sem,
    recv_sem,
    post_sem,
    mail_sem,
):
    rows, model = total.shape
    adapt = grad_down.shape[1]
    slots = probs.shape[0]
    pairs = HEADS // 2
    loads = {}

    def load(name, source, target):
        loads[name] = pltpu.make_async_copy(source, target, load_sem.at[len(loads)])
        loads[name].start()

    def probs_copy(kept, pair):
        slot = pair % slots
        return pltpu.make_async_copy(kept.at[pl.ds(pair * 2, 2)], probs.at[slot], probs_sem.at[slot])

    load("total", grad_kept, total)
    load("cross_out", attn_kept.at[7], attn.at[7])
    load("mass", adapt_grads, mass)
    load("joined", cross_kept.at[3], saved.at[3])
    load("cross_value", cross_kept.at[2], saved.at[2])
    load("cross_query", cross_kept.at[0], saved.at[0])
    load("cross_key", cross_key_kept, saved_key.at[0])
    for pair in range(slots - 1):
        probs_copy(cross_probs, pair).start()
    load("cross_qkv", attn_kept.at[pl.ds(4, 3)], attn.at[pl.ds(4, 3)])
    load("normal", normal_kept, normal)
    load("inverse", inverse_kept, inverse)
    load("vectors", vector_grads, vectors.at[0])
    load("self_out", attn_kept.at[3], attn.at[3])
    load("self_query", self_kept.at[0], saved.at[4])
    load("self_value", self_kept.at[2], saved.at[6])
    load("mixed", self_kept.at[3], saved.at[7])
    load("self_key", self_key_kept, saved_key.at[1])
    load("self_qkv", attn_kept.at[pl.ds(0, 3)], attn.at[pl.ds(0, 3)])
    reduction = Reduction(
        count, copies, mass, inbox, whole, send_sem, recv_sem, vectors, letters, post_sem, mail_sem
    )
    reduction.enter()
    loads["mass"].wait()
    reduction.tick()
    outs = []

    def put(source, target):
        copy = pltpu.make_async_copy(source, target, out_sem.at[len(outs)])
        copy.start()
        outs.append(copy)

    def attention_back(kept, base, key_t, weight, causal, ready, following, ticks):
        for half in range(2):
            columns = pl.ds(half * (model // 2), model // 2)
            grad[:, columns] = dot_t(low[...], attn[weight, columns, :]).astype(bf16)
            reduction.tick()
        for name in ready:
            loads[name].wait()
        head = lax.broadcasted_iota(jnp.int32, (HEADS, model), 0)
        lane = lax.broadcasted_iota(jnp.int32, (HEADS, model), 1)
        chosen = (lane // 64 == head).astype(bf16)
        product = grad[...].astype(f32) * saved[base + 3].astype(f32)
        rough = product.astype(bf16)
        fine = (product - rough.astype(f32)).astype(bf16)
        delta[...] = dot_t(chosen, rough) + dot_t(chosen, fine)
        reduction.tick()
        steps = reduction.take(ticks)
        each = -(-len(steps) // pairs)

        @pl.loop(0, pairs)
        def _(pair):
            probs_copy(kept, pair).wait()

            @pl.when(pair + slots - 1 < pairs)
            def _():
                probs_copy(kept, pair + slots - 1).start()

            back_pair(
                pair,
                saved.at[base],
                key_t,
                saved.at[base + 2],
                grad,
                probs.at[pair % slots],
                delta,
                grad_query,
                grad_key,
                grad_value,
                causal,
            )
            for at in range(pairs):
                mine_now = steps[each * at : each * (at + 1)]
                if mine_now:

                    @pl.when(pair == at)
                    def _():
                        for step in mine_now:
                            step()

        if following is not None:
            for pair in range(slots - 1):
                probs_copy(following, pair).start()

    loads["total"].wait()
    low[...] = total[...].astype(bf16)
    loads["cross_out"].wait()
    attention_back(
        cross_probs,
        0,
        saved_key.at[0],
        7,
        False,
        ("joined", "cross_value", "cross_query", "cross_key"),
        self_probs,
        8,
    )
    loads["cross_qkv"].wait()
    for half in range(2):
        columns = pl.ds(half * (model // 2), model // 2)
        total[:, columns] += dot_t(grad_query[...], attn[4, columns, :])
        reduction.tick()
    for name in ("normal", "inverse", "vectors"):
        loads[name].wait()
    block_rows = 128

    @pl.loop(0, rows // block_rows)
    def _(block):
        here = part(block, block_rows)
        grad_first = total[here, :]
        normal_one = normal[here, :]
        vectors[0, 0:1, :] += jnp.sum(grad_first * normal_one, 0, keepdims=True)
        vectors[0, 3:4, :] += jnp.sum(grad_first, 0, keepdims=True)
        grad_one = norm_back(grad_first, normal_one, inverse[here, 0:1], norm_gain[0:1, :])
        total[here, :] = grad_one
        low[here, :] = grad_one.astype(bf16)

    for half in range(2):
        columns = pl.ds(half * (model // 2), model // 2)
        encoder_part = dot_t(grad_key[...], attn[5, columns, :]) + dot_t(grad_value[...], attn[6, columns, :])
        saved[1, :, columns] = encoder_part.astype(bf16)
        reduction.tick()
    put(saved.at[1], grad_encoder)
    reduction.mix()
    loads["self_out"].wait()
    attention_back(
        self_probs,
        4,
        saved_key.at[1],
        3,
        True,
        ("mixed", "self_value", "self_query", "self_key"),
        None,
        len(reduction.steps),
    )
    reduction.tick(len(reduction.steps))
    quarter = whole.shape[1]
    for at in range(adapt // quarter):
        put(whole.at[pl.ds(at * model, model)], grad_down.at[:, pl.ds(at * quarter, quarter)])
    for at in range(model // quarter):
        put(
            whole.at[pl.ds(model * adapt // quarter + at * adapt, adapt)],
            grad_up.at[:, pl.ds(at * quarter, quarter)],
        )
    put(vectors.at[reduction.bits], vector_sums)
    loads["self_qkv"].wait()
    for half in range(2):
        columns = pl.ds(half * (model // 2), model // 2)
        token_part = total[:, columns]
        for at, source in enumerate((grad_query, grad_key, grad_value)):
            token_part += dot_t(source[...], attn[at, columns, :])
        saved[5, :, columns] = token_part.astype(bf16)
    put(saved.at[5], grad_tokens)
    reduction.finish()
    for copy in outs:
        copy.wait()


def backward(count, copies, *args):
    rows, model = args[9].shape
    packed = args[10].shape
    adapt = packed[0] * packed[1] // (2 * model)
    bits = (count * copies).bit_length() - 1
    shape = jax.ShapeDtypeStruct
    return pl.pallas_call(
        functools.partial(backward_kernel, count, copies),
        out_shape=[
            shape((rows, model), bf16),
            shape((rows, model), bf16),
            shape((model, adapt), bf16),
            shape((adapt, model), bf16),
            shape((8, model), f32),
        ],
        in_specs=[ANY] * 12 + [pl.BlockSpec(memory_space=pltpu.VMEM)],
        out_specs=[ANY] * 5,
        scratch_shapes=[
            pltpu.VMEM((8, model, model), bf16),
            pltpu.VMEM((8, rows, model), bf16),
            pltpu.VMEM((2, model, rows), bf16),
            pltpu.VMEM((3, 2, rows, rows), bf16),
            pltpu.VMEM((rows, model), f32),
            pltpu.VMEM((rows, model), f32),
            pltpu.VMEM((rows, 128), f32),
            pltpu.VMEM((rows, model), bf16),
            pltpu.VMEM((rows, model), bf16),
            pltpu.VMEM((rows, model), bf16),
            pltpu.VMEM((rows, model), bf16),
            pltpu.VMEM((rows, model), bf16),
            pltpu.VMEM((HEADS, rows), f32),
            pltpu.VMEM(packed, bf16),
            pltpu.VMEM(packed, bf16),
            pltpu.VMEM(packed, bf16),
            pltpu.VMEM((bits + 1, 8, model), f32),
            pltpu.VMEM((bits, 8, model), f32),
            pltpu.SemaphoreType.DMA((18,)),
            pltpu.SemaphoreType.DMA((3,)),
            pltpu.SemaphoreType.DMA((16,)),
            pltpu.SemaphoreType.DMA((4 * bits,)),
            pltpu.SemaphoreType.DMA((4 * bits,)),
            pltpu.SemaphoreType.DMA((bits,)),
            pltpu.SemaphoreType.DMA((bits,)),
        ],
        compiler_params=pltpu.CompilerParams(
            collective_id=1, has_side_effects=True, vmem_limit_bytes=62 * 2**20
        ),
        name="attention_back_and_sums",
    )(*args)


def local(*args):
    count, copies = lax.axis_size("fsdp"), lax.axis_size("dp")
    args = list(args)
    args[10], args[12] = args[10][None], args[12][None]
    norm_gain = args[13]
    output, *kept = forward(count, *args)
    grad_tokens, grad_encoder, down, up, sums = backward(count, copies, *kept, norm_gain)
    adapt = down.shape[1]
    return (
        output,
        grad_tokens,
        grad_encoder,
        down.astype(f32),
        sums[7, :adapt],
        up.astype(f32),
        sums[6],
        sums[0:3],
        sums[3:6],
    )


def solution(mesh):
    rows = P(("fsdp", "dp"), None)
    placed = (
        (rows,) * 3
        + (P(None, "fsdp", None), P("fsdp", None)) * 2
        + (P("fsdp", None),) * 2
        + (P(),) * 6
        + (P(("fsdp", "dp")), rows, rows)
    )
    return jax.shard_map(
        local, mesh=mesh, in_specs=placed, out_specs=(rows,) * 3 + (P(),) * 6, check_vma=False
    )
```

```python
import functools

import jax
import jax.numpy as jnp
from jax import lax
from jax.experimental import pallas as pl
from jax.experimental.pallas import tpu as pltpu
from jax.sharding import PartitionSpec as P

HEADS = 16
STEP = 12
LINE = 4
MESH = pl.DeviceIdType.MESH
ANY = pl.BlockSpec(memory_space=pl.ANY)
SMEM = pl.BlockSpec(memory_space=pltpu.SMEM)
bf16 = jnp.bfloat16
f32 = jnp.float32

epsilon = 1e-05
ramp_steps = 4.0
masked_score = -1e30
lead = 1.0


def dot(left, right):
    return jnp.dot(left, right, preferred_element_type=f32)


def dot_t(left, right):
    return lax.dot_general(left, right, (((1,), (1,)), ((), ())), preferred_element_type=f32)


def t_dot(left, right):
    return lax.dot_general(left, right, (((0,), (0,)), ((), ())), preferred_element_type=f32)


def part(index, size):
    return pl.ds(pl.multiple_of(index * size, size), size)


def layer_stats(values_in):
    average = jnp.mean(values_in, -1, keepdims=True)
    centred = values_in - average
    inverse = lax.rsqrt(jnp.mean(centred * centred, -1, keepdims=True) + epsilon)
    return (centred * inverse, inverse)


def norm_back(grad_out, normal, inverse, norm_scale):
    grad_normal = grad_out * norm_scale
    return inverse * (
        grad_normal
        - jnp.mean(grad_normal, -1, keepdims=True)
        - normal * jnp.mean(grad_normal * normal, -1, keepdims=True)
    )


def nearest(place, count, rank):
    under, over = place, count - 1 - place
    both = jnp.minimum(under, over)
    side = jnp.where(under > over, -1, 1)
    paired = place + (side * ((rank + 1) // 2) if rank % 2 == 1 else -side * (rank // 2))
    alone = jnp.where(over > under, place + rank - both, place - (rank - both))
    return jnp.where(rank <= 2 * both, paired, alone)


def mesh_shape(count):
    line = min(LINE, count // 2)
    return line, count // (2 * line)


def sends_per_phase(count):
    line, wide = mesh_shape(count)
    across = 1 if wide == 2 else 2
    each = 2 * (2 + across) + 1
    return line * each + (wide - 1) * line * 2 * (1 + across) + (line - 1) + (wide - 1) * line * 2


class Gather:
    def __init__(self, count, views, send_sem, recv_sem):
        self.views, self.send_sem, self.recv_sem = views, send_sem, recv_sem
        self.line, self.wide = mesh_shape(count)
        index = lax.axis_index("fsdp")
        self.dp = lax.axis_index("dp")
        self.core = index % 2
        self.x = (index // 2) % self.wide
        self.z = index // (2 * self.wide)
        p = self.dp % 2
        self.other_core = (self.place(self.z, self.x, 1 - self.core), self.dp)
        self.other_plane = (index, self.dp + 1 - 2 * p)
        self.same = ((2 * p, 2), (4, 4), (2 - 2 * p, 2))
        self.cross = ((2 * p, 2), (4 + p, 3), (2 - 2 * p, 2), (7 - 3 * p, 1))
        self.single = (4 + 3 * p, 1)
        self.z_up = (self.along_z(1), self.z < self.line - 1)
        self.z_down = (self.along_z(-1), self.z > 0)
        if self.wide == 2:
            self.x_ways = ((self.along_x(1 - 2 * self.x), None),)
        else:
            self.x_ways = ((self.along_x(1), self.x < self.wide - 1), (self.along_x(-1), self.x > 0))
        self.sends = {}
        self.counts = [0] * len(views)
        self.steps = self.plan()
        self.done = 0

    def place(self, z, x, core):
        return (z * self.wide + x) * 2 + core

    def along_z(self, step):
        return (self.place(self.z + step, self.x, self.core), self.dp)

    def along_x(self, step):
        return (self.place(self.z, self.x + step, self.core), self.dp)

    def enter(self, others):
        barrier = pltpu.get_barrier_semaphore()

        def greet(target):
            pl.semaphore_signal(barrier, inc=1, device_id=target, device_id_type=MESH)

        greet(self.other_core)
        greet(self.other_plane)
        for target in others:
            greet(target)
        total = 2 + len(others)
        for target, inside in (self.z_up, self.z_down) + self.x_ways:
            if inside is None:
                greet(target)
                total = total + 1
            else:
                pl.when(inside)(functools.partial(greet, target))
                total = total + inside.astype(jnp.int32)
        pl.semaphore_wait(barrier, total)

    def copy(self, at, kind, span, slot, target):
        phase, core, z, x = at
        view = self.views[phase](self.place(z, x, core), *span)
        return pltpu.make_async_remote_copy(
            src_ref=view,
            dst_ref=view,
            send_sem=self.send_sem.at[phase % 2, slot],
            recv_sem=self.recv_sem.at[phase, core, z * self.wide + x, kind],
            device_id=target,
            device_id_type=MESH,
        )

    def send(self, at, kind, span, target, when=None):
        slot = self.counts[at[0]]
        self.counts[at[0]] += 1
        remake = functools.partial(self.copy, at, kind, span, slot, target)
        before = self.sends.pop((at[0] - 2, slot), None)

        def start():
            if before is not None:
                before[0]().wait_send()
            remake().start()

        if when is None:
            start()
        else:
            pl.when(when)(start)
        self.sends[at[0], slot] = (remake, when)

    def arrive(self, at, kind, span):
        phase, core, z, x = at
        view = self.views[phase](self.place(z, x, core), *span)
        pltpu.make_async_copy(view, view, self.recv_sem.at[phase, core, z * self.wide + x, kind]).wait()

    def plan(self):
        span = self.line - 1
        steps = []
        for phase in range(len(self.views)):
            base = span * phase

            def add(when, makers, chip=None):
                steps.extend((base + when, phase, maker, chip) for maker in makers)

            for far in range(self.line):
                z_from = nearest(self.z, self.line, far)
                if far:
                    add(far, self.from_z((phase, self.core, z_from, self.x)), (far, 0))
                    add(far + 1.1, self.from_plane((phase, self.core, z_from, self.x), self.same), (far, 0))
                for apart in range(1, self.wide):
                    at = (phase, self.core, z_from, nearest(self.x, self.wide, apart))
                    add(far + apart + 0.05, self.from_x(at), (far, apart))
                    add(far + apart + 1.15, self.from_plane(at, self.cross), (far, apart))
            if phase:
                add(-lead, [functools.partial(self.own, phase)])
        return sorted(steps, key=lambda item: item[0])

    def own(self, phase):
        at = (phase, self.core, self.z, self.x)
        for kind in (0, 1):
            self.send(at, kind, self.same[kind], *self.z_up)
            self.send(at, kind, self.same[kind], *self.z_down)
            self.over_x(at, kind)
        self.send(at, 0, (0, 8), self.other_core)

    def over_x(self, at, kind):
        for way in self.x_ways:
            self.send(at, kind, self.cross[kind], *way)

    def from_z(self, at):
        upward = at[2] < self.z
        onward = (upward & self.z_up[1]) | (~upward & self.z_down[1])
        target = self.along_z(jnp.where(upward, 1, -1))

        def step(kind):
            self.arrive(at, kind, self.same[kind])
            self.send(at, kind, self.same[kind], target, onward)
            self.over_x(at, kind)
            if kind == 0:
                self.send(at, 2, self.same[0], self.other_plane)
            self.send(at, kind, self.same[kind], self.other_core)

        return [functools.partial(step, 0), functools.partial(step, 1)]

    def from_x(self, at):
        upward = at[3] < self.x
        onward = (upward & (self.x < self.wide - 1)) | (~upward & (self.x > 0))
        target = self.along_x(jnp.where(upward, 1, -1))

        def step(kind):
            self.arrive(at, kind, self.cross[kind])
            if self.wide > 2:
                self.send(at, kind, self.cross[kind], target, onward)
            self.send(at, kind + 2, self.cross[0] if kind == 0 else self.single, self.other_plane)
            self.send(at, kind, self.cross[kind], self.other_core)

        return [functools.partial(step, 0), functools.partial(step, 1)]

    def from_plane(self, at, spans):
        def step():
            for kind in range(2, len(spans)):
                self.arrive(at, kind, spans[kind])
                self.send(at, kind, spans[kind], self.other_core)

        return [step]

    def tick(self, many=1):
        for _ in range(many):
            if self.done < len(self.steps):
                self.done += 1
                self.steps[self.done - 1][2]()

    def take(self, many):
        first = self.done
        self.done = min(len(self.steps), first + many)
        return [step[2] for step in self.steps[first : self.done]]

    def need(self, phase):
        last = max(i for i, step in enumerate(self.steps) if step[1] == phase)
        self.tick(last + 1 - self.done)
        for z in range(self.line):
            for x in range(self.wide):
                self.other_half(phase, z, x)

    def chips(self, phase):
        for far in range(self.line):
            for apart in range(self.wide):
                own = [i for i, step in enumerate(self.steps) if step[1] == phase and step[3] == (far, apart)]
                self.tick(max(own, default=-1) + 1 - self.done)
                z, x = nearest(self.z, self.line, far), nearest(self.x, self.wide, apart)
                self.other_half(phase, z, x)
                yield self.place(z, x, 0) // 2

    def other_half(self, phase, z, x):
        at = (phase, 1 - self.core, z, x)

        def pieces(spans):
            for kind, span in enumerate(spans):
                self.arrive(at, kind, span)

        own_chip = (z == self.z) & (x == self.x)
        pl.when(own_chip)(lambda: self.arrive(at, 0, (0, 8)))
        pl.when((x == self.x) & (z != self.z))(lambda: pieces(self.same))
        pl.when(x != self.x)(lambda: pieces(self.cross))

    def finish(self):
        for remake, when in self.sends.values():
            if when is None:
                remake().wait_send()
            else:
                pl.when(when)(lambda: remake().wait_send())


def place_masks(bias, shift, lengths, causal):
    rows = bias.shape[0]
    wide = 128
    bits = shift + (rows // 4).bit_length() - 1

    @pl.loop(0, rows // wide)
    def _(block):
        shape = (wide, rows)
        key = lax.broadcasted_iota(jnp.int32, shape, 0) + block * wide
        query = lax.broadcasted_iota(jnp.int32, shape, 1)
        key_seq = lax.shift_right_logical(key, jnp.full(shape, bits, jnp.int32))
        query_seq = lax.shift_right_logical(query, jnp.full(shape, bits, jnp.int32))
        start = lax.shift_left(key_seq, jnp.full(shape, bits, jnp.int32))
        length = jnp.zeros(shape, jnp.int32)
        for slot in range(4):
            length = jnp.where(key_seq == slot, lengths[0, slot], length)
        allowed = (key_seq == query_seq) & (key - start < length)
        if causal:
            allowed = allowed & (key <= query)
        bias[part(block, wide), :] = jnp.where(allowed, 0.0, masked_score).astype(bf16)


def tiles_of(rows, causal):
    half = rows // 2
    return ((0, half, half), (half, half, rows)) if causal else ((0, rows, rows),)


def head_lanes(values, half):
    lane = lax.broadcasted_iota(jnp.int32, values.shape, 1)
    return jnp.where((lane // 64) == half, values, jnp.zeros_like(values))


def attend_pair(pair, query, key, value_t, bias, probs, out, causal):
    rows = query.shape[0]
    columns = part(pair, 128)
    keys = key[:, columns]
    queries = query[:, columns]
    halves = []
    for half in range(2):
        head_queries = head_lanes(queries, half)
        lanes = pl.ds(pl.multiple_of(pair * 128 + half * 64, 64), 64)
        pieces = []
        for first, many, deep in tiles_of(rows, causal):
            scores = dot_t(keys[:deep], head_queries[first : first + many])
            scores = scores + bias[:deep, first : first + many].astype(f32)
            expanded = jnp.exp(scores - jnp.max(scores, 0, keepdims=True))
            total = jnp.sum(expanded, 0, keepdims=True)
            block = (expanded * (1.0 / total)).astype(bf16)
            probs[half, :deep, first : first + many] = block
            pieces.append(dot(value_t[lanes, :deep], block))
        halves.append(jnp.concatenate(pieces, 1) if len(pieces) > 1 else pieces[0])
    both = jnp.concatenate(halves, 0).astype(bf16)
    out[:, columns] = both.T


def gelu_both(inner):
    spread = 0.5 + 0.5 * lax.erf(inner * (0.5**0.5))
    bell = jnp.exp(inner * inner * -0.5) * 0.3989422804014327
    return inner * spread, spread + inner * bell


def box_rows(height, bits):
    return sum(max(16, height >> (step + 1)) for step in range(bits))


class Reduction:
    def __init__(self, count, copies, mass, inbox, send_sem, recv_sem, free_sem, vectors, letters, post_sem, mail_sem):
        self.mass, self.inbox, self.free_sem = mass, inbox, free_sem
        self.send_sem, self.recv_sem = send_sem, recv_sem
        self.vectors, self.letters, self.post_sem, self.mail_sem = vectors, letters, post_sem, mail_sem
        line, wide = mesh_shape(count)
        index, dp = lax.axis_index("fsdp"), lax.axis_index("dp")

        def along(coordinate, weight, size, move):
            found = []
            step = 1
            while step < size:
                bit = (coordinate // step) % 2
                found.append((bit, move((1 - 2 * bit) * step * weight)))
                step *= 2
            return found

        def fsdp(weight, size):
            return along((index // weight) % size, weight, size, lambda by: (index + by, dp))

        core, x, z = fsdp(1, 2), fsdp(2, wide), fsdp(2 * wide, line)
        planes = along(dp, 1, copies, lambda by: (index, dp + by))
        self.orders = (core + x + planes + z, core + planes + x + z)
        self.bits = len(self.orders[0])
        self.partners = [target for _, target in self.orders[0]]
        self.sends = []
        self.regions = []
        height, width = mass.shape[0] // len(self.orders), mass.shape[1]
        for at, order in enumerate(self.orders):
            first, high, left, broad, box = at * height, height, 0, width, at * box_rows(height, self.bits)
            regions = []
            for bit, target in order:
                if high > 16:
                    high //= 2
                    kept = (first + bit * high, high, left, broad)
                    away = (first + (1 - bit) * high, high, left, broad)
                else:
                    broad //= 2
                    kept = (first, high, left + bit * broad, broad)
                    away = (first, high, left + (1 - bit) * broad, broad)
                first, left = kept[0], kept[2]
                regions.append((kept, away, box, target))
                box += high
            self.regions.append(regions)
        last = self.bits - 1
        self.steps = [functools.partial(self.scatter, 0)]
        for step in range(last):
            self.steps.append(functools.partial(self.turn, (self.add, step), (self.scatter, step + 1)))
        self.steps.append(functools.partial(self.turn, (self.add, last), (self.spread, last)))
        for step in range(last, 0, -1):
            self.steps.append(functools.partial(self.turn, (self.landed, step), (self.spread, step - 1)))
        self.steps.append(functools.partial(self.landed, 0))
        self.post_steps = [functools.partial(self.post, 0)]
        for step in range(last):
            self.post_steps.append(functools.partial(self.turn, (self.read, step), (self.post, step + 1)))
        self.post_steps.append(functools.partial(self.read, last))

    def turn(self, one, other):
        one[0](one[1])
        other[0](other[1])

    def tick(self, many=1):
        for _ in range(min(many, len(self.steps))):
            self.steps.pop(0)()

    def post_tick(self, many=1):
        for _ in range(min(many, len(self.post_steps))):
            self.post_steps.pop(0)()

    def remote(self, source, target_ref, sems, slot, target):
        return pltpu.make_async_remote_copy(
            src_ref=source,
            dst_ref=target_ref,
            send_sem=sems[0].at[slot],
            recv_sem=sems[1].at[slot],
            device_id=target,
            device_id_type=MESH,
        )

    def view(self, region):
        first, high, left, broad = region
        return self.mass.at[
            pl.ds(pl.multiple_of(first, 16), high), pl.ds(pl.multiple_of(left, 128), broad)
        ]

    def box(self, at, step):
        (_, high, _, broad), _, box, _ = self.regions[at][step]
        return self.inbox.at[pl.ds(box, high), pl.ds(0, broad)]

    def scatter_copy(self, at, step):
        _, away, _, target = self.regions[at][step]
        sems = (self.send_sem, self.recv_sem)
        return self.remote(self.view(away), self.box(at, step), sems, at * 2 * self.bits + step, target)

    def spread_copy(self, at, step):
        kept, _, _, target = self.regions[at][step]
        sems = (self.send_sem, self.recv_sem)
        slot = at * 2 * self.bits + self.bits + step
        return self.remote(self.view(kept), self.view(kept), sems, slot, target)

    def scatter(self, step):
        for at in range(len(self.orders)):
            self.scatter_copy(at, step).start()

    def add(self, step):
        for at in range(len(self.orders)):
            self.scatter_copy(at, step).wait()
            pl.semaphore_signal(
                self.free_sem.at[at * self.bits + step],
                inc=1,
                device_id=self.regions[at][step][3],
                device_id_type=MESH,
            )
            mine, arrived = self.view(self.regions[at][step][0]), self.box(at, step)
            rows = min(64, mine.shape[0])

            @pl.loop(0, mine.shape[0] // rows)
            def _(block):
                here = part(block, rows)
                mine[here, :] = (mine[here, :].astype(f32) + arrived[here, :].astype(f32)).astype(bf16)

    def spread(self, step):
        for at in range(len(self.orders)):
            pl.semaphore_wait(self.free_sem.at[at * self.bits + step], 1)
            self.spread_copy(at, step).start()
            self.sends.append(functools.partial(self.spread_copy, at, step))

    def landed(self, step):
        for at in range(len(self.orders)):
            view = self.view(self.regions[at][step][1])
            slot = at * 2 * self.bits + self.bits + step
            pltpu.make_async_copy(view, view, self.recv_sem.at[slot]).wait()

    def post_copy(self, step):
        return self.remote(
            self.vectors.at[step],
            self.letters.at[step],
            (self.post_sem, self.mail_sem),
            step,
            self.orders[0][step][1],
        )

    def post(self, step):
        self.post_copy(step).start()
        self.sends.append(functools.partial(self.post_copy, step))

    def read(self, step):
        self.post_copy(step).wait_recv()
        self.vectors[step + 1] = self.vectors[step] + self.letters[step]

    def finish(self):
        for remake in self.sends:
            remake().wait_send()


def back_pair(pair, query, key_t, value, grad, probs, delta, grad_query, grad_key, grad_value, causal):
    rows = query.shape[0]
    columns = part(pair, 128)
    values, queries, grads = value[:, columns], query[:, columns], grad[:, columns]
    tiles = tiles_of(rows, causal)
    key_sums = [None] * len(tiles)
    value_sums = [None] * len(tiles)
    halves = []
    for half in range(2):
        head_grads = head_lanes(grads, half)
        head_queries = head_lanes(queries, half)
        lanes = pl.ds(pl.multiple_of(pair * 128 + half * 64, 64), 64)
        shift = delta[pl.ds(pair * 2 + half, 1), :]
        pieces = []
        for at, (first, many, deep) in enumerate(tiles):
            weights = probs[half, :deep, first : first + many]
            grown = dot_t(values[:deep], head_grads[first : first + many])
            slopes = (weights.astype(f32) * (grown - shift[:, first : first + many])).astype(bf16)
            value_part = dot(weights, head_grads[first : first + many])
            key_part = dot(slopes, head_queries[first : first + many])
            value_sums[at] = value_part if half == 0 else value_sums[at] + value_part
            key_sums[at] = key_part if half == 0 else key_sums[at] + key_part
            pieces.append(dot(key_t[lanes, :deep], slopes))
        halves.append(jnp.concatenate(pieces, 1) if len(pieces) > 1 else pieces[0])
    both = jnp.concatenate(halves, 0).astype(bf16)
    grad_query[:, columns] = both.T
    for sums, out in ((key_sums, grad_key), (value_sums, grad_value)):
        if len(tiles) == 1:
            out[:, columns] = sums[0].astype(bf16)
        else:
            half_rows = rows // 2
            out[:half_rows, columns] = (sums[0] + sums[1][:half_rows]).astype(bf16)
            out[half_rows:, columns] = sums[1][half_rows:].astype(bf16)


def layer_kernel(
    count,
    copies,
    tokens,
    encoder,
    cotangent,
    self_qkv,
    self_out,
    cross_qkv,
    cross_out,
    ffn_in,
    ffn_out,
    adapt_down,
    down_bias,
    adapt_up,
    up_bias,
    norm_gain,
    norm_bias,
    shift,
    seq_lengths,
    enc_lengths,
    output,
    attn_kept,
    self_kept,
    self_key_kept,
    self_probs,
    cross_kept,
    cross_key_kept,
    cross_probs,
    normal_kept,
    inverse_kept,
    total_kept,
    cross_grads,
    self_grads,
    adapt_sums,
    vector_sums,
    mass,
    inbox,
    letters,
    vectors,
    attn,
    wide_in,
    wide_out,
    held,
    turned,
    low,
    tok,
    bias,
    probs,
    total,
    normal,
    inverse,
    narrow_act,
    narrow_slope,
    down,
    up,
    delta,
    send_sem,
    recv_sem,
    own_sem,
    load_sem,
    kept_sem,
    probs_sem,
    back_sem,
    sum_send_sem,
    sum_recv_sem,
    free_sem,
    post_sem,
    mail_sem,
):
    index = lax.axis_index("fsdp")
    thin = self_out.shape[0]
    deep = ffn_out.shape[0]
    rows, model = tok.shape
    unit = model // 8
    unit_in = ffn_in.shape[1] // 8
    hidden = ffn_in.shape[1]
    step_value = jnp.float32(STEP)
    branch_scale = step_value / (step_value + ramp_steps)

    def columns_of(first, units, width):
        return pl.ds(pl.multiple_of(first * width, width), units * width)

    views = (
        lambda f, first, units: attn.at[pl.ds(0, 3), part(f, thin), columns_of(first, units, unit)],
        lambda f, first, units: attn.at[pl.ds(3, 5), part(f, thin), columns_of(first, units, unit)],
        lambda f, first, units: wide_in.at[part(f, thin), columns_of(first, units, unit_in)],
        lambda f, first, units: wide_out.at[part(f, deep), columns_of(first, units, unit)],
    )
    mine = part(index, thin)
    owned = (
        ((self_qkv, attn.at[pl.ds(0, 3), mine]),),
        ((self_out, attn.at[3, mine]), (cross_qkv, attn.at[pl.ds(4, 3), mine]), (cross_out, attn.at[7, mine])),
        ((ffn_in, wide_in.at[mine]),),
        ((ffn_out, wide_out.at[part(index, deep)]),),
    )
    loads = []
    for group in owned:
        for source, target in group:
            loads.append(pltpu.make_async_copy(source, target, own_sem.at[len(loads)]))
    for load in loads:
        load.start()
    load_tok = pltpu.make_async_copy(tokens, tok, load_sem.at[0])
    load_enc = pltpu.make_async_copy(encoder, held.at[7], load_sem.at[1])
    load_down = pltpu.make_async_copy(adapt_down, down, load_sem.at[2])
    load_up = pltpu.make_async_copy(adapt_up, up, load_sem.at[3])
    for load in (load_tok, load_enc, load_down, load_up):
        load.start()
    gather = Gather(count, views, send_sem, recv_sem)
    reduction = Reduction(
        count,
        copies,
        mass,
        inbox,
        sum_send_sem,
        sum_recv_sem,
        free_sem,
        vectors,
        letters,
        post_sem,
        mail_sem,
    )
    gather.enter(reduction.partners)
    loads[0].wait()
    gather.own(0)
    for load in loads[1:]:
        load.wait()
    kept = []

    def keep(source, target):
        copy = pltpu.make_async_copy(source, target, kept_sem.at[len(kept)])
        copy.start()
        kept.append(copy)
        return copy

    def project(source, target, weight, scale=None):
        for block in range(2):
            columns = pl.ds(block * (model // 2), model // 2)
            product = dot(source[...], attn[weight, :, columns]).astype(bf16)
            target[:, columns] = product if scale is None else product * scale
            gather.tick()

    def attention(query, key, value, mixed, saved, key_saved, probs_saved, causal):
        turned[0] = value[...].T
        gather.tick()
        turned[1] = (key[...] * bf16(0.125)).T
        gather.tick()
        keep(turned.at[1], key_saved)
        steps = gather.take(16)

        def out_copy(pair, slot):
            return pltpu.make_async_copy(probs.at[slot], probs_saved.at[pl.ds(pair * 2, 2)], probs_sem.at[slot])

        pairs = HEADS // 2

        @pl.loop(0, pairs)
        def _(pair):
            slot = pair % 2
            pl.when(pair >= 2)(lambda: out_copy(pair - 2, slot).wait())
            attend_pair(pair, query, key, turned.at[0], bias, probs.at[slot], mixed, causal)
            out_copy(pair, slot).start()
            for at in range(pairs):
                mine_now = steps[2 * at : 2 * at + 2]

                @pl.when(pair == at)
                def _():
                    for step in mine_now:
                        step()

        for pair in (pairs - 2, pairs - 1):
            out_copy(pair, pair % 2).wait()

    def probs_in(saved, pair):
        slot = pair % 2
        return pltpu.make_async_copy(saved.at[pl.ds(pair * 2, 2)], probs.at[slot], probs_sem.at[slot])

    place_masks(bias, shift[0], seq_lengths, True)
    load_tok.wait()
    gather.need(0)
    keep(attn.at[pl.ds(0, 3)], attn_kept.at[pl.ds(0, 3)])
    project(tok, held.at[0], 0, bf16(0.125))
    project(tok, held.at[1], 1)
    project(tok, held.at[2], 2)
    attention(held.at[0], held.at[1], held.at[2], held.at[3], self_kept, self_key_kept, self_probs, True)
    keep(held.at[pl.ds(0, 4)], self_kept)
    turned_out = kept[1]

    gather.need(1)
    keep(attn.at[pl.ds(5, 2)], attn_kept.at[pl.ds(3, 2)])
    block_rows = 128
    blocks = rows // block_rows
    for half in range(2):
        columns = pl.ds(half * (model // 2), model // 2)
        total[:, columns] = tok[:, columns].astype(f32) + dot(held[3], attn[3, :, columns])
        gather.tick()

    @pl.loop(0, blocks)
    def _(block):
        here = part(block, block_rows)
        normal_one, inverse_one = layer_stats(total[here, :])
        normal[here, :] = normal_one
        inverse[here, :] = jnp.broadcast_to(inverse_one, (block_rows, 128))
        low[here, :] = (normal_one * norm_gain[0:1, :] + norm_bias[0:1, :]).astype(bf16)

    normal_out = keep(normal, normal_kept)
    inverse_out = keep(inverse, inverse_kept)
    place_masks(bias, shift[0], enc_lengths, False)
    load_enc.wait()
    turned_out.wait()
    project(low, held.at[4], 4, bf16(0.125))
    project(held.at[7], held.at[5], 5)
    project(held.at[7], held.at[6], 6)
    attention(held.at[4], held.at[5], held.at[6], held.at[7], cross_kept, cross_key_kept, cross_probs, False)
    keep(held.at[pl.ds(4, 4)], cross_kept)
    for half in range(2):
        columns = pl.ds(half * (model // 2), model // 2)
        first = normal[:, columns] * norm_gain[0:1, columns] + norm_bias[0:1, columns]
        total[:, columns] = first + dot(held[7], attn[7, :, columns])
        gather.tick()
    normal_out.wait()
    inverse_out.wait()

    @pl.loop(0, blocks)
    def _(block):
        here = part(block, block_rows)
        normal_two, inverse_two = layer_stats(total[here, :])
        normal[here, :] = normal_two
        inverse[here, :] = jnp.broadcast_to(inverse_two, (block_rows, 128))
        second = normal_two * norm_gain[1:2, :] + norm_bias[1:2, :]
        low[here, :] = second.astype(bf16)
        total[here, :] = second

    load_down.wait()
    load_up.wait()
    narrow = dot(low[...], down[...]) + down_bias[...]
    gate = 1.0 / (1.0 + jnp.exp(-narrow))
    narrow_act[...] = (narrow * gate).astype(bf16)
    narrow_slope[...] = (gate * (1.0 + narrow * (1.0 - gate))).astype(bf16)
    gather.tick()
    for half in range(2):
        columns = pl.ds(half * (model // 2), model // 2)
        branch = dot(narrow_act[...], up[:, columns]) + up_bias[:, columns]
        total[:, columns] += branch_scale * branch
        gather.tick()

    for copy in kept:
        if copy is not normal_out and copy is not inverse_out and copy is not turned_out:
            copy.wait()
    load_cots = [
        pltpu.make_async_copy(
            cotangent.at[:, pl.ds(half * (model // 2), model // 2)],
            turned.at[half, pl.ds(0, rows)],
            load_sem.at[half],
        )
        for half in range(2)
    ]
    for load in load_cots:
        load.start()
    gather.need(2)
    tile = model // 2
    act, slope = held.at[pl.ds(0, 4)], held.at[pl.ds(4, 4)]
    for block in range(hidden // tile):
        at, columns = block // 2, pl.ds((block % 2) * tile, tile)
        inner = dot(low[...], wide_in[:, pl.ds(block * tile, tile)])
        active, slant = gelu_both(inner)
        act[at, :, columns] = active.astype(bf16)
        slope[at, :, columns] = slant.astype(bf16)
        gather.tick(2)
    chunk = 2 * deep
    for chip in gather.chips(3):
        first = pl.multiple_of(chip * chunk, chunk)
        for half in range(2):
            columns = pl.ds(half * tile, tile)
            active = act[first // model, :, pl.ds(pl.multiple_of(first % model, chunk), chunk)]
            total[:, columns] += dot(active, wide_out[pl.ds(first, chunk), columns])
    for load in load_cots:
        load.wait()
    feed_grad = tok
    for name in range(8):
        vectors[0, name : name + 1, :] = jnp.zeros((1, model), f32)

    @pl.loop(0, blocks)
    def _(block):
        here = part(block, block_rows)
        normal_three, inverse_three = layer_stats(total[here, :])
        mass[part(block + blocks, block_rows), :] = (
            normal_three * norm_gain[2:3, :] + norm_bias[2:3, :]
        ).astype(bf16)
        low_grad = jnp.concatenate([turned[0, here, :], turned[1, here, :]], 1).astype(f32)
        grad_three = norm_back(low_grad, normal_three, inverse_three, norm_gain[2:3, :])
        total[here, :] = grad_three
        tok[here, :] = grad_three.astype(bf16)
        scaled = (branch_scale * grad_three).astype(bf16)
        turned[0, here, :] = scaled[:, : model // 2]
        turned[1, here, :] = scaled[:, model // 2 :]
        vectors[0, 2:3, :] += jnp.sum(low_grad * normal_three, 0, keepdims=True)
        vectors[0, 5:6, :] += jnp.sum(low_grad, 0, keepdims=True)
        vectors[0, 6:7, :] += jnp.sum(scaled.astype(f32), 0, keepdims=True)

    out_copy = pltpu.make_async_copy(mass.at[pl.ds(rows, rows)], output, load_sem.at[2])
    out_copy.start()
    adapt = narrow_act.shape[1]
    for half in range(2):
        columns = pl.ds(half * tile, tile)
        mass[pl.ds(0, adapt), columns] = t_dot(narrow_act[...], turned[half, :rows, :]).astype(bf16)
    grown = sum(dot_t(turned[half, :rows, :], up[:, pl.ds(half * tile, tile)]) for half in range(2))
    small = grown * narrow_slope[...].astype(f32)
    narrow_grad = narrow_act
    narrow_grad[...] = small.astype(bf16)
    vectors[0, 7:8, :adapt] = jnp.sum(narrow_grad[...].astype(f32), 0, keepdims=True)
    lowered = t_dot(low[...], narrow_grad[...]).astype(bf16)
    out_copy.wait()
    for at in range(model // adapt):
        mass[pl.ds(adapt, adapt), pl.ds(at * adapt, adapt)] = lowered[at * adapt : (at + 1) * adapt]
    reduction.tick()
    for pair in range(2):
        probs_in(cross_probs, pair).start()
    for at in range(hidden // model):
        for half in range(2):
            columns = pl.ds(half * tile, tile)
            grown = dot_t(feed_grad[...], wide_out[pl.ds(at * model + half * tile, tile), :])
            act[at, :, columns] = (grown * slope[at, :, columns].astype(f32)).astype(bf16)
        if at == 2:
            reduction.tick()
    gather.finish()
    old = {}

    def back(name, source, target):
        old[name] = pltpu.make_async_copy(source, target, back_sem.at[len(old)])
        old[name].start()

    def tile_out(at):
        return wide_out.at[pl.ds(at * rows, rows)]

    back("joined", cross_kept.at[3], tile_out(3))
    back("cross_value", cross_kept.at[2], tile_out(2))
    back("cross_query", cross_kept.at[0], tile_out(0))
    back("mixed", self_kept.at[3], tile_out(7))
    back("self_value", self_kept.at[2], tile_out(6))
    back("self_query", self_kept.at[0], tile_out(4))
    for half in range(2):
        columns = pl.ds(half * tile, tile)
        second_grad = total[:, columns] + dot_t(narrow_grad[...], down[columns, :])
        for at in range(hidden // model):
            second_grad += dot_t(act[at], wide_in[columns, pl.ds(at * model, model)])
        total[:, columns] = second_grad
    back("cross_key", cross_key_kept, wide_in.at[:, pl.ds(0, rows)])
    back("self_key", self_key_kept, wide_in.at[:, pl.ds(rows, rows)])

    @pl.loop(0, blocks)
    def _(block):
        here = part(block, block_rows)
        grad_second = total[here, :]
        normal_two = normal[here, :]
        vectors[0, 1:2, :] += jnp.sum(grad_second * normal_two, 0, keepdims=True)
        vectors[0, 4:5, :] += jnp.sum(grad_second, 0, keepdims=True)
        grad_two = norm_back(grad_second, normal_two, inverse[here, 0:1], norm_gain[1:2, :])
        total[here, :] = grad_two
        low[here, :] = grad_two.astype(bf16)

    reduction.tick()
    back("normal", normal_kept, normal)
    back("inverse", inverse_kept, inverse)
    grad, grad_query = held.at[0], held.at[1]

    def attention_back(probs_saved, base, key_t, weight, causal, names, grads, ticks):
        for half in range(2):
            columns = pl.ds(half * tile, tile)
            grad[:, columns] = dot_t(low[...], attn[weight, columns, :]).astype(bf16)
        for name in names:
            old[name].wait()
        head = lax.broadcasted_iota(jnp.int32, (HEADS, model), 0)
        lane = lax.broadcasted_iota(jnp.int32, (HEADS, model), 1)
        chosen = (lane // 64 == head).astype(bf16)
        product = grad[...].astype(f32) * tile_out(base + 3)[...].astype(f32)
        rough = product.astype(bf16)
        fine = (product - rough.astype(f32)).astype(bf16)
        delta[...] = dot_t(chosen, rough) + dot_t(chosen, fine)
        pairs = HEADS // 2

        @pl.loop(0, pairs)
        def _(pair):
            slot = pair % 2
            probs_in(probs_saved, pair).wait()
            back_pair(
                pair,
                tile_out(base),
                key_t,
                tile_out(base + 2),
                grad,
                probs.at[slot],
                delta,
                *grads,
                causal,
            )

            @pl.when(pair + 2 < pairs)
            def _():
                probs_in(probs_saved, pair + 2).start()

            for at, tick in ticks:
                pl.when(pair == at)(functools.partial(tick))

    attention_back(
        cross_probs,
        0,
        wide_in.at[:, pl.ds(0, rows)],
        7,
        False,
        ("joined", "cross_value", "cross_query", "cross_key"),
        (grad_query, held.at[2], held.at[3]),
        ((0, reduction.tick), (3, reduction.tick), (5, reduction.tick)),
    )
    for pair in range(2):
        probs_in(self_probs, pair).start()
    back("cross_grads", held.at[pl.ds(2, 2)], cross_grads)
    reduction.tick()
    for half in range(2):
        columns = pl.ds(half * tile, tile)
        total[:, columns] += dot_t(grad_query[...], attn[4, columns, :])
    for name in ("normal", "inverse"):
        old[name].wait()

    @pl.loop(0, blocks)
    def _(block):
        here = part(block, block_rows)
        grad_first = total[here, :]
        normal_one = normal[here, :]
        vectors[0, 0:1, :] += jnp.sum(grad_first * normal_one, 0, keepdims=True)
        vectors[0, 3:4, :] += jnp.sum(grad_first, 0, keepdims=True)
        grad_one = norm_back(grad_first, normal_one, inverse[here, 0:1], norm_gain[0:1, :])
        total[here, :] = grad_one
        low[here, :] = grad_one.astype(bf16)

    reduction.tick()
    reduction.post_tick()
    back("total", total, total_kept)

    def both_ticks():
        reduction.tick()
        reduction.post_tick()

    attention_back(
        self_probs,
        4,
        wide_in.at[:, pl.ds(rows, rows)],
        3,
        True,
        ("mixed", "self_value", "self_query", "self_key"),
        tuple(held.at[at] for at in (4, 5, 6)),
        ((0, both_ticks), (2, reduction.post_tick), (4, both_ticks), (6, reduction.post_tick)),
    )
    back("self_grads", held.at[pl.ds(4, 3)], self_grads)
    reduction.tick(99)
    back("sums", mass, adapt_sums)
    reduction.post_tick(99)
    back("vectors", vectors.at[reduction.bits], vector_sums)
    reduction.finish()
    for name in ("cross_grads", "self_grads", "total", "sums", "vectors"):
        old[name].wait()


def layer(count, copies, *args):
    tokens, ffn_in, adapt_down = args[0], args[7], args[9]
    rows, model = tokens.shape
    hidden, adapt = ffn_in.shape[1], adapt_down.shape[1]
    bits = (count * copies).bit_length() - 1
    shape = jax.ShapeDtypeStruct
    return pl.pallas_call(
        functools.partial(layer_kernel, count, copies),
        out_shape=[
            shape((rows, model), bf16),
            shape((5, model, model), bf16),
            shape((4, rows, model), bf16),
            shape((model, rows), bf16),
            shape((HEADS, rows, rows), bf16),
            shape((4, rows, model), bf16),
            shape((model, rows), bf16),
            shape((HEADS, rows, rows), bf16),
            shape((rows, model), f32),
            shape((rows, 128), f32),
            shape((rows, model), f32),
            shape((2, rows, model), bf16),
            shape((3, rows, model), bf16),
            shape((2 * adapt, model), bf16),
            shape((8, model), f32),
        ],
        in_specs=[ANY] * 10
        + [pl.BlockSpec(memory_space=pltpu.VMEM), ANY]
        + [pl.BlockSpec(memory_space=pltpu.VMEM)] * 3
        + [SMEM] * 3,
        out_specs=[ANY] * 15,
        scratch_shapes=[
            pltpu.VMEM((2 * adapt, model), bf16),
            pltpu.VMEM((2 * box_rows(adapt, bits), model), bf16),
            pltpu.VMEM((bits, 8, model), f32),
            pltpu.VMEM((bits + 1, 8, model), f32),
            pltpu.VMEM((8, model, model), bf16),
            pltpu.VMEM((model, hidden), bf16),
            pltpu.VMEM((hidden, model), bf16),
            pltpu.VMEM((8, rows, model), bf16),
            pltpu.VMEM((2, model, rows), bf16),
            pltpu.VMEM((rows, model), bf16),
            pltpu.VMEM((rows, model), bf16),
            pltpu.VMEM((rows, rows), bf16),
            pltpu.VMEM((2, 2, rows, rows), bf16),
            pltpu.VMEM((rows, model), f32),
            pltpu.VMEM((rows, model), f32),
            pltpu.VMEM((rows, 128), f32),
            pltpu.VMEM((rows, adapt), bf16),
            pltpu.VMEM((rows, adapt), bf16),
            pltpu.VMEM((model, adapt), bf16),
            pltpu.VMEM((adapt, model), bf16),
            pltpu.VMEM((HEADS, rows), f32),
            pltpu.SemaphoreType.DMA((2, sends_per_phase(count))),
            pltpu.SemaphoreType.DMA((4, 2, count // 2, 4)),
            pltpu.SemaphoreType.DMA((6,)),
            pltpu.SemaphoreType.DMA((4,)),
            pltpu.SemaphoreType.DMA((10,)),
            pltpu.SemaphoreType.DMA((2,)),
            pltpu.SemaphoreType.DMA((16,)),
            pltpu.SemaphoreType.DMA((4 * bits,)),
            pltpu.SemaphoreType.DMA((4 * bits,)),
            pltpu.SemaphoreType.REGULAR((2 * bits,)),
            pltpu.SemaphoreType.DMA((bits,)),
            pltpu.SemaphoreType.DMA((bits,)),
        ],
        compiler_params=pltpu.CompilerParams(
            collective_id=0, has_side_effects=True, vmem_limit_bytes=63 * 2**20
        ),
        name="decoder_layer",
    )(*args)


def results_kernel(
    output,
    attn_kept,
    total_kept,
    cross_grads,
    self_grads,
    adapt_sums,
    vector_sums,
    output_out,
    tokens_out,
    encoder_out,
    down_out,
    down_bias_out,
    up_out,
    up_bias_out,
    gain_out,
    bias_out,
    attn,
    total,
    crossed,
    selfed,
    sums,
    down,
    up,
    tokens,
    encoder,
    passed,
    sem,
    out_sem,
):
    rows, model = total.shape
    adapt = up.shape[0]
    half = model // 2
    loads = [
        pltpu.make_async_copy(source, target, sem.at[at])
        for at, (source, target) in enumerate(
            (
                (cross_grads, crossed),
                (attn_kept.at[pl.ds(3, 2)], attn.at[pl.ds(3, 2)]),
                (adapt_sums, sums),
                (self_grads, selfed),
                (attn_kept.at[pl.ds(0, 3)], attn.at[pl.ds(0, 3)]),
                (total_kept, total),
                (output, passed),
            )
        )
    ]
    for load in loads:
        load.start()
    outs = []

    def put(source, target):
        outs.append(pltpu.make_async_copy(source, target, out_sem.at[len(outs)]))
        outs[-1].start()

    for at, out in ((0, gain_out), (3, bias_out)):
        out[...] = vector_sums[at : at + 3, :]
    up_bias_out[...] = vector_sums[6, :]
    down_bias_out[...] = vector_sums[7, :adapt]
    loads[0].wait()
    loads[1].wait()
    for at in range(2):
        columns = pl.ds(at * half, half)
        gathered = dot_t(crossed[0], attn[3, columns, :]) + dot_t(crossed[1], attn[4, columns, :])
        encoder[:, columns] = gathered.astype(bf16)
    put(encoder, encoder_out)
    loads[6].wait()
    put(passed, output_out)
    loads[2].wait()
    up[...] = sums[:adapt, :].astype(f32)
    put(up, up_out)
    for at in range(model // adapt):
        down[pl.ds(at * adapt, adapt), :] = sums[pl.ds(adapt, adapt), pl.ds(at * adapt, adapt)].astype(f32)
    put(down, down_out)
    for load in loads[3:6]:
        load.wait()
    for at in range(2):
        columns = pl.ds(at * half, half)
        gathered = total[:, columns]
        for name in range(3):
            gathered += dot_t(selfed[name], attn[name, columns, :])
        tokens[:, columns] = gathered.astype(bf16)
    put(tokens, tokens_out)
    for copy in outs:
        copy.wait()


def results(adapt, output, attn_kept, total, cross_grads, self_grads, adapt_sums, vector_sums):
    rows, model = output.shape
    shape = jax.ShapeDtypeStruct
    inside = pl.BlockSpec(memory_space=pltpu.VMEM)
    return pl.pallas_call(
        results_kernel,
        out_shape=[
            shape((rows, model), bf16),
            shape((rows, model), bf16),
            shape((rows, model), bf16),
            shape((model, adapt), f32),
            shape((adapt,), f32),
            shape((adapt, model), f32),
            shape((model,), f32),
            shape((3, model), f32),
            shape((3, model), f32),
        ],
        in_specs=[ANY] * 6 + [inside],
        out_specs=[ANY] * 4 + [inside, ANY] + [inside] * 3,
        scratch_shapes=[
            pltpu.VMEM((5, model, model), bf16),
            pltpu.VMEM((rows, model), f32),
            pltpu.VMEM((2, rows, model), bf16),
            pltpu.VMEM((3, rows, model), bf16),
            pltpu.VMEM((2 * adapt, model), bf16),
            pltpu.VMEM((model, adapt), f32),
            pltpu.VMEM((adapt, model), f32),
            pltpu.VMEM((rows, model), bf16),
            pltpu.VMEM((rows, model), bf16),
            pltpu.VMEM((rows, model), bf16),
            pltpu.SemaphoreType.DMA((7,)),
            pltpu.SemaphoreType.DMA((5,)),
        ],
        compiler_params=pltpu.CompilerParams(vmem_limit_bytes=63 * 2**20),
        name="last_projections",
    )(output, attn_kept, total, cross_grads, self_grads, adapt_sums, vector_sums)


def local(*args):
    count, copies = lax.axis_size("fsdp"), lax.axis_size("dp")
    args = list(args)
    adapt = args[10].shape[0]
    args[10], args[12] = args[10][None], args[12][None]
    kept = layer(count, copies, *args)
    return tuple(results(adapt, kept[0], kept[1], *kept[10:]))


def solution(mesh):
    rows = P(("fsdp", "dp"), None)
    placed = (
        (rows,) * 3
        + (P(None, "fsdp", None), P("fsdp", None)) * 2
        + (P("fsdp", None),) * 2
        + (P(),) * 6
        + (P(("fsdp", "dp")), rows, rows)
    )
    return jax.shard_map(
        local, mesh=mesh, in_specs=placed, out_specs=(rows,) * 3 + (P(),) * 6, check_vma=False
    )
```

```python
import functools

import jax
import jax.numpy as jnp
from jax import lax
from jax.experimental import pallas as pl
from jax.experimental.pallas import tpu as pltpu
from jax.sharding import PartitionSpec as P

HEADS = 16
STEP = 12
LINE = 4
MESH = pl.DeviceIdType.MESH
ANY = pl.BlockSpec(memory_space=pl.ANY)
SMEM = pl.BlockSpec(memory_space=pltpu.SMEM)
bf16 = jnp.bfloat16
f32 = jnp.float32

epsilon = 1e-05
ramp_steps = 4.0
masked_score = -1e30
lead = 1.0
even_phases = (0, 1)
x_slack = 0.05
plane_slack = 0.1
out_cut = 0.5


def dot(left, right):
    return jnp.dot(left, right, preferred_element_type=f32)


def dot_t(left, right):
    return lax.dot_general(left, right, (((1,), (1,)), ((), ())), preferred_element_type=f32)


def t_dot(left, right):
    return lax.dot_general(left, right, (((0,), (0,)), ((), ())), preferred_element_type=f32)


def part(index, size):
    return pl.ds(pl.multiple_of(index * size, size), size)


def layer_stats(values_in):
    average = jnp.mean(values_in, -1, keepdims=True)
    centred = values_in - average
    inverse = lax.rsqrt(jnp.mean(centred * centred, -1, keepdims=True) + epsilon)
    return (centred * inverse, inverse)


def norm_back(grad_out, normal, inverse, norm_scale):
    grad_normal = grad_out * norm_scale
    return inverse * (
        grad_normal
        - jnp.mean(grad_normal, -1, keepdims=True)
        - normal * jnp.mean(grad_normal * normal, -1, keepdims=True)
    )


def nearest(place, count, rank):
    under, over = place, count - 1 - place
    both = jnp.minimum(under, over)
    side = jnp.where(under > over, -1, 1)
    paired = place + (side * ((rank + 1) // 2) if rank % 2 == 1 else -side * (rank // 2))
    alone = jnp.where(over > under, place + rank - both, place - (rank - both))
    return jnp.where(rank <= 2 * both, paired, alone)


def mesh_shape(count):
    line = min(LINE, count // 2)
    return line, count // (2 * line)


def sends_per_phase(count):
    line, wide = mesh_shape(count)
    across = 1 if wide == 2 else 2
    each = 2 * (2 + across) + 1
    return line * each + (wide - 1) * line * 2 * (1 + across) + (line - 1) + (wide - 1) * line * 2


class Gather:
    def __init__(self, count, views, sizes, send_sem, recv_sem):
        self.views, self.sizes, self.send_sem, self.recv_sem = views, sizes, send_sem, recv_sem
        self.line, self.wide = mesh_shape(count)
        index = lax.axis_index("fsdp")
        self.dp = lax.axis_index("dp")
        self.core = index % 2
        self.x = (index // 2) % self.wide
        self.z = index // (2 * self.wide)
        p = self.dp % 2
        self.other_core = (self.place(self.z, self.x, 1 - self.core), self.dp)
        self.other_plane = (index, self.dp + 1 - 2 * p)
        self.same = ((2 * p, 2), (4, 4), (2 - 2 * p, 2))
        uneven = ((2 * p, 2), (4 + p, 3), (2 - 2 * p, 2), (7 - 3 * p, 1))
        even = ((2 * p, 2), (4 + 2 * p, 2), (2 - 2 * p, 2), (6 - 2 * p, 2))
        self.cross = [even if phase in even_phases else uneven for phase in range(len(views))]
        self.single = [(4 + 2 * p, 2) if phase in even_phases else (4 + 3 * p, 1) for phase in range(len(views))]
        self.z_up = (self.along_z(1), self.z < self.line - 1)
        self.z_down = (self.along_z(-1), self.z > 0)
        if self.wide == 2:
            self.x_ways = ((self.along_x(1 - 2 * self.x), None),)
        else:
            self.x_ways = ((self.along_x(1), self.x < self.wide - 1), (self.along_x(-1), self.x > 0))
        self.sends = {}
        self.counts = [0] * len(views)
        self.steps = self.plan()
        self.done = 0

    def place(self, z, x, core):
        return (z * self.wide + x) * 2 + core

    def along_z(self, step):
        return (self.place(self.z + step, self.x, self.core), self.dp)

    def along_x(self, step):
        return (self.place(self.z, self.x + step, self.core), self.dp)

    def copy(self, at, kind, span, slot, target):
        phase, core, z, x = at
        view = self.views[phase](self.place(z, x, core), *span)
        return pltpu.make_async_remote_copy(
            src_ref=view,
            dst_ref=view,
            send_sem=self.send_sem.at[phase, slot],
            recv_sem=self.recv_sem.at[phase, core, z * self.wide + x, kind],
            device_id=target,
            device_id_type=MESH,
        )

    def send(self, at, kind, span, target, when=None):
        slot = self.counts[at[0]]
        self.counts[at[0]] += 1
        remake = functools.partial(self.copy, at, kind, span, slot, target)
        if when is None:
            remake().start()
        else:
            pl.when(when)(lambda: remake().start())
        self.sends[at[0], slot] = (remake, when)

    def arrive(self, at, kind, span):
        phase, core, z, x = at
        view = self.views[phase](self.place(z, x, core), *span)
        pltpu.make_async_copy(view, view, self.recv_sem.at[phase, core, z * self.wide + x, kind]).wait()

    def plan(self):
        span = self.line - 1
        steps = []
        for phase in range(len(self.views)):
            base, size = span * sum(self.sizes[:phase]), self.sizes[phase]

            def add(when, slack, makers, chip):
                steps.extend((base + size * when + slack, phase, maker, chip) for maker in makers)

            for far in range(self.line):
                z_from = nearest(self.z, self.line, far)
                if far:
                    add(far, 0.0, self.from_z((phase, self.core, z_from, self.x)), (far, 0))
                    add(far + 1, plane_slack, self.from_plane((phase, self.core, z_from, self.x), self.same), (far, 0))
                for apart in range(1, self.wide):
                    at = (phase, self.core, z_from, nearest(self.x, self.wide, apart))
                    add(far + apart, x_slack, self.from_x(at), (far, apart))
                    add(far + apart + 1, x_slack + plane_slack, self.from_plane(at, self.cross[phase]), (far, apart))
            if phase:
                steps.append((base - lead, phase, functools.partial(self.own, phase), None))
        return sorted(steps, key=lambda item: item[0])

    def own(self, phase):
        at = (phase, self.core, self.z, self.x)
        for kind in (0, 1):
            self.send(at, kind, self.same[kind], *self.z_up)
            self.send(at, kind, self.same[kind], *self.z_down)
            self.over_x(at, kind)
        self.send(at, 0, (0, 8), self.other_core)

    def over_x(self, at, kind):
        for way in self.x_ways:
            self.send(at, kind, self.cross[at[0]][kind], *way)

    def from_z(self, at):
        upward = at[2] < self.z
        onward = (upward & self.z_up[1]) | (~upward & self.z_down[1])
        target = self.along_z(jnp.where(upward, 1, -1))

        def step(kind):
            self.arrive(at, kind, self.same[kind])
            self.send(at, kind, self.same[kind], target, onward)
            self.over_x(at, kind)
            if kind == 0:
                self.send(at, 2, self.same[0], self.other_plane)
            self.send(at, kind, self.same[kind], self.other_core)

        return [functools.partial(step, 0), functools.partial(step, 1)]

    def from_x(self, at):
        cross = self.cross[at[0]]
        upward = at[3] < self.x
        onward = (upward & (self.x < self.wide - 1)) | (~upward & (self.x > 0))
        target = self.along_x(jnp.where(upward, 1, -1))

        def step(kind):
            self.arrive(at, kind, cross[kind])
            if self.wide > 2:
                self.send(at, kind, cross[kind], target, onward)
            self.send(at, kind + 2, cross[0] if kind == 0 else self.single[at[0]], self.other_plane)
            self.send(at, kind, cross[kind], self.other_core)

        return [functools.partial(step, 0), functools.partial(step, 1)]

    def from_plane(self, at, spans):
        def step():
            for kind in range(2, len(spans)):
                self.arrive(at, kind, spans[kind])
                self.send(at, kind, spans[kind], self.other_core)

        return [step]

    def tick(self, many=1):
        for _ in range(many):
            if self.done < len(self.steps):
                self.done += 1
                self.steps[self.done - 1][2]()

    def take(self, many):
        first = self.done
        self.done = min(len(self.steps), first + many)
        return [step[2] for step in self.steps[first : self.done]]

    def need(self, phase):
        last = max(i for i, step in enumerate(self.steps) if step[1] == phase)
        self.tick(last + 1 - self.done)
        for z in range(self.line):
            for x in range(self.wide):
                self.other_half(phase, z, x)

    def chips(self, phase):
        for far in range(self.line):
            for apart in range(self.wide):
                own = [i for i, step in enumerate(self.steps) if step[1] == phase and step[3] == (far, apart)]
                self.tick(max(own, default=-1) + 1 - self.done)
                z, x = nearest(self.z, self.line, far), nearest(self.x, self.wide, apart)
                self.other_half(phase, z, x)
                yield self.place(z, x, 0) // 2

    def other_half(self, phase, z, x):
        at = (phase, 1 - self.core, z, x)

        def pieces(spans):
            for kind, span in enumerate(spans):
                self.arrive(at, kind, span)

        own_chip = (z == self.z) & (x == self.x)
        pl.when(own_chip)(lambda: self.arrive(at, 0, (0, 8)))
        pl.when((x == self.x) & (z != self.z))(lambda: pieces(self.same))
        pl.when(x != self.x)(lambda: pieces(self.cross[phase]))

    def finish(self, phases):
        for key in [key for key in self.sends if key[0] in phases]:
            remake, when = self.sends.pop(key)
            if when is None:
                remake().wait_send()
            else:
                pl.when(when)(lambda: remake().wait_send())


def place_masks(bias, shift, lengths, causal):
    rows = bias.shape[0]
    wide = 128
    bits = shift + (rows // 4).bit_length() - 1

    @pl.loop(0, rows // wide)
    def _(block):
        shape = (wide, rows)
        key = lax.broadcasted_iota(jnp.int32, shape, 0) + block * wide
        query = lax.broadcasted_iota(jnp.int32, shape, 1)
        key_seq = lax.shift_right_logical(key, jnp.full(shape, bits, jnp.int32))
        query_seq = lax.shift_right_logical(query, jnp.full(shape, bits, jnp.int32))
        start = lax.shift_left(key_seq, jnp.full(shape, bits, jnp.int32))
        length = jnp.zeros(shape, jnp.int32)
        for slot in range(4):
            length = jnp.where(key_seq == slot, lengths[0, slot], length)
        allowed = (key_seq == query_seq) & (key - start < length)
        if causal:
            allowed = allowed & (key <= query)
        bias[part(block, wide), :] = jnp.where(allowed, 0.0, masked_score).astype(bf16)


def tiles_of(rows, causal):
    half = rows // 2
    return ((0, half, half), (half, half, rows)) if causal else ((0, rows, rows),)


def head_lanes(values, half):
    lane = lax.broadcasted_iota(jnp.int32, values.shape, 1)
    return jnp.where((lane // 64) == half, values, jnp.zeros_like(values))


def attend_pair(pair, query, key, value_t, bias, probs, out, causal):
    rows = query.shape[0]
    columns = part(pair, 128)
    keys = key[:, columns]
    queries = query[:, columns]
    halves = []
    for half in range(2):
        head_queries = head_lanes(queries, half)
        lanes = pl.ds(pl.multiple_of(pair * 128 + half * 64, 64), 64)
        pieces = []
        for first, many, deep in tiles_of(rows, causal):
            scores = dot_t(keys[:deep], head_queries[first : first + many])
            scores = scores + bias[:deep, first : first + many].astype(f32)
            expanded = jnp.exp(scores - jnp.max(scores, 0, keepdims=True))
            total = jnp.sum(expanded, 0, keepdims=True)
            block = (expanded * (1.0 / total)).astype(bf16)
            probs[half, :deep, first : first + many] = block
            pieces.append(dot(value_t[lanes, :deep], block))
        halves.append(jnp.concatenate(pieces, 1) if len(pieces) > 1 else pieces[0])
    both = jnp.concatenate(halves, 0).astype(bf16)
    out[:, columns] = both.T


def gelu_both(inner):
    spread = 0.5 + 0.5 * lax.erf(inner * (0.5**0.5))
    bell = jnp.exp(inner * inner * -0.5) * 0.3989422804014327
    return inner * spread, spread + inner * bell


def exchange_groups(count, copies):
    line, wide = mesh_shape(count)
    groups, size = [[]], 1
    for name, long in (("core", 2), ("x", wide), ("dp", copies), ("z", line)):
        if size * long > 8:
            groups.append([])
            size = 1
        groups[-1].append(name)
        size *= long
    return groups


def letters_of(count, copies):
    line, wide = mesh_shape(count)
    sizes = {"core": 2, "x": wide, "dp": copies, "z": line}
    found = 0
    for names in exchange_groups(count, copies):
        size = 1
        for name in names:
            size *= sizes[name]
        found += size
    return found


class Exchange:
    def __init__(self, count, copies, held, letters, send_sem, recv_sem):
        self.held, self.letters, self.send_sem, self.recv_sem = held, letters, send_sem, recv_sem
        line, wide = mesh_shape(count)
        index, dp = lax.axis_index("fsdp"), lax.axis_index("dp")
        places = {
            "core": (index % 2, 2),
            "x": ((index // 2) % wide, wide),
            "dp": (dp, copies),
            "z": (index // (2 * wide), line),
        }
        self.groups, self.ranks = [], []
        for names in exchange_groups(count, copies):
            size = 1
            rank = 0
            for name in names:
                rank = rank + places[name][0] * size
                size *= places[name][1]
            targets = []
            for ahead in range(1, size):
                other = (rank + ahead) % size
                at = {name: place for name, (place, _) in places.items()}
                for name in names:
                    at[name] = other % places[name][1]
                    other = other // places[name][1]
                targets.append(((at["z"] * wide + at["x"]) * 2 + at["core"], at["dp"]))
            self.groups.append(targets)
            self.ranks.append(rank)
        self.targets = [target for group in self.groups for target in group]
        last = len(self.groups) - 1
        self.steps = [[functools.partial(self.send, 0)]]
        for stage in range(last):
            self.steps.append([functools.partial(self.add, stage), functools.partial(self.send, stage + 1)])
        self.steps.append([functools.partial(self.add, last)])

    def enter(self):
        barrier = pltpu.get_barrier_semaphore()
        for target in self.targets:
            pl.semaphore_signal(barrier, inc=1, device_id=target, device_id_type=MESH)
        pl.semaphore_wait(barrier, len(self.targets))

    def first(self, stage):
        return sum(len(group) + 1 for group in self.groups[:stage])

    def copies_of(self, stage):
        first = self.first(stage)
        for at, target in enumerate(self.groups[stage]):
            yield pltpu.make_async_remote_copy(
                src_ref=self.held.at[stage],
                dst_ref=self.letters.at[first + self.ranks[stage]],
                send_sem=self.send_sem.at[first + at],
                recv_sem=self.recv_sem.at[first + at],
                device_id=target,
                device_id_type=MESH,
            )

    def send(self, stage):
        for copy in self.copies_of(stage):
            copy.start()
        self.letters[self.first(stage) + self.ranks[stage]] = self.held[stage]

    def add(self, stage):
        for copy in self.copies_of(stage):
            copy.wait_send()
        first, size = self.first(stage), len(self.groups[stage]) + 1
        for ahead in range(1, size):
            box = self.letters.at[first + (self.ranks[stage] - ahead + size) % size]
            pltpu.make_async_copy(box, box, self.recv_sem.at[first + ahead - 1]).wait()
        total = self.letters[first]
        for at in range(1, size):
            total = total + self.letters[first + at]
        self.held[stage + 1] = total

    def tick(self, many=1):
        for _ in range(min(many, len(self.steps))):
            for step in self.steps.pop(0):
                step()


def box_rows(height, bits):
    return sum(max(16, height >> (step + 1)) for step in range(bits))


class Reduction:
    def __init__(self, count, copies, mass, inbox, send_sem, recv_sem, free_sem):
        self.mass, self.inbox, self.free_sem = mass, inbox, free_sem
        self.send_sem, self.recv_sem = send_sem, recv_sem
        line, wide = mesh_shape(count)
        index, dp = lax.axis_index("fsdp"), lax.axis_index("dp")

        def along(coordinate, weight, size, move):
            found = []
            step = 1
            while step < size:
                bit = (coordinate // step) % 2
                found.append((bit, move((1 - 2 * bit) * step * weight)))
                step *= 2
            return found

        def fsdp(weight, size):
            return along((index // weight) % size, weight, size, lambda by: (index + by, dp))

        core, x, z = fsdp(1, 2), fsdp(2, wide), fsdp(2 * wide, line)
        planes = along(dp, 1, copies, lambda by: (index, dp + by))
        self.orders = (core + x + planes + z, core + planes + x + z)
        self.bits = len(self.orders[0])
        self.sends = []
        self.regions = []
        height, width = mass.shape[0] // len(self.orders), mass.shape[1]
        for at, order in enumerate(self.orders):
            first, high, left, broad, box = at * height, height, 0, width, at * box_rows(height, self.bits)
            regions = []
            for bit, target in order:
                if high > 16:
                    high //= 2
                    kept = (first + bit * high, high, left, broad)
                    away = (first + (1 - bit) * high, high, left, broad)
                else:
                    broad //= 2
                    kept = (first, high, left + bit * broad, broad)
                    away = (first, high, left + (1 - bit) * broad, broad)
                first, left = kept[0], kept[2]
                regions.append((kept, away, box, target))
                box += high
            self.regions.append(regions)
        last = self.bits - 1
        self.steps = [functools.partial(self.scatter, 0)]
        for step in range(last):
            self.steps.append(functools.partial(self.turn, (self.add, step), (self.scatter, step + 1)))
        self.steps.append(functools.partial(self.turn, (self.add, last), (self.spread, last)))
        for step in range(last, 0, -1):
            self.steps.append(functools.partial(self.turn, (self.landed, step), (self.spread, step - 1)))
        self.steps.append(functools.partial(self.landed, 0))

    def turn(self, one, other):
        one[0](one[1])
        other[0](other[1])

    def tick(self, many=1):
        for _ in range(min(many, len(self.steps))):
            self.steps.pop(0)()

    def remote(self, source, target_ref, sems, slot, target):
        return pltpu.make_async_remote_copy(
            src_ref=source,
            dst_ref=target_ref,
            send_sem=sems[0].at[slot],
            recv_sem=sems[1].at[slot],
            device_id=target,
            device_id_type=MESH,
        )

    def view(self, region):
        first, high, left, broad = region
        return self.mass.at[
            pl.ds(pl.multiple_of(first, 16), high), pl.ds(pl.multiple_of(left, 128), broad)
        ]

    def box(self, at, step):
        (_, high, _, broad), _, box, _ = self.regions[at][step]
        return self.inbox.at[pl.ds(box, high), pl.ds(0, broad)]

    def scatter_copy(self, at, step):
        _, away, _, target = self.regions[at][step]
        sems = (self.send_sem, self.recv_sem)
        return self.remote(self.view(away), self.box(at, step), sems, at * 2 * self.bits + step, target)

    def spread_copy(self, at, step):
        kept, _, _, target = self.regions[at][step]
        sems = (self.send_sem, self.recv_sem)
        slot = at * 2 * self.bits + self.bits + step
        return self.remote(self.view(kept), self.view(kept), sems, slot, target)

    def scatter(self, step):
        for at in range(len(self.orders)):
            self.scatter_copy(at, step).start()

    def add(self, step):
        for at in range(len(self.orders)):
            self.scatter_copy(at, step).wait()
            pl.semaphore_signal(
                self.free_sem.at[at * self.bits + step],
                inc=1,
                device_id=self.regions[at][step][3],
                device_id_type=MESH,
            )
            mine, arrived = self.view(self.regions[at][step][0]), self.box(at, step)
            rows = min(64, mine.shape[0])

            @pl.loop(0, mine.shape[0] // rows)
            def _(block):
                here = part(block, rows)
                mine[here, :] = (mine[here, :].astype(f32) + arrived[here, :].astype(f32)).astype(bf16)

    def spread(self, step):
        for at in range(len(self.orders)):
            pl.semaphore_wait(self.free_sem.at[at * self.bits + step], 1)
            self.spread_copy(at, step).start()
            self.sends.append(functools.partial(self.spread_copy, at, step))

    def landed(self, step):
        for at in range(len(self.orders)):
            view = self.view(self.regions[at][step][1])
            slot = at * 2 * self.bits + self.bits + step
            pltpu.make_async_copy(view, view, self.recv_sem.at[slot]).wait()

    def finish(self):
        for remake in self.sends:
            remake().wait_send()


def back_pair(pair, query, key_t, value, grad, probs, delta, grad_query, grad_key, grad_value, causal):
    rows = query.shape[0]
    columns = part(pair, 128)
    values, queries, grads = value[:, columns], query[:, columns], grad[:, columns]
    tiles = tiles_of(rows, causal)
    key_sums = [None] * len(tiles)
    value_sums = [None] * len(tiles)
    halves = []
    for half in range(2):
        head_grads = head_lanes(grads, half)
        head_queries = head_lanes(queries, half)
        lanes = pl.ds(pl.multiple_of(pair * 128 + half * 64, 64), 64)
        shift = delta[pl.ds(pair * 2 + half, 1), :]
        pieces = []
        for at, (first, many, deep) in enumerate(tiles):
            weights = probs[half, :deep, first : first + many]
            grown = dot_t(values[:deep], head_grads[first : first + many])
            slopes = (weights.astype(f32) * (grown - shift[:, first : first + many])).astype(bf16)
            value_part = dot(weights, head_grads[first : first + many])
            key_part = dot(slopes, head_queries[first : first + many])
            value_sums[at] = value_part if half == 0 else value_sums[at] + value_part
            key_sums[at] = key_part if half == 0 else key_sums[at] + key_part
            pieces.append(dot(key_t[lanes, :deep], slopes))
        halves.append(jnp.concatenate(pieces, 1) if len(pieces) > 1 else pieces[0])
    both = jnp.concatenate(halves, 0).astype(bf16)
    grad_query[:, columns] = both.T
    for sums, out in ((key_sums, grad_key), (value_sums, grad_value)):
        if len(tiles) == 1:
            out[:, columns] = sums[0].astype(bf16)
        else:
            half_rows = rows // 2
            out[:half_rows, columns] = (sums[0] + sums[1][:half_rows]).astype(bf16)
            out[half_rows:, columns] = sums[1][half_rows:].astype(bf16)


def layer_kernel(
    count,
    copies,
    tokens,
    encoder,
    cotangent,
    self_qkv,
    self_out,
    cross_qkv,
    cross_out,
    ffn_in,
    ffn_out,
    adapt_down,
    down_bias,
    adapt_up,
    up_bias,
    norm_gain,
    norm_bias,
    shift,
    seq_lengths,
    enc_lengths,
    output,
    self_kept,
    self_key_kept,
    self_probs,
    cross_kept,
    cross_key_kept,
    cross_probs,
    normal_kept,
    inverse_kept,
    grad_encoder,
    grad_tokens,
    adapt_sums,
    vector_sums,
    mass,
    inbox,
    letters,
    vectors,
    late_letters,
    late_vectors,
    attn,
    wide_in,
    wide_out,
    held,
    turned,
    low,
    tok,
    bias,
    probs,
    total,
    normal,
    inverse,
    narrow_act,
    narrow_slope,
    down,
    up,
    delta,
    send_sem,
    recv_sem,
    own_sem,
    load_sem,
    kept_sem,
    probs_sem,
    back_sem,
    sum_send_sem,
    sum_recv_sem,
    free_sem,
    post_sem,
    mail_sem,
    late_post_sem,
    late_mail_sem,
):
    index = lax.axis_index("fsdp")
    thin = self_out.shape[0]
    deep = ffn_out.shape[0]
    rows, model = tok.shape
    unit = model // 8
    unit_in = ffn_in.shape[1] // 8
    hidden = ffn_in.shape[1]
    step_value = jnp.float32(STEP)
    branch_scale = step_value / (step_value + ramp_steps)

    def columns_of(first, units, width):
        return pl.ds(pl.multiple_of(first * width, width), units * width)

    cut = int(deep * out_cut)

    def out_rows(f, late):
        return pl.ds(pl.multiple_of(f * deep + late * cut, 16), deep - cut if late else cut)

    views = (
        lambda f, first, units: attn.at[pl.ds(0, 3), part(f, thin), columns_of(first, units, unit)],
        lambda f, first, units: attn.at[pl.ds(3, 3), part(f, thin), columns_of(first, units, unit)],
        lambda f, first, units: attn.at[pl.ds(6, 2), part(f, thin), columns_of(first, units, unit)],
        lambda f, first, units: wide_in.at[part(f, thin), columns_of(first, units, unit_in)],
        lambda f, first, units: wide_out.at[out_rows(f, 0), columns_of(first, units, unit)],
        lambda f, first, units: wide_out.at[out_rows(f, 1), columns_of(first, units, unit)],
    )
    sizes = (0.75, 0.75, 0.5, 1.0, out_cut, 1.0 - out_cut)
    mine = part(index, thin)
    owned = (
        ((self_qkv, attn.at[pl.ds(0, 3), mine]),),
        ((self_out, attn.at[3, mine]), (cross_qkv, attn.at[pl.ds(4, 3), mine]), (cross_out, attn.at[7, mine])),
        ((ffn_in, wide_in.at[mine]),),
        ((ffn_out, wide_out.at[part(index, deep)]),),
    )
    loads = []
    for group in owned:
        for source, target in group:
            loads.append(pltpu.make_async_copy(source, target, own_sem.at[len(loads)]))
    for load in loads:
        load.start()
    load_tok = pltpu.make_async_copy(tokens, tok, load_sem.at[0])
    load_enc = pltpu.make_async_copy(encoder, held.at[7], load_sem.at[1])
    load_down = pltpu.make_async_copy(adapt_down, down, load_sem.at[2])
    load_up = pltpu.make_async_copy(adapt_up, up, load_sem.at[3])
    for load in (load_tok, load_enc, load_down, load_up):
        load.start()
    gather = Gather(count, views, sizes, send_sem, recv_sem)
    reduction = Reduction(
        count,
        copies,
        mass,
        inbox,
        sum_send_sem,
        sum_recv_sem,
        free_sem,
    )
    early = Exchange(count, copies, vectors, letters, post_sem, mail_sem)
    late = Exchange(count, copies, late_vectors, late_letters, late_post_sem, late_mail_sem)
    early.enter()
    loads[0].wait()
    gather.own(0)
    for load in loads[1:]:
        load.wait()
    kept = []

    def keep(source, target):
        copy = pltpu.make_async_copy(source, target, kept_sem.at[len(kept)])
        copy.start()
        kept.append(copy)
        return copy

    def project(source, target, weight, scale=None):
        for block in range(2):
            columns = pl.ds(block * (model // 2), model // 2)
            product = dot(source[...], attn[weight, :, columns]).astype(bf16)
            target[:, columns] = product if scale is None else product * scale
            gather.tick()

    def attention(query, key, value, mixed, saved, key_saved, probs_saved, causal):
        turned[0] = value[...].T
        gather.tick()
        turned[1] = (key[...] * bf16(0.125)).T
        gather.tick()
        keep(turned.at[1], key_saved)
        steps = gather.take(16)

        def out_copy(pair, slot):
            return pltpu.make_async_copy(probs.at[slot], probs_saved.at[pl.ds(pair * 2, 2)], probs_sem.at[slot])

        pairs = HEADS // 2

        @pl.loop(0, pairs)
        def _(pair):
            slot = pair % 2
            pl.when(pair >= 2)(lambda: out_copy(pair - 2, slot).wait())
            attend_pair(pair, query, key, turned.at[0], bias, probs.at[slot], mixed, causal)
            out_copy(pair, slot).start()
            for at in range(pairs):
                mine_now = steps[2 * at : 2 * at + 2]

                @pl.when(pair == at)
                def _():
                    for step in mine_now:
                        step()

        for pair in (pairs - 2, pairs - 1):
            out_copy(pair, pair % 2).wait()

    def probs_in(saved, pair):
        slot = pair % 2
        return pltpu.make_async_copy(saved.at[pl.ds(pair * 2, 2)], probs.at[slot], probs_sem.at[slot])

    place_masks(bias, shift[0], seq_lengths, True)
    load_tok.wait()
    gather.need(0)
    project(tok, held.at[0], 0, bf16(0.125))
    project(tok, held.at[1], 1)
    project(tok, held.at[2], 2)
    attention(held.at[0], held.at[1], held.at[2], held.at[3], self_kept, self_key_kept, self_probs, True)
    keep(held.at[pl.ds(0, 4)], self_kept)
    turned_out = kept[0]

    gather.need(1)
    block_rows = 128
    blocks = rows // block_rows
    for half in range(2):
        columns = pl.ds(half * (model // 2), model // 2)
        total[:, columns] = tok[:, columns].astype(f32) + dot(held[3], attn[3, :, columns])
        gather.tick()

    @pl.loop(0, blocks)
    def _(block):
        here = part(block, block_rows)
        normal_one, inverse_one = layer_stats(total[here, :])
        normal[here, :] = normal_one
        inverse[here, :] = jnp.broadcast_to(inverse_one, (block_rows, 128))
        low[here, :] = (normal_one * norm_gain[0:1, :] + norm_bias[0:1, :]).astype(bf16)

    normal_out = keep(normal, normal_kept)
    inverse_out = keep(inverse, inverse_kept)
    place_masks(bias, shift[0], enc_lengths, False)
    load_enc.wait()
    turned_out.wait()
    project(low, held.at[4], 4, bf16(0.125))
    project(held.at[7], held.at[5], 5)
    gather.need(2)
    project(held.at[7], held.at[6], 6)
    attention(held.at[4], held.at[5], held.at[6], held.at[7], cross_kept, cross_key_kept, cross_probs, False)
    keep(held.at[pl.ds(4, 4)], cross_kept)
    for half in range(2):
        columns = pl.ds(half * (model // 2), model // 2)
        first = normal[:, columns] * norm_gain[0:1, columns] + norm_bias[0:1, columns]
        total[:, columns] = first + dot(held[7], attn[7, :, columns])
        gather.tick()
    normal_out.wait()
    inverse_out.wait()

    @pl.loop(0, blocks)
    def _(block):
        here = part(block, block_rows)
        normal_two, inverse_two = layer_stats(total[here, :])
        normal[here, :] = normal_two
        inverse[here, :] = jnp.broadcast_to(inverse_two, (block_rows, 128))
        second = normal_two * norm_gain[1:2, :] + norm_bias[1:2, :]
        low[here, :] = second.astype(bf16)
        total[here, :] = second

    load_down.wait()
    load_up.wait()
    narrow = dot(low[...], down[...]) + down_bias[...]
    gate = 1.0 / (1.0 + jnp.exp(-narrow))
    narrow_act[...] = (narrow * gate).astype(bf16)
    narrow_slope[...] = (gate * (1.0 + narrow * (1.0 - gate))).astype(bf16)
    gather.tick()
    for half in range(2):
        columns = pl.ds(half * (model // 2), model // 2)
        branch = dot(narrow_act[...], up[:, columns]) + up_bias[:, columns]
        total[:, columns] += branch_scale * branch
        gather.tick()

    for copy in kept:
        if copy is not normal_out and copy is not inverse_out and copy is not turned_out:
            copy.wait()
    load_cots = [
        pltpu.make_async_copy(
            cotangent.at[:, pl.ds(half * (model // 2), model // 2)],
            turned.at[half, pl.ds(0, rows)],
            load_sem.at[half],
        )
        for half in range(2)
    ]
    for load in load_cots:
        load.start()
    gather.need(3)
    gather.finish((0, 1))
    tile = model // 2
    act, slope = held.at[pl.ds(0, 4)], held.at[pl.ds(4, 4)]
    for block in range(hidden // tile):
        at, columns = block // 2, pl.ds((block % 2) * tile, tile)
        inner = dot(low[...], wide_in[:, pl.ds(block * tile, tile)])
        active, slant = gelu_both(inner)
        act[at, :, columns] = active.astype(bf16)
        slope[at, :, columns] = slant.astype(bf16)
        gather.tick(2)
    for phase in (4, 5):
        offset, piece = (0, cut) if phase == 4 else (cut, deep - cut)
        gather.finish((phase - 2,))
        for chip in gather.chips(phase):
            if cut % 128:
                if phase == 4:
                    continue
                offset, piece = 0, deep
            actives, weights = [], []
            for core in range(2):
                first = pl.multiple_of((2 * chip + core) * deep, deep)
                columns = pl.ds(pl.multiple_of(first % model + offset, 128), piece)
                actives.append(act[first // model, :, columns])
                weights.append(wide_out[pl.ds(pl.multiple_of(first + offset, 64), piece), :])
            active, weight = jnp.concatenate(actives, 1), jnp.concatenate(weights, 0)
            for half in range(2):
                total[:, pl.ds(half * tile, tile)] += dot(active, weight[:, half * tile : (half + 1) * tile])
    for load in load_cots:
        load.wait()
    feed_grad = tok
    for name in range(8):
        vectors[0, name : name + 1, :] = jnp.zeros((1, model), f32)

    @pl.loop(0, blocks)
    def _(block):
        here = part(block, block_rows)
        normal_three, inverse_three = layer_stats(total[here, :])
        mass[part(block + blocks, block_rows), :] = (
            normal_three * norm_gain[2:3, :] + norm_bias[2:3, :]
        ).astype(bf16)
        low_grad = jnp.concatenate([turned[0, here, :], turned[1, here, :]], 1).astype(f32)
        grad_three = norm_back(low_grad, normal_three, inverse_three, norm_gain[2:3, :])
        total[here, :] = grad_three
        tok[here, :] = grad_three.astype(bf16)
        scaled = (branch_scale * grad_three).astype(bf16)
        turned[0, here, :] = scaled[:, : model // 2]
        turned[1, here, :] = scaled[:, model // 2 :]
        vectors[0, 2:3, :] += jnp.sum(low_grad * normal_three, 0, keepdims=True)
        vectors[0, 5:6, :] += jnp.sum(low_grad, 0, keepdims=True)
        vectors[0, 6:7, :] += jnp.sum(scaled.astype(f32), 0, keepdims=True)

    out_copy = pltpu.make_async_copy(mass.at[pl.ds(rows, rows)], output, load_sem.at[2])
    out_copy.start()
    adapt = narrow_act.shape[1]
    for half in range(2):
        columns = pl.ds(half * tile, tile)
        mass[pl.ds(0, adapt), columns] = t_dot(narrow_act[...], turned[half, :rows, :]).astype(bf16)
    grown = sum(dot_t(turned[half, :rows, :], up[:, pl.ds(half * tile, tile)]) for half in range(2))
    small = grown * narrow_slope[...].astype(f32)
    narrow_grad = narrow_act
    narrow_grad[...] = small.astype(bf16)
    vectors[0, 7:8, :adapt] = jnp.sum(narrow_grad[...].astype(f32), 0, keepdims=True)
    lowered = t_dot(low[...], narrow_grad[...]).astype(bf16)
    out_copy.wait()
    for at in range(model // adapt):
        mass[pl.ds(adapt, adapt), pl.ds(at * adapt, adapt)] = lowered[at * adapt : (at + 1) * adapt]
    reduction.tick()
    for pair in range(2):
        probs_in(cross_probs, pair).start()
    for at in range(hidden // model):
        for half in range(2):
            columns = pl.ds(half * tile, tile)
            grown = dot_t(feed_grad[...], wide_out[pl.ds(at * model + half * tile, tile), :])
            act[at, :, columns] = (grown * slope[at, :, columns].astype(f32)).astype(bf16)
        if at == 2:
            reduction.tick()
    gather.finish((4, 5))
    old = {}

    def back(name, source, target):
        old[name] = pltpu.make_async_copy(source, target, back_sem.at[len(old)])
        old[name].start()

    def tile_out(at):
        return wide_out.at[pl.ds(at * rows, rows)]

    back("joined", cross_kept.at[3], tile_out(3))
    back("cross_value", cross_kept.at[2], tile_out(2))
    back("cross_query", cross_kept.at[0], tile_out(0))
    back("mixed", self_kept.at[3], tile_out(7))
    back("self_value", self_kept.at[2], tile_out(6))
    back("self_query", self_kept.at[0], tile_out(4))
    for half in range(2):
        columns = pl.ds(half * tile, tile)
        second_grad = total[:, columns] + dot_t(narrow_grad[...], down[columns, :])
        for at in range(hidden // model):
            second_grad += dot_t(act[at], wide_in[columns, pl.ds(at * model, model)])
        total[:, columns] = second_grad
    reduction.tick()
    back("cross_key", cross_key_kept, wide_in.at[:, pl.ds(0, rows)])
    back("self_key", self_key_kept, wide_in.at[:, pl.ds(rows, rows)])

    @pl.loop(0, blocks)
    def _(block):
        here = part(block, block_rows)
        grad_second = total[here, :]
        normal_two = normal[here, :]
        vectors[0, 1:2, :] += jnp.sum(grad_second * normal_two, 0, keepdims=True)
        vectors[0, 4:5, :] += jnp.sum(grad_second, 0, keepdims=True)
        grad_two = norm_back(grad_second, normal_two, inverse[here, 0:1], norm_gain[1:2, :])
        total[here, :] = grad_two
        low[here, :] = grad_two.astype(bf16)

    early.tick()
    back("normal", normal_kept, normal)
    back("inverse", inverse_kept, inverse)
    grad, grad_query = held.at[0], held.at[1]

    def attention_back(probs_saved, base, key_t, weight, causal, names, grads, ticks):
        for half in range(2):
            columns = pl.ds(half * tile, tile)
            grad[:, columns] = dot_t(low[...], attn[weight, columns, :]).astype(bf16)
        for name in names:
            old[name].wait()
        head = lax.broadcasted_iota(jnp.int32, (HEADS, model), 0)
        lane = lax.broadcasted_iota(jnp.int32, (HEADS, model), 1)
        chosen = (lane // 64 == head).astype(bf16)
        product = grad[...].astype(f32) * tile_out(base + 3)[...].astype(f32)
        rough = product.astype(bf16)
        fine = (product - rough.astype(f32)).astype(bf16)
        delta[...] = dot_t(chosen, rough) + dot_t(chosen, fine)
        pairs = HEADS // 2

        @pl.loop(0, pairs)
        def _(pair):
            slot = pair % 2
            probs_in(probs_saved, pair).wait()
            back_pair(
                pair,
                tile_out(base),
                key_t,
                tile_out(base + 2),
                grad,
                probs.at[slot],
                delta,
                *grads,
                causal,
            )

            @pl.when(pair + 2 < pairs)
            def _():
                probs_in(probs_saved, pair + 2).start()

            for at, tick in ticks:
                pl.when(pair == at)(functools.partial(tick))

    attention_back(
        cross_probs,
        0,
        wide_in.at[:, pl.ds(0, rows)],
        7,
        False,
        ("joined", "cross_value", "cross_query", "cross_key"),
        (grad_query, held.at[2], held.at[3]),
        (
            (0, reduction.tick),
            (1, early.tick),
            (2, reduction.tick),
            (4, reduction.tick),
            (5, early.tick),
            (6, reduction.tick),
        ),
    )
    for pair in range(2):
        probs_in(self_probs, pair).start()
    for half in range(2):
        columns = pl.ds(half * tile, tile)
        total[:, columns] += dot_t(grad_query[...], attn[4, columns, :])
    reduction.tick()
    for name in ("normal", "inverse"):
        old[name].wait()
    late_vectors[0] = jnp.zeros(late_vectors.shape[1:], f32)

    @pl.loop(0, blocks)
    def _(block):
        here = part(block, block_rows)
        grad_first = total[here, :]
        normal_one = normal[here, :]
        gain_one = jnp.sum(grad_first * normal_one, 0, keepdims=True)
        bias_one = jnp.sum(grad_first, 0, keepdims=True)
        for at in range(4):
            columns = slice(at * (model // 4), (at + 1) * (model // 4))
            late_vectors[0, at : at + 1, :] += gain_one[:, columns]
            late_vectors[0, 4 + at : 5 + at, :] += bias_one[:, columns]
        grad_one = norm_back(grad_first, normal_one, inverse[here, 0:1], norm_gain[0:1, :])
        total[here, :] = grad_one
        low[here, :] = grad_one.astype(bf16)

    late.tick()

    attention_back(
        self_probs,
        4,
        wide_in.at[:, pl.ds(rows, rows)],
        3,
        True,
        ("mixed", "self_value", "self_query", "self_key"),
        tuple(held.at[at] for at in (4, 5, 6)),
        ((0, reduction.tick), (1, late.tick), (5, late.tick), (7, reduction.tick)),
    )
    for half in range(2):
        columns = pl.ds(half * tile, tile)
        gathered = dot_t(held[2], attn[5, columns, :]) + dot_t(held[3], attn[6, columns, :])
        held[7, :, columns] = gathered.astype(bf16)
    back("encoder", held.at[7], grad_encoder)
    early.tick(99)
    late.tick(99)
    stages = len(early.groups)
    for at in range(4):
        columns = pl.ds(at * (model // 4), model // 4)
        vectors[stages, 0:1, columns] = late_vectors[stages, at : at + 1, :]
        vectors[stages, 3:4, columns] = late_vectors[stages, 4 + at : 5 + at, :]
    back("vectors", vectors.at[stages], vector_sums)
    for half in range(2):
        columns = pl.ds(half * tile, tile)
        gathered = total[:, columns]
        for at in range(3):
            gathered += dot_t(held[4 + at], attn[at, columns, :])
        low[:, columns] = gathered.astype(bf16)
    back("tokens", low, grad_tokens)
    reduction.tick(99)
    back("sums", mass, adapt_sums)
    reduction.finish()
    for name in ("encoder", "tokens", "sums", "vectors"):
        old[name].wait()


def layer(count, copies, *args):
    tokens, ffn_in, adapt_down = args[0], args[7], args[9]
    rows, model = tokens.shape
    hidden, adapt = ffn_in.shape[1], adapt_down.shape[1]
    bits = (count * copies).bit_length() - 1
    letters, stages = letters_of(count, copies), len(exchange_groups(count, copies))
    shape = jax.ShapeDtypeStruct
    return pl.pallas_call(
        functools.partial(layer_kernel, count, copies),
        out_shape=[
            shape((rows, model), bf16),
            shape((4, rows, model), bf16),
            shape((model, rows), bf16),
            shape((HEADS, rows, rows), bf16),
            shape((4, rows, model), bf16),
            shape((model, rows), bf16),
            shape((HEADS, rows, rows), bf16),
            shape((rows, model), f32),
            shape((rows, 128), f32),
            shape((rows, model), bf16),
            shape((rows, model), bf16),
            shape((2 * adapt, model), bf16),
            shape((8, model), f32),
        ],
        in_specs=[ANY] * 10
        + [pl.BlockSpec(memory_space=pltpu.VMEM), ANY]
        + [pl.BlockSpec(memory_space=pltpu.VMEM)] * 3
        + [SMEM] * 3,
        out_specs=[ANY] * 13,
        scratch_shapes=[
            pltpu.VMEM((2 * adapt, model), bf16),
            pltpu.VMEM((2 * box_rows(adapt, bits), model), bf16),
            pltpu.VMEM((letters, 8, model), f32),
            pltpu.VMEM((stages + 1, 8, model), f32),
            pltpu.VMEM((letters, 8, model // 4), f32),
            pltpu.VMEM((stages + 1, 8, model // 4), f32),
            pltpu.VMEM((8, model, model), bf16),
            pltpu.VMEM((model, hidden), bf16),
            pltpu.VMEM((hidden, model), bf16),
            pltpu.VMEM((8, rows, model), bf16),
            pltpu.VMEM((2, model, rows), bf16),
            pltpu.VMEM((rows, model), bf16),
            pltpu.VMEM((rows, model), bf16),
            pltpu.VMEM((rows, rows), bf16),
            pltpu.VMEM((2, 2, rows, rows), bf16),
            pltpu.VMEM((rows, model), f32),
            pltpu.VMEM((rows, model), f32),
            pltpu.VMEM((rows, 128), f32),
            pltpu.VMEM((rows, adapt), bf16),
            pltpu.VMEM((rows, adapt), bf16),
            pltpu.VMEM((model, adapt), bf16),
            pltpu.VMEM((adapt, model), bf16),
            pltpu.VMEM((HEADS, rows), f32),
            pltpu.SemaphoreType.DMA((6, sends_per_phase(count))),
            pltpu.SemaphoreType.DMA((6, 2, count // 2, 4)),
            pltpu.SemaphoreType.DMA((6,)),
            pltpu.SemaphoreType.DMA((4,)),
            pltpu.SemaphoreType.DMA((10,)),
            pltpu.SemaphoreType.DMA((2,)),
            pltpu.SemaphoreType.DMA((16,)),
            pltpu.SemaphoreType.DMA((4 * bits,)),
            pltpu.SemaphoreType.DMA((4 * bits,)),
            pltpu.SemaphoreType.REGULAR((2 * bits,)),
            pltpu.SemaphoreType.DMA((letters,)),
            pltpu.SemaphoreType.DMA((letters,)),
            pltpu.SemaphoreType.DMA((letters,)),
            pltpu.SemaphoreType.DMA((letters,)),
        ],
        compiler_params=pltpu.CompilerParams(
            collective_id=0, has_side_effects=True, vmem_limit_bytes=63 * 2**20
        ),
        name="decoder_layer",
    )(*args)


def results_kernel(
    output,
    grad_encoder,
    grad_tokens,
    adapt_sums,
    vector_sums,
    output_out,
    tokens_out,
    encoder_out,
    down_out,
    down_bias_out,
    up_out,
    up_bias_out,
    gain_out,
    bias_out,
    passed,
    sums,
    down,
    up,
    sem,
    out_sem,
):
    adapt, model = up.shape
    pieces = ((output, output_out), (grad_encoder, encoder_out), (grad_tokens, tokens_out))
    loads = [pltpu.make_async_copy(adapt_sums, sums, sem.at[0])]
    for at, (source, _) in enumerate(pieces):
        loads.append(pltpu.make_async_copy(source, passed.at[at], sem.at[at + 1]))
    for load in loads:
        load.start()
    outs = []

    def put(source, target):
        outs.append(pltpu.make_async_copy(source, target, out_sem.at[len(outs)]))
        outs[-1].start()

    for at, out in ((0, gain_out), (3, bias_out)):
        out[...] = vector_sums[at : at + 3, :]
    up_bias_out[...] = vector_sums[6, :]
    down_bias_out[...] = vector_sums[7, :adapt]
    loads[0].wait()
    up[...] = sums[:adapt, :].astype(f32)
    put(up, up_out)
    for at in range(model // adapt):
        down[pl.ds(at * adapt, adapt), :] = sums[pl.ds(adapt, adapt), pl.ds(at * adapt, adapt)].astype(f32)
    put(down, down_out)
    for at, (_, target) in enumerate(pieces):
        loads[at + 1].wait()
        put(passed.at[at], target)
    for copy in outs:
        copy.wait()


def results(adapt, output, grad_encoder, grad_tokens, adapt_sums, vector_sums):
    rows, model = output.shape
    shape = jax.ShapeDtypeStruct
    inside = pl.BlockSpec(memory_space=pltpu.VMEM)
    return pl.pallas_call(
        results_kernel,
        out_shape=[
            shape((rows, model), bf16),
            shape((rows, model), bf16),
            shape((rows, model), bf16),
            shape((model, adapt), f32),
            shape((adapt,), f32),
            shape((adapt, model), f32),
            shape((model,), f32),
            shape((3, model), f32),
            shape((3, model), f32),
        ],
        in_specs=[ANY] * 4 + [inside],
        out_specs=[ANY] * 4 + [inside, ANY] + [inside] * 3,
        scratch_shapes=[
            pltpu.VMEM((3, rows, model), bf16),
            pltpu.VMEM((2 * adapt, model), bf16),
            pltpu.VMEM((model, adapt), f32),
            pltpu.VMEM((adapt, model), f32),
            pltpu.SemaphoreType.DMA((4,)),
            pltpu.SemaphoreType.DMA((5,)),
        ],
        compiler_params=pltpu.CompilerParams(vmem_limit_bytes=63 * 2**20),
        name="write_results",
    )(output, grad_encoder, grad_tokens, adapt_sums, vector_sums)


def local(*args):
    count, copies = lax.axis_size("fsdp"), lax.axis_size("dp")
    args = list(args)
    adapt = args[10].shape[0]
    args[10], args[12] = args[10][None], args[12][None]
    kept = layer(count, copies, *args)
    return tuple(results(adapt, kept[0], *kept[9:]))


def solution(mesh):
    rows = P(("fsdp", "dp"), None)
    placed = (
        (rows,) * 3
        + (P(None, "fsdp", None), P("fsdp", None)) * 2
        + (P("fsdp", None),) * 2
        + (P(),) * 6
        + (P(("fsdp", "dp")), rows, rows)
    )
    return jax.shard_map(
        local, mesh=mesh, in_specs=placed, out_specs=(rows,) * 3 + (P(),) * 6, check_vma=False
    )
```

```python
import functools

import jax
import jax.numpy as jnp
from jax import lax
from jax.experimental import pallas as pl
from jax.experimental.pallas import tpu as pltpu
from jax.sharding import PartitionSpec as P

HEADS = 16
STEP = 12
LINE = 4
MESH = pl.DeviceIdType.MESH
ANY = pl.BlockSpec(memory_space=pl.ANY)
SMEM = pl.BlockSpec(memory_space=pltpu.SMEM)
bf16 = jnp.bfloat16
f32 = jnp.float32

epsilon = 1e-05
ramp_steps = 4.0
masked_score = -1e30
lead = 1.0
even_phases = (0, 1)
x_slack = 0.5
plane_slack = 0.5
out_cut = 0.5


def dot(left, right):
    return jnp.dot(left, right, preferred_element_type=f32)


def dot_t(left, right):
    return lax.dot_general(left, right, (((1,), (1,)), ((), ())), preferred_element_type=f32)


def t_dot(left, right):
    return lax.dot_general(left, right, (((0,), (0,)), ((), ())), preferred_element_type=f32)


def part(index, size):
    return pl.ds(pl.multiple_of(index * size, size), size)


def layer_stats(values_in):
    average = jnp.mean(values_in, -1, keepdims=True)
    centred = values_in - average
    inverse = lax.rsqrt(jnp.mean(centred * centred, -1, keepdims=True) + epsilon)
    return (centred * inverse, inverse)


def norm_back(grad_out, normal, inverse, norm_scale):
    grad_normal = grad_out * norm_scale
    return inverse * (
        grad_normal
        - jnp.mean(grad_normal, -1, keepdims=True)
        - normal * jnp.mean(grad_normal * normal, -1, keepdims=True)
    )


def nearest(place, count, rank):
    under, over = place, count - 1 - place
    both = jnp.minimum(under, over)
    side = jnp.where(under > over, -1, 1)
    paired = place + (side * ((rank + 1) // 2) if rank % 2 == 1 else -side * (rank // 2))
    alone = jnp.where(over > under, place + rank - both, place - (rank - both))
    return jnp.where(rank <= 2 * both, paired, alone)


def mesh_shape(count):
    line = min(LINE, count // 2)
    return line, count // (2 * line)


def sends_per_phase(count):
    line, wide = mesh_shape(count)
    across = 1 if wide == 2 else 2
    each = 2 * (2 + across) + 1
    return line * each + (wide - 1) * line * 2 * (1 + across) + (line - 1) + (wide - 1) * line * 2


class Gather:
    def __init__(self, count, views, sizes, send_sem, recv_sem):
        self.views, self.sizes, self.send_sem, self.recv_sem = views, sizes, send_sem, recv_sem
        self.line, self.wide = mesh_shape(count)
        index = lax.axis_index("fsdp")
        self.dp = lax.axis_index("dp")
        self.core = index % 2
        self.x = (index // 2) % self.wide
        self.z = index // (2 * self.wide)
        p = self.dp % 2
        self.other_core = (self.place(self.z, self.x, 1 - self.core), self.dp)
        self.other_plane = (index, self.dp + 1 - 2 * p)
        self.same = ((2 * p, 2), (4, 4), (2 - 2 * p, 2))
        uneven = ((2 * p, 2), (4 + p, 3), (2 - 2 * p, 2), (7 - 3 * p, 1))
        even = ((2 * p, 2), (4 + 2 * p, 2), (2 - 2 * p, 2), (6 - 2 * p, 2))
        self.cross = [even if phase in even_phases else uneven for phase in range(len(views))]
        self.single = [(4 + 2 * p, 2) if phase in even_phases else (4 + 3 * p, 1) for phase in range(len(views))]
        self.z_up = (self.along_z(1), self.z < self.line - 1)
        self.z_down = (self.along_z(-1), self.z > 0)
        if self.wide == 2:
            self.x_ways = ((self.along_x(1 - 2 * self.x), None),)
        else:
            self.x_ways = ((self.along_x(1), self.x < self.wide - 1), (self.along_x(-1), self.x > 0))
        self.sends = {}
        self.counts = [0] * len(views)
        self.steps = self.plan()
        self.done = 0

    def place(self, z, x, core):
        return (z * self.wide + x) * 2 + core

    def along_z(self, step):
        return (self.place(self.z + step, self.x, self.core), self.dp)

    def along_x(self, step):
        return (self.place(self.z, self.x + step, self.core), self.dp)

    def copy(self, at, kind, span, slot, target):
        phase, core, z, x = at
        view = self.views[phase](self.place(z, x, core), *span)
        return pltpu.make_async_remote_copy(
            src_ref=view,
            dst_ref=view,
            send_sem=self.send_sem.at[phase, slot],
            recv_sem=self.recv_sem.at[phase, core, z * self.wide + x, kind],
            device_id=target,
            device_id_type=MESH,
        )

    def send(self, at, kind, span, target, when=None):
        slot = self.counts[at[0]]
        self.counts[at[0]] += 1
        remake = functools.partial(self.copy, at, kind, span, slot, target)
        if when is None:
            remake().start()
        else:
            pl.when(when)(lambda: remake().start())
        self.sends[at[0], slot] = (remake, when)

    def arrive(self, at, kind, span):
        phase, core, z, x = at
        view = self.views[phase](self.place(z, x, core), *span)
        pltpu.make_async_copy(view, view, self.recv_sem.at[phase, core, z * self.wide + x, kind]).wait()

    def plan(self):
        span = self.line - 1
        steps = []
        for phase in range(len(self.views)):
            base, size = span * sum(self.sizes[:phase]), self.sizes[phase]

            def add(when, slack, makers, chip):
                steps.extend((base + size * when + slack, phase, maker, chip) for maker in makers)

            for far in range(self.line):
                z_from = nearest(self.z, self.line, far)
                if far:
                    add(far, 0.0, self.from_z((phase, self.core, z_from, self.x)), (far, 0))
                    add(far + 1, plane_slack, self.from_plane((phase, self.core, z_from, self.x), self.same), (far, 0))
                for apart in range(1, self.wide):
                    at = (phase, self.core, z_from, nearest(self.x, self.wide, apart))
                    add(far + apart, x_slack, self.from_x(at), (far, apart))
                    add(far + apart + 1, x_slack + plane_slack, self.from_plane(at, self.cross[phase]), (far, apart))
            if phase:
                steps.append((base - lead, phase, functools.partial(self.own, phase), None))
        return sorted(steps, key=lambda item: item[0])

    def own(self, phase):
        at = (phase, self.core, self.z, self.x)
        for kind in (0, 1):
            self.send(at, kind, self.same[kind], *self.z_up)
            self.send(at, kind, self.same[kind], *self.z_down)
            self.over_x(at, kind)
        self.send(at, 0, (0, 8), self.other_core)

    def over_x(self, at, kind):
        for way in self.x_ways:
            self.send(at, kind, self.cross[at[0]][kind], *way)

    def from_z(self, at):
        upward = at[2] < self.z
        onward = (upward & self.z_up[1]) | (~upward & self.z_down[1])
        target = self.along_z(jnp.where(upward, 1, -1))

        def step(kind):
            self.arrive(at, kind, self.same[kind])
            self.send(at, kind, self.same[kind], target, onward)
            self.over_x(at, kind)
            if kind == 0:
                self.send(at, 2, self.same[0], self.other_plane)
            self.send(at, kind, self.same[kind], self.other_core)

        return [functools.partial(step, 0), functools.partial(step, 1)]

    def from_x(self, at):
        cross = self.cross[at[0]]
        upward = at[3] < self.x
        onward = (upward & (self.x < self.wide - 1)) | (~upward & (self.x > 0))
        target = self.along_x(jnp.where(upward, 1, -1))

        def step(kind):
            self.arrive(at, kind, cross[kind])
            if self.wide > 2:
                self.send(at, kind, cross[kind], target, onward)
            self.send(at, kind + 2, cross[0] if kind == 0 else self.single[at[0]], self.other_plane)
            self.send(at, kind, cross[kind], self.other_core)

        return [functools.partial(step, 0), functools.partial(step, 1)]

    def from_plane(self, at, spans):
        def step():
            for kind in range(2, len(spans)):
                self.arrive(at, kind, spans[kind])
                self.send(at, kind, spans[kind], self.other_core)

        return [step]

    def tick(self, many=1):
        for _ in range(many):
            if self.done < len(self.steps):
                self.done += 1
                self.steps[self.done - 1][2]()

    def take(self, many):
        first = self.done
        self.done = min(len(self.steps), first + many)
        return [step[2] for step in self.steps[first : self.done]]

    def need(self, phase):
        last = max(i for i, step in enumerate(self.steps) if step[1] == phase)
        self.tick(last + 1 - self.done)
        for z in range(self.line):
            for x in range(self.wide):
                self.other_half(phase, z, x)

    def chips(self, phase):
        for far in range(self.line):
            for apart in range(self.wide):
                own = [i for i, step in enumerate(self.steps) if step[1] == phase and step[3] == (far, apart)]
                self.tick(max(own, default=-1) + 1 - self.done)
                z, x = nearest(self.z, self.line, far), nearest(self.x, self.wide, apart)
                self.other_half(phase, z, x)
                yield self.place(z, x, 0) // 2

    def other_half(self, phase, z, x):
        at = (phase, 1 - self.core, z, x)

        def pieces(spans):
            for kind, span in enumerate(spans):
                self.arrive(at, kind, span)

        own_chip = (z == self.z) & (x == self.x)
        pl.when(own_chip)(lambda: self.arrive(at, 0, (0, 8)))
        pl.when((x == self.x) & (z != self.z))(lambda: pieces(self.same))
        pl.when(x != self.x)(lambda: pieces(self.cross[phase]))

    def finish(self, phases):
        for key in [key for key in self.sends if key[0] in phases]:
            remake, when = self.sends.pop(key)
            if when is None:
                remake().wait_send()
            else:
                pl.when(when)(lambda: remake().wait_send())


def place_masks(bias, shift, lengths, causal):
    rows = bias.shape[0]
    wide = 128
    bits = shift + (rows // 4).bit_length() - 1

    @pl.loop(0, rows // wide)
    def _(block):
        shape = (wide, rows)
        key = lax.broadcasted_iota(jnp.int32, shape, 0) + block * wide
        query = lax.broadcasted_iota(jnp.int32, shape, 1)
        key_seq = lax.shift_right_logical(key, jnp.full(shape, bits, jnp.int32))
        query_seq = lax.shift_right_logical(query, jnp.full(shape, bits, jnp.int32))
        start = lax.shift_left(key_seq, jnp.full(shape, bits, jnp.int32))
        length = jnp.zeros(shape, jnp.int32)
        for slot in range(4):
            length = jnp.where(key_seq == slot, lengths[0, slot], length)
        allowed = (key_seq == query_seq) & (key - start < length)
        if causal:
            allowed = allowed & (key <= query)
        bias[part(block, wide), :] = jnp.where(allowed, 0.0, masked_score).astype(bf16)


def tiles_of(rows, causal):
    half = rows // 2
    return ((0, half, half), (half, half, rows)) if causal else ((0, rows, rows),)


def head_lanes(values, half):
    lane = lax.broadcasted_iota(jnp.int32, values.shape, 1)
    return jnp.where((lane // 64) == half, values, jnp.zeros_like(values))


def attend_pair(pair, query, key, value_t, bias, probs, out, causal):
    rows = query.shape[0]
    columns = part(pair, 128)
    keys = key[:, columns]
    queries = query[:, columns]
    halves = []
    for half in range(2):
        head_queries = head_lanes(queries, half)
        lanes = pl.ds(pl.multiple_of(pair * 128 + half * 64, 64), 64)
        pieces = []
        for first, many, deep in tiles_of(rows, causal):
            scores = dot_t(keys[:deep], head_queries[first : first + many])
            scores = scores + bias[:deep, first : first + many].astype(f32)
            expanded = jnp.exp(scores - jnp.max(scores, 0, keepdims=True))
            total = jnp.sum(expanded, 0, keepdims=True)
            block = (expanded * (1.0 / total)).astype(bf16)
            probs[half, :deep, first : first + many] = block
            pieces.append(dot(value_t[lanes, :deep], block))
        halves.append(jnp.concatenate(pieces, 1) if len(pieces) > 1 else pieces[0])
    both = jnp.concatenate(halves, 0).astype(bf16)
    out[:, columns] = both.T


def gelu_both(inner):
    spread = 0.5 + 0.5 * lax.erf(inner * (0.5**0.5))
    bell = jnp.exp(inner * inner * -0.5) * 0.3989422804014327
    return inner * spread, spread + inner * bell


def exchange_groups(count, copies):
    line, wide = mesh_shape(count)
    groups, size = [[]], 1
    for name, long in (("core", 2), ("x", wide), ("dp", copies), ("z", line)):
        if size * long > 8:
            groups.append([])
            size = 1
        groups[-1].append(name)
        size *= long
    return groups


def letters_of(count, copies):
    line, wide = mesh_shape(count)
    sizes = {"core": 2, "x": wide, "dp": copies, "z": line}
    found = 0
    for names in exchange_groups(count, copies):
        size = 1
        for name in names:
            size *= sizes[name]
        found += size
    return found


def reduction_sizes(count, copies):
    line, wide = mesh_shape(count)
    return [2] * ((count * copies // line).bit_length() - 1) + [line]


def slots_of(count, copies):
    return sum(size - 1 for size in reduction_sizes(count, copies))


def box_rows(height, count, copies):
    rows = 0
    for size in reduction_sizes(count, copies):
        height = height // size if height >= 16 * size else height
        rows += (size - 1) * height
    return rows


class Exchange:
    def __init__(self, count, copies, held, letters, send_sem, recv_sem):
        self.held, self.letters, self.send_sem, self.recv_sem = held, letters, send_sem, recv_sem
        line, wide = mesh_shape(count)
        index, dp = lax.axis_index("fsdp"), lax.axis_index("dp")
        places = {
            "core": (index % 2, 2),
            "x": ((index // 2) % wide, wide),
            "dp": (dp, copies),
            "z": (index // (2 * wide), line),
        }
        self.groups, self.ranks = [], []
        for names in exchange_groups(count, copies):
            size = 1
            rank = 0
            for name in names:
                rank = rank + places[name][0] * size
                size *= places[name][1]
            targets = []
            for ahead in range(1, size):
                other = (rank + ahead) % size
                at = {name: place for name, (place, _) in places.items()}
                for name in names:
                    at[name] = other % places[name][1]
                    other = other // places[name][1]
                targets.append(((at["z"] * wide + at["x"]) * 2 + at["core"], at["dp"]))
            self.groups.append(targets)
            self.ranks.append(rank)
        self.targets = [target for group in self.groups for target in group]
        last = len(self.groups) - 1
        self.steps = [[functools.partial(self.send, 0)]]
        for stage in range(last):
            self.steps.append([functools.partial(self.add, stage), functools.partial(self.send, stage + 1)])
        self.steps.append([functools.partial(self.add, last)])

    def enter(self):
        barrier = pltpu.get_barrier_semaphore()
        for target in self.targets:
            pl.semaphore_signal(barrier, inc=1, device_id=target, device_id_type=MESH)
        pl.semaphore_wait(barrier, len(self.targets))

    def first(self, stage):
        return sum(len(group) + 1 for group in self.groups[:stage])

    def copies_of(self, stage):
        first = self.first(stage)
        for at, target in enumerate(self.groups[stage]):
            yield pltpu.make_async_remote_copy(
                src_ref=self.held.at[stage],
                dst_ref=self.letters.at[first + self.ranks[stage]],
                send_sem=self.send_sem.at[first + at],
                recv_sem=self.recv_sem.at[first + at],
                device_id=target,
                device_id_type=MESH,
            )

    def send(self, stage):
        for copy in self.copies_of(stage):
            copy.start()
        self.letters[self.first(stage) + self.ranks[stage]] = self.held[stage]

    def add(self, stage):
        for copy in self.copies_of(stage):
            copy.wait_send()
        first, size = self.first(stage), len(self.groups[stage]) + 1
        for ahead in range(1, size):
            box = self.letters.at[first + (self.ranks[stage] - ahead + size) % size]
            pltpu.make_async_copy(box, box, self.recv_sem.at[first + ahead - 1]).wait()
        total = self.letters[first]
        for at in range(1, size):
            total = total + self.letters[first + at]
        self.held[stage + 1] = total

    def tick(self, many=1):
        for _ in range(min(many, len(self.steps))):
            for step in self.steps.pop(0):
                step()


class Reduction:
    def __init__(self, count, copies, mass, inbox, send_sem, recv_sem, free_sem):
        self.mass, self.inbox, self.free_sem = mass, inbox, free_sem
        self.send_sem, self.recv_sem = send_sem, recv_sem
        line, wide = mesh_shape(count)
        index, dp = lax.axis_index("fsdp"), lax.axis_index("dp")

        def bits_of(coordinate, size, move):
            found, step = [], 1
            while step < size:
                bit = (coordinate // step) % 2
                found.append((2, bit, (move((1 - 2 * bit) * step),)))
                step *= 2
            return found

        def whole_line(coordinate, size, move):
            ahead = [(coordinate + by) % size - coordinate for by in range(1, size)]
            return [(size, coordinate, tuple(move(by) for by in ahead))]

        core = bits_of(index % 2, 2, lambda by: (index + by, dp))
        x = bits_of((index // 2) % wide, wide, lambda by: (index + 2 * by, dp))
        z = whole_line(index // (2 * wide), line, lambda by: (index + 2 * wide * by, dp))
        planes = bits_of(dp, copies, lambda by: (index, dp + by))
        self.orders = (core + x + planes + z, core + planes + x + z)
        self.count = len(self.orders[0])
        self.sends = []
        self.parts = []
        height, width = mass.shape[0] // len(self.orders), mass.shape[1]
        for at, order in enumerate(self.orders):
            first, high, left, broad = at * height, height, 0, width
            box, slot = at * box_rows(height, count, copies), at * slots_of(count, copies)
            steps = []
            for size, rank, targets in order:
                tall = high >= 16 * size
                high, broad = (high // size, broad) if tall else (high, broad // size)

                def region(place, first=first, left=left, high=high, broad=broad, tall=tall):
                    if tall:
                        return (first + place * high, high, left, broad)
                    return (first, high, left + place * broad, broad)

                exchanges = []
                for by, target in enumerate(targets, 1):
                    exchanges.append((target, region((rank + by) % size), region((rank - by + size) % size), box, slot))
                    box += high
                    slot += 1
                steps.append((region(rank), exchanges))
                first, left = region(rank)[0], region(rank)[2]
            self.parts.append(steps)
        self.slots = len(self.orders) * slots_of(count, copies)
        last = self.count - 1
        self.steps = [functools.partial(self.scatter, 0)]
        for step in range(last):
            self.steps.append(functools.partial(self.turn, (self.add, step), (self.scatter, step + 1)))
        self.steps.append(functools.partial(self.turn, (self.add, last), (self.spread, last)))
        for step in range(last, 0, -1):
            self.steps.append(functools.partial(self.turn, (self.landed, step), (self.spread, step - 1)))
        self.steps.append(functools.partial(self.landed, 0))

    def turn(self, one, other):
        one[0](one[1])
        other[0](other[1])

    def tick(self, many=1):
        for _ in range(min(many, len(self.steps))):
            self.steps.pop(0)()

    def remote(self, source, target_ref, sems, slot, target):
        return pltpu.make_async_remote_copy(
            src_ref=source,
            dst_ref=target_ref,
            send_sem=sems[0].at[slot],
            recv_sem=sems[1].at[slot],
            device_id=target,
            device_id_type=MESH,
        )

    def view(self, region):
        first, high, left, broad = region
        return self.mass.at[
            pl.ds(pl.multiple_of(first, 16), high), pl.ds(pl.multiple_of(left, 128), broad)
        ]

    def box(self, kept, row):
        return self.inbox.at[pl.ds(row, kept[1]), pl.ds(0, kept[3])]

    def scatter_copies(self, step):
        for steps in self.parts:
            kept, exchanges = steps[step]
            for target, away, _, row, slot in exchanges:
                sems = (self.send_sem, self.recv_sem)
                yield self.remote(self.view(away), self.box(kept, row), sems, slot, target), slot

    def spread_copies(self, step):
        for steps in self.parts:
            kept, exchanges = steps[step]
            for target, _, _, _, slot in exchanges:
                sems = (self.send_sem, self.recv_sem)
                view = self.view(kept)
                yield self.remote(view, view, sems, self.slots + slot, target), slot

    def scatter(self, step):
        for copy, _ in self.scatter_copies(step):
            copy.start()

    def add(self, step):
        for copy, _ in self.scatter_copies(step):
            copy.wait()
        for steps in self.parts:
            kept, exchanges = steps[step]
            size = len(exchanges) + 1
            for by in range(1, size):
                target, slot = exchanges[by - 1][0], exchanges[size - by - 1][4]
                pl.semaphore_signal(self.free_sem.at[slot], inc=1, device_id=target, device_id_type=MESH)
            mine = self.view(kept)
            arrived = [self.box(kept, row) for _, _, _, row, _ in exchanges]
            rows = min(64, kept[1])

            @pl.loop(0, kept[1] // rows)
            def _(block):
                here = part(block, rows)
                total = mine[here, :].astype(f32)
                for box in arrived:
                    total = total + box[here, :].astype(f32)
                mine[here, :] = total.astype(bf16)

    def spread(self, step):
        for copy, slot in self.spread_copies(step):
            pl.semaphore_wait(self.free_sem.at[slot], 1)
            copy.start()
        self.sends.append(functools.partial(self.spread_copies, step))

    def landed(self, step):
        for steps in self.parts:
            for _, _, source, _, slot in steps[step][1]:
                view = self.view(source)
                pltpu.make_async_copy(view, view, self.recv_sem.at[self.slots + slot]).wait()

    def finish(self):
        for remake in self.sends:
            for copy, _ in remake():
                copy.wait_send()


def back_pair(pair, query, key_t, value, grad, probs, delta, grad_query, grad_key, grad_value, causal):
    rows = query.shape[0]
    columns = part(pair, 128)
    values, queries, grads = value[:, columns], query[:, columns], grad[:, columns]
    tiles = tiles_of(rows, causal)
    key_sums = [None] * len(tiles)
    value_sums = [None] * len(tiles)
    halves = []
    for half in range(2):
        head_grads = head_lanes(grads, half)
        head_queries = head_lanes(queries, half)
        lanes = pl.ds(pl.multiple_of(pair * 128 + half * 64, 64), 64)
        shift = delta[pl.ds(pair * 2 + half, 1), :]
        pieces = []
        for at, (first, many, deep) in enumerate(tiles):
            weights = probs[half, :deep, first : first + many]
            grown = dot_t(values[:deep], head_grads[first : first + many])
            slopes = (weights.astype(f32) * (grown - shift[:, first : first + many])).astype(bf16)
            value_part = dot(weights, head_grads[first : first + many])
            key_part = dot(slopes, head_queries[first : first + many])
            value_sums[at] = value_part if half == 0 else value_sums[at] + value_part
            key_sums[at] = key_part if half == 0 else key_sums[at] + key_part
            pieces.append(dot(key_t[lanes, :deep], slopes))
        halves.append(jnp.concatenate(pieces, 1) if len(pieces) > 1 else pieces[0])
    both = jnp.concatenate(halves, 0).astype(bf16)
    grad_query[:, columns] = both.T
    for sums, out in ((key_sums, grad_key), (value_sums, grad_value)):
        if len(tiles) == 1:
            out[:, columns] = sums[0].astype(bf16)
        else:
            half_rows = rows // 2
            out[:half_rows, columns] = (sums[0] + sums[1][:half_rows]).astype(bf16)
            out[half_rows:, columns] = sums[1][half_rows:].astype(bf16)


def layer_kernel(
    count,
    copies,
    tokens,
    encoder,
    cotangent,
    self_qkv,
    self_out,
    cross_qkv,
    cross_out,
    ffn_in,
    ffn_out,
    adapt_down,
    down_bias,
    adapt_up,
    up_bias,
    norm_gain,
    norm_bias,
    shift,
    seq_lengths,
    enc_lengths,
    output,
    self_kept,
    self_key_kept,
    self_probs,
    cross_kept,
    cross_key_kept,
    cross_probs,
    normal_kept,
    inverse_kept,
    grad_encoder,
    grad_tokens,
    adapt_sums,
    vector_sums,
    mass,
    inbox,
    letters,
    vectors,
    late_letters,
    late_vectors,
    attn,
    wide_in,
    wide_out,
    held,
    turned,
    low,
    tok,
    bias,
    probs,
    total,
    normal,
    inverse,
    narrow_act,
    narrow_slope,
    down,
    up,
    delta,
    send_sem,
    recv_sem,
    own_sem,
    load_sem,
    kept_sem,
    probs_sem,
    back_sem,
    sum_send_sem,
    sum_recv_sem,
    free_sem,
    post_sem,
    mail_sem,
    late_post_sem,
    late_mail_sem,
):
    index = lax.axis_index("fsdp")
    thin = self_out.shape[0]
    deep = ffn_out.shape[0]
    rows, model = tok.shape
    unit = model // 8
    unit_in = ffn_in.shape[1] // 8
    hidden = ffn_in.shape[1]
    step_value = jnp.float32(STEP)
    branch_scale = step_value / (step_value + ramp_steps)

    def columns_of(first, units, width):
        return pl.ds(pl.multiple_of(first * width, width), units * width)

    cut = int(deep * out_cut)

    def out_rows(f, late):
        return pl.ds(pl.multiple_of(f * deep + late * cut, 16), deep - cut if late else cut)

    views = (
        lambda f, first, units: attn.at[pl.ds(0, 3), part(f, thin), columns_of(first, units, unit)],
        lambda f, first, units: attn.at[pl.ds(3, 3), part(f, thin), columns_of(first, units, unit)],
        lambda f, first, units: attn.at[pl.ds(6, 2), part(f, thin), columns_of(first, units, unit)],
        lambda f, first, units: wide_in.at[part(f, thin), columns_of(first, units, unit_in)],
        lambda f, first, units: wide_out.at[out_rows(f, 0), columns_of(first, units, unit)],
        lambda f, first, units: wide_out.at[out_rows(f, 1), columns_of(first, units, unit)],
    )
    sizes = (0.75, 0.75, 0.5, 1.0, out_cut, 1.0 - out_cut)
    mine = part(index, thin)
    owned = (
        ((self_qkv, attn.at[pl.ds(0, 3), mine]),),
        ((self_out, attn.at[3, mine]), (cross_qkv, attn.at[pl.ds(4, 3), mine]), (cross_out, attn.at[7, mine])),
        ((ffn_in, wide_in.at[mine]),),
        ((ffn_out, wide_out.at[part(index, deep)]),),
    )
    loads = []
    for group in owned:
        for source, target in group:
            loads.append(pltpu.make_async_copy(source, target, own_sem.at[len(loads)]))
    for load in loads:
        load.start()
    load_tok = pltpu.make_async_copy(tokens, tok, load_sem.at[0])
    load_enc = pltpu.make_async_copy(encoder, held.at[7], load_sem.at[1])
    load_down = pltpu.make_async_copy(adapt_down, down, load_sem.at[2])
    load_up = pltpu.make_async_copy(adapt_up, up, load_sem.at[3])
    for load in (load_tok, load_enc, load_down, load_up):
        load.start()
    gather = Gather(count, views, sizes, send_sem, recv_sem)
    reduction = Reduction(
        count,
        copies,
        mass,
        inbox,
        sum_send_sem,
        sum_recv_sem,
        free_sem,
    )
    early = Exchange(count, copies, vectors, letters, post_sem, mail_sem)
    late = Exchange(count, copies, late_vectors, late_letters, late_post_sem, late_mail_sem)
    early.enter()
    loads[0].wait()
    gather.own(0)
    for load in loads[1:]:
        load.wait()
    kept = []

    def keep(source, target):
        copy = pltpu.make_async_copy(source, target, kept_sem.at[len(kept)])
        copy.start()
        kept.append(copy)
        return copy

    def project(source, target, weight, scale=None):
        for block in range(2):
            columns = pl.ds(block * (model // 2), model // 2)
            product = dot(source[...], attn[weight, :, columns]).astype(bf16)
            target[:, columns] = product if scale is None else product * scale
            gather.tick()

    def attention(query, key, value, mixed, saved, key_saved, probs_saved, causal):
        turned[0] = value[...].T
        gather.tick()
        turned[1] = (key[...] * bf16(0.125)).T
        gather.tick()
        keep(turned.at[1], key_saved)
        steps = gather.take(16)

        def out_copy(pair, slot):
            return pltpu.make_async_copy(probs.at[slot], probs_saved.at[pl.ds(pair * 2, 2)], probs_sem.at[slot])

        pairs = HEADS // 2

        @pl.loop(0, pairs)
        def _(pair):
            slot = pair % 2
            pl.when(pair >= 2)(lambda: out_copy(pair - 2, slot).wait())
            attend_pair(pair, query, key, turned.at[0], bias, probs.at[slot], mixed, causal)
            out_copy(pair, slot).start()
            for at in range(pairs):
                mine_now = steps[2 * at : 2 * at + 2]

                @pl.when(pair == at)
                def _():
                    for step in mine_now:
                        step()

        for pair in (pairs - 2, pairs - 1):
            out_copy(pair, pair % 2).wait()

    def probs_in(saved, pair):
        slot = pair % 2
        return pltpu.make_async_copy(saved.at[pl.ds(pair * 2, 2)], probs.at[slot], probs_sem.at[slot])

    place_masks(bias, shift[0], seq_lengths, True)
    load_tok.wait()
    gather.need(0)
    project(tok, held.at[0], 0, bf16(0.125))
    project(tok, held.at[1], 1)
    project(tok, held.at[2], 2)
    attention(held.at[0], held.at[1], held.at[2], held.at[3], self_kept, self_key_kept, self_probs, True)
    keep(held.at[pl.ds(0, 4)], self_kept)
    turned_out = kept[0]

    gather.need(1)
    block_rows = 128
    blocks = rows // block_rows
    for half in range(2):
        columns = pl.ds(half * (model // 2), model // 2)
        total[:, columns] = tok[:, columns].astype(f32) + dot(held[3], attn[3, :, columns])
        gather.tick()

    @pl.loop(0, blocks)
    def _(block):
        here = part(block, block_rows)
        normal_one, inverse_one = layer_stats(total[here, :])
        normal[here, :] = normal_one
        inverse[here, :] = jnp.broadcast_to(inverse_one, (block_rows, 128))
        low[here, :] = (normal_one * norm_gain[0:1, :] + norm_bias[0:1, :]).astype(bf16)

    normal_out = keep(normal, normal_kept)
    inverse_out = keep(inverse, inverse_kept)
    place_masks(bias, shift[0], enc_lengths, False)
    load_enc.wait()
    turned_out.wait()
    project(low, held.at[4], 4, bf16(0.125))
    project(held.at[7], held.at[5], 5)
    gather.need(2)
    project(held.at[7], held.at[6], 6)
    attention(held.at[4], held.at[5], held.at[6], held.at[7], cross_kept, cross_key_kept, cross_probs, False)
    keep(held.at[pl.ds(4, 4)], cross_kept)
    for half in range(2):
        columns = pl.ds(half * (model // 2), model // 2)
        first = normal[:, columns] * norm_gain[0:1, columns] + norm_bias[0:1, columns]
        total[:, columns] = first + dot(held[7], attn[7, :, columns])
        gather.tick()
    normal_out.wait()
    inverse_out.wait()

    @pl.loop(0, blocks)
    def _(block):
        here = part(block, block_rows)
        normal_two, inverse_two = layer_stats(total[here, :])
        normal[here, :] = normal_two
        inverse[here, :] = jnp.broadcast_to(inverse_two, (block_rows, 128))
        second = normal_two * norm_gain[1:2, :] + norm_bias[1:2, :]
        low[here, :] = second.astype(bf16)
        total[here, :] = second

    load_down.wait()
    load_up.wait()
    narrow = dot(low[...], down[...]) + down_bias[...]
    gate = 1.0 / (1.0 + jnp.exp(-narrow))
    narrow_act[...] = (narrow * gate).astype(bf16)
    narrow_slope[...] = (gate * (1.0 + narrow * (1.0 - gate))).astype(bf16)
    gather.tick()
    for half in range(2):
        columns = pl.ds(half * (model // 2), model // 2)
        branch = dot(narrow_act[...], up[:, columns]) + up_bias[:, columns]
        total[:, columns] += branch_scale * branch
        gather.tick()

    for copy in kept:
        if copy is not normal_out and copy is not inverse_out and copy is not turned_out:
            copy.wait()
    load_cots = [
        pltpu.make_async_copy(
            cotangent.at[:, pl.ds(half * (model // 2), model // 2)],
            turned.at[half, pl.ds(0, rows)],
            load_sem.at[half],
        )
        for half in range(2)
    ]
    for load in load_cots:
        load.start()
    gather.need(3)
    gather.finish((0, 1))
    tile = model // 2
    act, slope = held.at[pl.ds(0, 4)], held.at[pl.ds(4, 4)]
    for block in range(hidden // tile):
        at, columns = block // 2, pl.ds((block % 2) * tile, tile)
        inner = dot(low[...], wide_in[:, pl.ds(block * tile, tile)])
        active, slant = gelu_both(inner)
        act[at, :, columns] = active.astype(bf16)
        slope[at, :, columns] = slant.astype(bf16)
        gather.tick(2)
    for phase in (4, 5):
        offset, piece = (0, cut) if phase == 4 else (cut, deep - cut)
        gather.finish((phase - 2,))
        for chip in gather.chips(phase):
            if cut % 128:
                if phase == 4:
                    continue
                offset, piece = 0, deep
            actives, weights = [], []
            for core in range(2):
                first = pl.multiple_of((2 * chip + core) * deep, deep)
                columns = pl.ds(pl.multiple_of(first % model + offset, 128), piece)
                actives.append(act[first // model, :, columns])
                weights.append(wide_out[pl.ds(pl.multiple_of(first + offset, 64), piece), :])
            active, weight = jnp.concatenate(actives, 1), jnp.concatenate(weights, 0)
            for half in range(2):
                total[:, pl.ds(half * tile, tile)] += dot(active, weight[:, half * tile : (half + 1) * tile])
    for load in load_cots:
        load.wait()
    feed_grad = tok
    for name in range(8):
        vectors[0, name : name + 1, :] = jnp.zeros((1, model), f32)

    @pl.loop(0, blocks)
    def _(block):
        here = part(block, block_rows)
        normal_three, inverse_three = layer_stats(total[here, :])
        mass[part(block + blocks, block_rows), :] = (
            normal_three * norm_gain[2:3, :] + norm_bias[2:3, :]
        ).astype(bf16)
        low_grad = jnp.concatenate([turned[0, here, :], turned[1, here, :]], 1).astype(f32)
        grad_three = norm_back(low_grad, normal_three, inverse_three, norm_gain[2:3, :])
        total[here, :] = grad_three
        tok[here, :] = grad_three.astype(bf16)
        scaled = (branch_scale * grad_three).astype(bf16)
        turned[0, here, :] = scaled[:, : model // 2]
        turned[1, here, :] = scaled[:, model // 2 :]
        vectors[0, 2:3, :] += jnp.sum(low_grad * normal_three, 0, keepdims=True)
        vectors[0, 5:6, :] += jnp.sum(low_grad, 0, keepdims=True)
        vectors[0, 6:7, :] += jnp.sum(scaled.astype(f32), 0, keepdims=True)

    out_copy = pltpu.make_async_copy(mass.at[pl.ds(rows, rows)], output, load_sem.at[2])
    out_copy.start()
    adapt = narrow_act.shape[1]
    for half in range(2):
        columns = pl.ds(half * tile, tile)
        mass[pl.ds(0, adapt), columns] = t_dot(narrow_act[...], turned[half, :rows, :]).astype(bf16)
    grown = sum(dot_t(turned[half, :rows, :], up[:, pl.ds(half * tile, tile)]) for half in range(2))
    small = grown * narrow_slope[...].astype(f32)
    narrow_grad = narrow_act
    narrow_grad[...] = small.astype(bf16)
    vectors[0, 7:8, :adapt] = jnp.sum(narrow_grad[...].astype(f32), 0, keepdims=True)
    lowered = t_dot(low[...], narrow_grad[...]).astype(bf16)
    out_copy.wait()
    for at in range(model // adapt):
        mass[pl.ds(adapt, adapt), pl.ds(at * adapt, adapt)] = lowered[at * adapt : (at + 1) * adapt]
    reduction.tick()
    for pair in range(2):
        probs_in(cross_probs, pair).start()
    for at in range(hidden // model):
        for half in range(2):
            columns = pl.ds(half * tile, tile)
            grown = dot_t(feed_grad[...], wide_out[pl.ds(at * model + half * tile, tile), :])
            act[at, :, columns] = (grown * slope[at, :, columns].astype(f32)).astype(bf16)
        if at == 2:
            reduction.tick()
    gather.finish((4, 5))
    old = {}

    def back(name, source, target):
        old[name] = pltpu.make_async_copy(source, target, back_sem.at[len(old)])
        old[name].start()

    def tile_out(at):
        return wide_out.at[pl.ds(at * rows, rows)]

    back("joined", cross_kept.at[3], tile_out(3))
    back("cross_value", cross_kept.at[2], tile_out(2))
    back("cross_query", cross_kept.at[0], tile_out(0))
    back("mixed", self_kept.at[3], tile_out(7))
    back("self_value", self_kept.at[2], tile_out(6))
    back("self_query", self_kept.at[0], tile_out(4))
    for half in range(2):
        columns = pl.ds(half * tile, tile)
        second_grad = total[:, columns] + dot_t(narrow_grad[...], down[columns, :])
        for at in range(hidden // model):
            second_grad += dot_t(act[at], wide_in[columns, pl.ds(at * model, model)])
        total[:, columns] = second_grad
    reduction.tick()
    back("cross_key", cross_key_kept, wide_in.at[:, pl.ds(0, rows)])
    back("self_key", self_key_kept, wide_in.at[:, pl.ds(rows, rows)])

    @pl.loop(0, blocks)
    def _(block):
        here = part(block, block_rows)
        grad_second = total[here, :]
        normal_two = normal[here, :]
        vectors[0, 1:2, :] += jnp.sum(grad_second * normal_two, 0, keepdims=True)
        vectors[0, 4:5, :] += jnp.sum(grad_second, 0, keepdims=True)
        grad_two = norm_back(grad_second, normal_two, inverse[here, 0:1], norm_gain[1:2, :])
        total[here, :] = grad_two
        low[here, :] = grad_two.astype(bf16)

    early.tick()
    back("normal", normal_kept, normal)
    back("inverse", inverse_kept, inverse)
    grad, grad_query = held.at[0], held.at[1]

    def attention_back(probs_saved, base, key_t, weight, causal, names, grads, ticks):
        for half in range(2):
            columns = pl.ds(half * tile, tile)
            grad[:, columns] = dot_t(low[...], attn[weight, columns, :]).astype(bf16)
        for name in names:
            old[name].wait()
        head = lax.broadcasted_iota(jnp.int32, (HEADS, model), 0)
        lane = lax.broadcasted_iota(jnp.int32, (HEADS, model), 1)
        chosen = (lane // 64 == head).astype(bf16)
        product = grad[...].astype(f32) * tile_out(base + 3)[...].astype(f32)
        delta[...] = dot_t(chosen, product.astype(bf16))
        pairs = HEADS // 2

        @pl.loop(0, pairs)
        def _(pair):
            slot = pair % 2
            probs_in(probs_saved, pair).wait()
            back_pair(
                pair,
                tile_out(base),
                key_t,
                tile_out(base + 2),
                grad,
                probs.at[slot],
                delta,
                *grads,
                causal,
            )

            @pl.when(pair + 2 < pairs)
            def _():
                probs_in(probs_saved, pair + 2).start()

            for at, tick in ticks:
                pl.when(pair == at)(functools.partial(tick))

    attention_back(
        cross_probs,
        0,
        wide_in.at[:, pl.ds(0, rows)],
        7,
        False,
        ("joined", "cross_value", "cross_query", "cross_key"),
        (grad_query, held.at[2], held.at[3]),
        (
            (0, reduction.tick),
            (1, early.tick),
            (4, reduction.tick),
            (5, early.tick),
        ),
    )
    for pair in range(2):
        probs_in(self_probs, pair).start()
    for half in range(2):
        columns = pl.ds(half * tile, tile)
        total[:, columns] += dot_t(grad_query[...], attn[4, columns, :])
    reduction.tick()
    for name in ("normal", "inverse"):
        old[name].wait()
    late_vectors[0] = jnp.zeros(late_vectors.shape[1:], f32)

    @pl.loop(0, blocks)
    def _(block):
        here = part(block, block_rows)
        grad_first = total[here, :]
        normal_one = normal[here, :]
        gain_one = jnp.sum(grad_first * normal_one, 0, keepdims=True)
        bias_one = jnp.sum(grad_first, 0, keepdims=True)
        for at in range(4):
            columns = slice(at * (model // 4), (at + 1) * (model // 4))
            late_vectors[0, at : at + 1, :] += gain_one[:, columns]
            late_vectors[0, 4 + at : 5 + at, :] += bias_one[:, columns]
        grad_one = norm_back(grad_first, normal_one, inverse[here, 0:1], norm_gain[0:1, :])
        total[here, :] = grad_one
        low[here, :] = grad_one.astype(bf16)

    late.tick()

    attention_back(
        self_probs,
        4,
        wide_in.at[:, pl.ds(rows, rows)],
        3,
        True,
        ("mixed", "self_value", "self_query", "self_key"),
        tuple(held.at[at] for at in (4, 5, 6)),
        ((0, reduction.tick), (1, late.tick), (5, late.tick), (6, reduction.tick)),
    )
    for half in range(2):
        columns = pl.ds(half * tile, tile)
        gathered = dot_t(held[2], attn[5, columns, :]) + dot_t(held[3], attn[6, columns, :])
        held[7, :, columns] = gathered.astype(bf16)
    back("encoder", held.at[7], grad_encoder)
    early.tick(99)
    late.tick(99)
    stages = len(early.groups)
    for at in range(4):
        columns = pl.ds(at * (model // 4), model // 4)
        vectors[stages, 0:1, columns] = late_vectors[stages, at : at + 1, :]
        vectors[stages, 3:4, columns] = late_vectors[stages, 4 + at : 5 + at, :]
    back("vectors", vectors.at[stages], vector_sums)
    for half in range(2):
        columns = pl.ds(half * tile, tile)
        gathered = total[:, columns]
        for at in range(3):
            gathered += dot_t(held[4 + at], attn[at, columns, :])
        low[:, columns] = gathered.astype(bf16)
    back("tokens", low, grad_tokens)
    reduction.tick(99)
    back("sums", mass, adapt_sums)
    reduction.finish()
    for name in ("encoder", "tokens", "sums", "vectors"):
        old[name].wait()


def layer(count, copies, *args):
    tokens, ffn_in, adapt_down = args[0], args[7], args[9]
    rows, model = tokens.shape
    hidden, adapt = ffn_in.shape[1], adapt_down.shape[1]
    letters, stages = letters_of(count, copies), len(exchange_groups(count, copies))
    shape = jax.ShapeDtypeStruct
    return pl.pallas_call(
        functools.partial(layer_kernel, count, copies),
        out_shape=[
            shape((rows, model), bf16),
            shape((4, rows, model), bf16),
            shape((model, rows), bf16),
            shape((HEADS, rows, rows), bf16),
            shape((4, rows, model), bf16),
            shape((model, rows), bf16),
            shape((HEADS, rows, rows), bf16),
            shape((rows, model), f32),
            shape((rows, 128), f32),
            shape((rows, model), bf16),
            shape((rows, model), bf16),
            shape((2 * adapt, model), bf16),
            shape((8, model), f32),
        ],
        in_specs=[ANY] * 10
        + [pl.BlockSpec(memory_space=pltpu.VMEM), ANY]
        + [pl.BlockSpec(memory_space=pltpu.VMEM)] * 3
        + [SMEM] * 3,
        out_specs=[ANY] * 13,
        scratch_shapes=[
            pltpu.VMEM((2 * adapt, model), bf16),
            pltpu.VMEM((2 * box_rows(adapt, count, copies), model), bf16),
            pltpu.VMEM((letters, 8, model), f32),
            pltpu.VMEM((stages + 1, 8, model), f32),
            pltpu.VMEM((letters, 8, model // 4), f32),
            pltpu.VMEM((stages + 1, 8, model // 4), f32),
            pltpu.VMEM((8, model, model), bf16),
            pltpu.VMEM((model, hidden), bf16),
            pltpu.VMEM((hidden, model), bf16),
            pltpu.VMEM((8, rows, model), bf16),
            pltpu.VMEM((2, model, rows), bf16),
            pltpu.VMEM((rows, model), bf16),
            pltpu.VMEM((rows, model), bf16),
            pltpu.VMEM((rows, rows), bf16),
            pltpu.VMEM((2, 2, rows, rows), bf16),
            pltpu.VMEM((rows, model), f32),
            pltpu.VMEM((rows, model), f32),
            pltpu.VMEM((rows, 128), f32),
            pltpu.VMEM((rows, adapt), bf16),
            pltpu.VMEM((rows, adapt), bf16),
            pltpu.VMEM((model, adapt), bf16),
            pltpu.VMEM((adapt, model), bf16),
            pltpu.VMEM((HEADS, rows), f32),
            pltpu.SemaphoreType.DMA((6, sends_per_phase(count))),
            pltpu.SemaphoreType.DMA((6, 2, count // 2, 4)),
            pltpu.SemaphoreType.DMA((6,)),
            pltpu.SemaphoreType.DMA((4,)),
            pltpu.SemaphoreType.DMA((10,)),
            pltpu.SemaphoreType.DMA((2,)),
            pltpu.SemaphoreType.DMA((16,)),
            pltpu.SemaphoreType.DMA((4 * slots_of(count, copies),)),
            pltpu.SemaphoreType.DMA((4 * slots_of(count, copies),)),
            pltpu.SemaphoreType.REGULAR((2 * slots_of(count, copies),)),
            pltpu.SemaphoreType.DMA((letters,)),
            pltpu.SemaphoreType.DMA((letters,)),
            pltpu.SemaphoreType.DMA((letters,)),
            pltpu.SemaphoreType.DMA((letters,)),
        ],
        compiler_params=pltpu.CompilerParams(
            collective_id=0, has_side_effects=True, vmem_limit_bytes=63 * 2**20
        ),
        name="decoder_layer",
    )(*args)


def results_kernel(
    output,
    grad_encoder,
    grad_tokens,
    adapt_sums,
    vector_sums,
    output_out,
    tokens_out,
    encoder_out,
    down_out,
    down_bias_out,
    up_out,
    up_bias_out,
    gain_out,
    bias_out,
    passed,
    sums,
    down,
    up,
    sem,
    out_sem,
):
    adapt, model = up.shape
    pieces = ((output, output_out), (grad_encoder, encoder_out), (grad_tokens, tokens_out))
    loads = [pltpu.make_async_copy(adapt_sums, sums, sem.at[0])]
    for at, (source, _) in enumerate(pieces):
        loads.append(pltpu.make_async_copy(source, passed.at[at], sem.at[at + 1]))
    for load in loads:
        load.start()
    outs = []

    def put(source, target):
        outs.append(pltpu.make_async_copy(source, target, out_sem.at[len(outs)]))
        outs[-1].start()

    for at, out in ((0, gain_out), (3, bias_out)):
        out[...] = vector_sums[at : at + 3, :]
    up_bias_out[...] = vector_sums[6, :]
    down_bias_out[...] = vector_sums[7, :adapt]
    loads[0].wait()
    for at in range(2):
        rows = pl.ds(at * (adapt // 2), adapt // 2)
        up[rows, :] = sums[rows, :].astype(f32)
        put(up.at[rows], up_out.at[rows])
    for at in range(model // adapt):
        rows = pl.ds(at * adapt, adapt)
        down[rows, :] = sums[pl.ds(adapt, adapt), rows].astype(f32)
        put(down.at[rows], down_out.at[rows])
    for at, (_, target) in enumerate(pieces):
        loads[at + 1].wait()
        put(passed.at[at], target)
    for copy in outs:
        copy.wait()


def results(adapt, output, grad_encoder, grad_tokens, adapt_sums, vector_sums):
    rows, model = output.shape
    shape = jax.ShapeDtypeStruct
    inside = pl.BlockSpec(memory_space=pltpu.VMEM)
    return pl.pallas_call(
        results_kernel,
        out_shape=[
            shape((rows, model), bf16),
            shape((rows, model), bf16),
            shape((rows, model), bf16),
            shape((model, adapt), f32),
            shape((adapt,), f32),
            shape((adapt, model), f32),
            shape((model,), f32),
            shape((3, model), f32),
            shape((3, model), f32),
        ],
        in_specs=[ANY] * 4 + [inside],
        out_specs=[ANY] * 4 + [inside, ANY] + [inside] * 3,
        scratch_shapes=[
            pltpu.VMEM((3, rows, model), bf16),
            pltpu.VMEM((2 * adapt, model), bf16),
            pltpu.VMEM((model, adapt), f32),
            pltpu.VMEM((adapt, model), f32),
            pltpu.SemaphoreType.DMA((4,)),
            pltpu.SemaphoreType.DMA((5 + model // adapt,)),
        ],
        compiler_params=pltpu.CompilerParams(vmem_limit_bytes=63 * 2**20),
        name="write_results",
    )(output, grad_encoder, grad_tokens, adapt_sums, vector_sums)


def local(*args):
    count, copies = lax.axis_size("fsdp"), lax.axis_size("dp")
    args = list(args)
    adapt = args[10].shape[0]
    args[10], args[12] = args[10][None], args[12][None]
    kept = layer(count, copies, *args)
    return tuple(results(adapt, kept[0], *kept[9:]))


def solution(mesh):
    rows = P(("fsdp", "dp"), None)
    placed = (
        (rows,) * 3
        + (P(None, "fsdp", None), P("fsdp", None)) * 2
        + (P("fsdp", None),) * 2
        + (P(),) * 6
        + (P(("fsdp", "dp")), rows, rows)
    )
    return jax.shard_map(
        local, mesh=mesh, in_specs=placed, out_specs=(rows,) * 3 + (P(),) * 6, check_vma=False
    )
```
